256 devices in a mesh: fx: 16 (over z, core), fy: 8 (over y, x_lo), sz: 2 (over x_hi).
Axes of the slice: x: 4 (x_hi: 2, x_lo: 2; x = x_hi * 2 + x_lo), y: 4, z: 8, core: 2. Of those that a mesh axis runs over, the one named last changes fastest.
Arguments:
- populations: float32 [19, 64, 64, 512], P(None, 'fx', 'fy', 'sz'), as said below
- relaxation: float32 [64, 64, 512], P('fx', 'fy', 'sz'), may hold values from 1 to 1.8
- struct_velocity: float32 [3, 65536], P(None, ('fy', 'sz')), may hold values from -0.12 to 0.12
- iface_count: int32 [16, 8, 2, 16], P('fx', 'fy', 'sz'), may hold values from 0 to 32, as said below
- iface_cell: int32 [16, 8, 2, 16, 32], P('fx', 'fy', 'sz'), may hold values from 0 to 8191
- rbf_node: int32 [16, 8, 2, 16, 16, 32], P('fx', 'fy', 'sz'), may hold values from 0 to 4095
- rbf_weight: float32 [16, 8, 2, 16, 16, 32], P('fx', 'fy', 'sz'), may hold values from 0 to 0.25
- disp_prev: float32 [3, 65536], P(None, ('fy', 'sz')), may hold values from -6 to 6
- node_mass: float32 [65536], P(('fy', 'sz')), may hold values from 0.5 to 2
- connect: int32 [16, 16, 8, 512], P('fx', ('fy', 'sz')), may hold values from 0 to 4351
- modulus: float32 [16, 16, 512], P('fx', ('fy', 'sz')), may hold values from 0.5 to 5
- strain_basis: float32 [24, 24], replicated, may hold values from -1.25 to 1.25
Outputs:
- populations_out: float32 [19, 64, 64, 512], P(None, 'fx', 'fy', 'sz')
- solution: float32 [3, 65536], P(None, ('fy', 'sz'))
- residual: float32 [3, 65536], P(None, ('fy', 'sz'))
The draws below stay inside these ranges and needn't reach their ends.
Inputs may be any that keep to these rules, and one draw needn't show every extreme that they name: `iface_count`: slots below the count are live. For some index of the first dimension, one subdomain gets 32 live slots from every block of it. `connect`: values below 256 name the last 256 nodes of the previous subdomain. All populations are positive.
All inputs are finite; a program needn't handle non-finite values.
Results may differ from the reference program's by a relative error of at most 0.0003.
Values sent between devices are 32-bit elements; how exact they have to be, the bound alone decides.
A program may use at most 128 MiB of HBM per device.

```python
import math
import jax
import jax.numpy as jnp
from jax import lax

CX = 4
CY = 8
CZ = 256
STEPS = 2
ITERS = 3
NODE_DEV = 4096
BND = 256
ELEM_DEV = 512
SLOTS = 32
RBF_K = 16
BLOCKS_X = 16
BLOCKS_Y = 8
BLOCKS_Z = 2
OWNERS = 16
GROUPS = 16
NODES = 65536
NX = 64
NY = 64
NZ = 512


VELOCITY_TABLE = [(0, 0, 0), (1, 0, 0), (-1, 0, 0), (0, 1, 0), (0, -1, 0), (0, 0, 1), (0, 0, -1), (1, 1, 0), (-1, -1, 0), (1, -1, 0), (-1, 1, 0), (1, 0, 1), (-1, 0, -1), (1, 0, -1), (-1, 0, 1), (0, 1, 1), (0, -1, -1), (0, 1, -1), (0, -1, 1)]


LATTICE_TABLE = [1.0 / 3.0] + [1.0 / 18.0] * 6 + [1.0 / 36.0] * 12


def draw_populations(key, part):
    key = jax.random.fold_in(key, 11)
    keys = jax.random.split(key, 3)
    density = jax.random.uniform(keys[0], (NX, NY, NZ), jnp.float32, 0.95, 1.05)
    flow = jax.random.uniform(keys[1], (3, NX, NY, NZ), jnp.float32, -0.05, 0.05)
    noise = jax.random.uniform(keys[2], (19, NX, NY, NZ), jnp.float32, 0.9, 1.1)
    square = flow[0] * flow[0] + flow[1] * flow[1] + flow[2] * flow[2]
    layers = []
    for corner in range(19):
        step_x, step_y, step_z = VELOCITY_TABLE[corner]
        aligned = step_x * flow[0] + step_y * flow[1] + step_z * flow[2]
        layers.append(LATTICE_TABLE[corner] * density * (1.0 + 3.0 * aligned + 4.5 * aligned * aligned - 1.5 * square))
    return jnp.stack(layers) * noise


def draw_iface_count(key, part):
    key = jax.random.fold_in(key, 23)
    keys = jax.random.split(key, 4)
    shape_all = (BLOCKS_X, BLOCKS_Y, BLOCKS_Z, OWNERS)
    base_count = jax.random.randint(keys[0], shape_all, 0, SLOTS + 1)
    nearby = jax.random.randint(keys[1], shape_all, 0, 4) == 0
    counts = jnp.where(nearby, base_count, base_count // 4)
    full_row = jax.random.randint(keys[2], (), 0, BLOCKS_X)
    full_owner = jax.random.randint(keys[3], (), 0, OWNERS)
    row_iota = lax.broadcasted_iota(jnp.int32, shape_all, 0)
    owner_iota = lax.broadcasted_iota(jnp.int32, shape_all, 3)
    filled = (row_iota == full_row) & (owner_iota == full_owner)
    return jnp.where(filled, SLOTS, counts).astype(jnp.int32)


def set_ends(drawn, rng, low, high):
    longest = drawn.shape.index(max(drawn.shape))
    spots = []
    for shift in (0, 1):
        where = [jax.random.randint(jax.random.fold_in(rng, axis), (), 0, length) for axis, length in enumerate(drawn.shape)]
        where[longest] = (where[longest] + shift) % drawn.shape[longest]
        spots.append(tuple(where))
    return drawn.at[spots[0]].set(low).at[spots[1]].set(high)


def block_levels(own_key, shape, cuts, low, largest):
    loudness = 1.0
    for dim, blocks in cuts:
        heights = jax.random.uniform(jax.random.fold_in(jax.random.fold_in(own_key, 6), dim), (blocks,), jnp.float32, low / len(cuts), largest / len(cuts))
        loudness = loudness * jnp.repeat(jnp.exp(heights), shape[dim] // blocks).reshape((-1,) + (1,) * (len(shape) - 1 - dim))
    return loudness


def scatter_about(own_key, shape, width, limit, cuts=(), kind=jnp.bfloat16):
    loudness = block_levels(own_key, shape, cuts, -0.22, 0.18) if cuts else 1.0
    drawn = jax.random.normal(own_key, shape, jnp.float32) * width * loudness
    return jnp.minimum(jnp.maximum(drawn, -limit), limit).astype(kind)


def setup_inputs(seed: int = 0) -> dict:
    key_list = jax.random.split(jax.random.key(seed), 13)
    populations = draw_populations(jax.random.fold_in(key_list[12], 71), 0)
    relaxation = jnp.clip(1.0 + 0.79999995 * jax.random.uniform(key_list[1], (NX, NY, NZ), jnp.float32) ** block_levels(key_list[1], (NX, NY, NZ), ((0, 16), (1, 8), (2, 2)), -0.2, 0.2), 1.0, 1.8)
    struct_velocity = scatter_about(key_list[2], (3, NODES), 0.02, 0.12, ((1, 16),), jnp.float32)
    iface_count = draw_iface_count(jax.random.fold_in(key_list[12], 71), 0)
    iface_cell = set_ends(jax.random.randint(key_list[4], (BLOCKS_X, BLOCKS_Y, BLOCKS_Z, OWNERS, SLOTS), 0, CX * CY * CZ), jax.random.fold_in(key_list[4], 1), 0, (CX * CY * CZ) - 1).astype(jnp.int32)
    rbf_node = set_ends(jax.random.randint(key_list[5], (BLOCKS_X, BLOCKS_Y, BLOCKS_Z, OWNERS, RBF_K, SLOTS), 0, NODE_DEV), jax.random.fold_in(key_list[5], 1), 0, NODE_DEV - 1).astype(jnp.int32)
    rbf_weight = jnp.clip(0.25 * jax.random.uniform(key_list[6], (BLOCKS_X, BLOCKS_Y, BLOCKS_Z, OWNERS, RBF_K, SLOTS), jnp.float32) ** block_levels(key_list[6], (BLOCKS_X, BLOCKS_Y, BLOCKS_Z, OWNERS, RBF_K, SLOTS), ((0, 16), (1, 8), (2, 2)), -0.2, 0.2), 0.0, 0.25)
    disp_prev = scatter_about(key_list[7], (3, NODES), 1.0, 6.0, ((1, 16),), jnp.float32)
    node_mass = jnp.clip(jnp.exp(math.log(2.0) - 1.3862944 * jax.random.uniform(key_list[8], (NODES,), jnp.float32) ** block_levels(key_list[8], (NODES,), ((0, 16),), -0.2, 0.2)), 0.5, 2.0)
    connect = set_ends(jax.random.randint(key_list[9], (GROUPS, OWNERS, 8, ELEM_DEV), 0, BND + NODE_DEV), jax.random.fold_in(key_list[9], 1), 0, (BND + NODE_DEV) - 1).astype(jnp.int32)
    modulus = jnp.clip(jnp.exp(math.log(5.0) - 2.3025851 * jax.random.uniform(key_list[10], (GROUPS, OWNERS, ELEM_DEV), jnp.float32) ** block_levels(key_list[10], (GROUPS, OWNERS, ELEM_DEV), ((0, 16), (1, 16)), -0.2, 0.2)), 0.5, 5.0)
    strain_basis = scatter_about(key_list[11], (24, 24), 24 ** -0.5, 1.25, (), jnp.float32)
    return dict(populations=populations, relaxation=relaxation, struct_velocity=struct_velocity, iface_count=iface_count, iface_cell=iface_cell, rbf_node=rbf_node, rbf_weight=rbf_weight, disp_prev=disp_prev, node_mass=node_mass, connect=connect, modulus=modulus, strain_basis=strain_basis)


PRECISE = lax.Precision.HIGHEST
VELOCITY_TABLE = [(0, 0, 0), (1, 0, 0), (-1, 0, 0), (0, 1, 0), (0, -1, 0), (0, 0, 1), (0, 0, -1),
                  (1, 1, 0), (-1, -1, 0), (1, -1, 0), (-1, 1, 0), (1, 0, 1), (-1, 0, -1),
                  (1, 0, -1), (-1, 0, 1), (0, 1, 1), (0, -1, -1), (0, 1, -1), (0, -1, 1)]
LATTICE_TABLE = [1.0 / 3.0] + [1.0 / 18.0] * 6 + [1.0 / 36.0] * 12
FORCE_SCALE = 20.0


def moments(field, vel_table):
    density = jnp.sum(field, axis=0)
    momentum = jnp.einsum("iq,ixyz->qxyz", vel_table, field, precision=PRECISE)
    return density, momentum


def collide(field, relaxation, vel_table, lattice):
    density, momentum = moments(field, vel_table)
    flow_speed = momentum / density
    aligned = jnp.einsum("iq,qxyz->ixyz", vel_table, flow_speed, precision=PRECISE)
    square = jnp.sum(flow_speed * flow_speed, axis=0)
    balance = lattice[:, None, None, None] * density * (1.0 + 3.0 * aligned + 4.5 * aligned * aligned - 1.5 * square)
    return field + relaxation * (balance - field), density


def apply_operator(field, connect, modulus, strain_basis, node_mass):
    owned = field.reshape(3, OWNERS, NODE_DEV)
    ghost = jnp.concatenate([jnp.zeros((3, 1, BND), jnp.float32), owned[:, :-1, NODE_DEV - BND:]], axis=1)
    extended = jnp.concatenate([ghost, owned], axis=2)

    def one_domain(ext_part, conn_part, mod_part):
        picked = ext_part[:, conn_part]
        picked = jnp.transpose(picked, (1, 0, 2, 3)).reshape(GROUPS, 24, ELEM_DEV)
        strain = jnp.einsum("ab,gbe->gae", strain_basis, picked, precision=PRECISE)
        spread = jnp.einsum("ab,gae->gbe", strain_basis, strain, precision=PRECISE)
        spread = spread * mod_part[:, None, :]
        spread = jnp.transpose(spread.reshape(GROUPS, 3, 8, ELEM_DEV), (1, 0, 2, 3)).reshape(3, -1)
        return jax.ops.segment_sum(spread.T, conn_part.reshape(-1), num_segments=BND + NODE_DEV).T

    summed = jax.vmap(one_domain, in_axes=(1, 1, 1), out_axes=1)(extended, connect, modulus)
    result = node_mass.reshape(1, OWNERS, NODE_DEV) * owned + summed[:, :, BND:]
    result = result.at[:, :-1, NODE_DEV - BND:].add(summed[:, 1:, :BND])
    return result.reshape(3, -1)


def reference(populations, relaxation, struct_velocity, iface_count, iface_cell, rbf_node, rbf_weight,
              disp_prev, node_mass, connect, modulus, strain_basis):
    vel_table = jnp.asarray(VELOCITY_TABLE, jnp.float32)
    lattice = jnp.asarray(LATTICE_TABLE, jnp.float32)
    slot_iota = lax.broadcasted_iota(jnp.int32, iface_cell.shape, 4)
    live = (slot_iota < iface_count[..., None]).astype(jnp.float32)
    owner_base = lax.broadcasted_iota(jnp.int32, rbf_node.shape, 3) * NODE_DEV
    global_node = rbf_node + owner_base
    picked = struct_velocity[:, global_node]
    wall = jnp.sum(rbf_weight * picked, axis=5) * live
    wall_flat = wall.reshape(3, -1)
    live_flat = live.reshape(-1)
    local_cell = iface_cell
    cell_x = lax.broadcasted_iota(jnp.int32, local_cell.shape, 0) * CX + local_cell // (CY * CZ)
    cell_y = lax.broadcasted_iota(jnp.int32, local_cell.shape, 1) * CY + (local_cell // CZ) % CY
    cell_z = lax.broadcasted_iota(jnp.int32, local_cell.shape, 2) * CZ + local_cell % CZ
    global_cell = ((cell_x * NY + cell_y) * NZ + cell_z).reshape(-1)
    push = 6.0 * lattice[:, None] * jnp.dot(vel_table, wall_flat, precision=PRECISE)
    field = populations
    for section in range(STEPS):
        post, density = collide(field, relaxation, vel_table, lattice)
        at_cells = density.reshape(-1)[global_cell]
        flat_post = post.reshape(19, -1).at[:, global_cell].add(push * at_cells[None, :])
        post = flat_post.reshape(post.shape)
        field = jnp.stack([jnp.roll(post[corner], VELOCITY_TABLE[corner], axis=(0, 1, 2)) for corner in range(19)])
    populations_out = field
    density, momentum = moments(field, vel_table)
    rho_slot = density.reshape(-1)[global_cell]
    mom_slot = momentum.reshape(3, -1)[:, global_cell]
    force = (mom_slot - rho_slot[None, :] * wall_flat) * live_flat[None, :]
    force_full = force.reshape(3, BLOCKS_X, BLOCKS_Y, BLOCKS_Z, OWNERS, 1, SLOTS)
    terms = rbf_weight[None] * force_full
    load = jax.ops.segment_sum(terms.reshape(3, -1).T, global_node.reshape(-1), num_segments=NODES).T
    load = load * FORCE_SCALE
    rhs = node_mass[None, :] * disp_prev + load
    solution = disp_prev
    residual = rhs - apply_operator(solution, connect, modulus, strain_basis, node_mass)
    direction = residual
    norm_now = jnp.sum(residual * residual)
    for section in range(ITERS):
        image = apply_operator(direction, connect, modulus, strain_basis, node_mass)
        alpha = norm_now / jnp.sum(direction * image)
        solution = solution + alpha * direction
        residual = residual - alpha * image
        norm_next = jnp.sum(residual * residual)
        direction = residual + (norm_next / norm_now) * direction
        norm_now = norm_next
    return populations_out, solution, residual
```

```python
import jax
import jax.numpy as jnp
from jax import lax
from jax.experimental import pallas as pl
from jax.experimental.pallas import tpu as pltpu
from jax.sharding import PartitionSpec as P

F32 = jnp.float32
BF16 = jnp.bfloat16
I32 = jnp.int32
FX, FY, SZ = 16, 8, 2
OWN = 16
ITERS = 3
APPS = ITERS + 1
FORCE_SCALE = 20.0
VEL = [
    (0, 0, 0),
    (1, 0, 0),
    (-1, 0, 0),
    (0, 1, 0),
    (0, -1, 0),
    (0, 0, 1),
    (0, 0, -1),
    (1, 1, 0),
    (-1, -1, 0),
    (1, -1, 0),
    (-1, 1, 0),
    (1, 0, 1),
    (-1, 0, -1),
    (1, 0, -1),
    (-1, 0, 1),
    (0, 1, 1),
    (0, -1, -1),
    (0, 1, -1),
    (0, -1, 1),
]
X_POPS = [[i for i in range(19) if VEL[i][0] == s] for s in (1, -1)]
Y_POPS = [[i for i in range(19) if VEL[i][1] == s] for s in (1, -1)]
Z_POPS = [i for i in range(19) if VEL[i][2] != 0]
DIAGONAL = (7, 8, 9, 10)
MESH = pl.DeviceIdType.MESH


def split2(x):
    top = x.astype(BF16)
    rest = (x - top.astype(F32)).astype(BF16)
    return jnp.concatenate([top, rest], axis=0)


def dot_nt(a, b):
    return lax.dot_general(a, b, (((1,), (1,)), ((), ())), preferred_element_type=F32)


def dot_nn(a, b):
    return lax.dot_general(a, b, (((1,), (0,)), ((), ())), preferred_element_type=F32)


def exact_dot(a, b, dims=((1,), (0,))):
    return lax.dot_general(
        a, b, (dims, ((), ())), preferred_element_type=F32, precision=lax.Precision.HIGHEST
    )


def iota(shape, dim):
    return lax.broadcasted_iota(I32, shape, dim)


def group_sum(x):
    x = x + pltpu.roll(x, 64, x.ndim - 1)
    return x + pltpu.roll(x, 32, x.ndim - 1)


def send(src, dst, ssem, rsem, device):
    pltpu.make_async_remote_copy(
        src_ref=src,
        dst_ref=dst,
        send_sem=ssem,
        recv_sem=rsem,
        device_id=device,
        device_id_type=MESH,
    ).start()


def wait(ref, sem):
    pltpu.make_async_copy(ref, ref, sem).wait()


def kernel(
    pop, relax, vel, count, cell, node, weight, disp, mass, connect, modulus, basis,
    out_pop, out_sol, out_res,
    sup_send, sup_recv, wall_send, wall_recv, frc_send, frc_recv, edge_send, edge_recv,
    xs, xr, ys, yr, ds, dr, zs, zr, zxr, zys, zyr,
    rs_send, rs_recv, gh_recv, sc_send, sc_recv, ag_send, ag_recv,
    post, field, rho_ref, gain, cell_lo, cell_hi, live_ref, wallp,
    sup_lo, sup_hi, lhs, el_lo, el_hi, pick, spread, ela, vec_r, vec_p, vec_s, vec_w, vec_x,
    massc, rc, load_ref,
    s_sup, r_sup, s_wall, r_wall, s_frc, r_frc, s_edge, r_edge, s_halo, r_halo,
    s_rs, r_rs, s_gh, r_gh, s_sc, r_sc, s_ag, r_ag, s_ag2,
):
    f = lax.axis_index("fx")
    y = lax.axis_index("fy")
    z = lax.axis_index("sz")
    own = y * SZ + z

    def at_owner(o, fx=None):
        return (f if fx is None else fx, o // SZ, lax.rem(o, SZ))

    def to_owners(src_of, dst, ssem, rsem):
        def go(d, _):
            o = lax.rem(own + d, OWN)
            send(src_of(o), dst, ssem, rsem, at_owner(o))
            return 0

        lax.fori_loop(1, OWN, go, 0)

    lane = iota((1, 128), 1)
    group = lane // 32
    expand = (iota((32, 128), 0) == lax.rem(iota((32, 128), 1), 32)).astype(F32)
    quarter = (iota((16, 128), 0) // 4) == (iota((16, 128), 1) // 32)
    upper = iota((8, 128), 0) < 4

    def pack(o, _):
        def packed(x):
            x = jnp.where(quarter, exact_dot(x, expand), 0.0)
            x = x[0:8] + x[8:16]
            return x + pltpu.roll(x, 4, 0)

        tile = jnp.where(upper, packed(node[o].astype(F32)), packed(weight[o]))
        sup_send[o] = tile

        @pl.when(o == own)
        def _():
            sup_recv[o] = tile

        return 0

    lax.fori_loop(0, OWN, pack, 0)
    to_owners(lambda o: sup_send.at[o], sup_recv.at[own], s_sup, r_sup)

    for c in range(3):
        edge_send[c : c + 1, :] = disp[c : c + 1, 3840:4096]
    edge_send[3:4, :] = jnp.zeros((1, 256), F32)
    after, before = lax.rem(own + 1, OWN), lax.rem(own + OWN - 1, OWN)
    send(edge_send, edge_recv, s_edge, r_edge, at_owner(after))

    def corner(j, _):
        n = connect[pl.ds(j, 1), :]
        lo = lax.rem(n, 256)
        hi = jnp.where(n < 256, 16, n // 256 - 1)
        el_lo[j] = jnp.where(iota((256, 512), 0) == lo, 1.0, 0.0).astype(BF16)
        el_hi[j] = jnp.where(iota((24, 512), 0) == hi, 1.0, 0.0)
        return 0

    lax.fori_loop(0, 8, corner, 0)
    base = basis[...]
    gram = exact_dot(base, base, ((0,), (0,)))

    cells = cell[...]
    cell_hi16 = exact_dot((cells // 256).astype(F32), expand)
    cell_lo16 = exact_dot(lax.rem(cells, 256).astype(F32), expand)
    diag = iota((16, 16), 0) == iota((16, 16), 1)
    counts = jnp.sum(jnp.where(diag, count[...].astype(F32), 0.0), axis=1, keepdims=True)
    live16 = (lax.rem(iota((16, 128), 1), 32).astype(F32) < counts).astype(F32)
    mine = lax.rem(iota((16, 128), 0), 4) == (iota((16, 128), 1) // 32)
    fold = ((iota((8, 16), 1) // 4) == iota((8, 16), 0)).astype(F32)

    def rows_of(x):
        return exact_dot(fold, jnp.where(mine, x, 0.0))

    hi_rows, lo_rows = rows_of(cell_hi16).astype(I32), rows_of(cell_lo16).astype(I32)
    live_ref[...] = rows_of(live16)
    for g in range(4):
        at = slice(g * 128, g * 128 + 128)
        cell_lo[:, at] = jnp.where(iota((256, 128), 0) == lo_rows[g : g + 1], 1.0, 0.0).astype(BF16)
        cell_hi[:, at] = jnp.where(iota((32, 128), 0) == hi_rows[g : g + 1], 1.0, 0.0)

    def moments(fs):
        rho = fs[0]
        for i in range(1, 19):
            rho = rho + fs[i]
        mom = []
        for a in range(3):
            total = None
            for i in range(1, 19, 2):
                s = VEL[i][a]
                if s:
                    pair = fs[i] - fs[i + 1] if s > 0 else fs[i + 1] - fs[i]
                    total = pair if total is None else total + pair
            mom.append(total)
        return rho, mom

    def along(c, v):
        total = None
        for a in range(3):
            if c[a] == 1:
                total = v[a] if total is None else total + v[a]
        for a in range(3):
            if c[a] == -1:
                total = -v[a] if total is None else total - v[a]
        return total

    def collide(source):
        for k in range(4):
            fs = [source[i, k] for i in range(19)]
            om = relax[k]
            rho, mom = moments(fs)
            inv = 1.0 / rho
            u = [m * inv for m in mom]
            sq = 1.5 * (u[0] * u[0] + u[1] * u[1] + u[2] * u[2])
            rho_ref[k] = rho
            keep = 1.0 - om
            scaled = om * rho
            post[0, k] = keep * fs[0] + (1.0 / 3.0) * scaled * (1.0 - sq)
            for i in range(1, 19, 2):
                t = (1.0 / 18.0) if i < 7 else (1.0 / 36.0)
                a = along(VEL[i], u)
                ts = t * scaled
                even = ts * (1.0 + 4.5 * a * a - sq)
                odd = ts * (3.0 * a)
                post[i, k] = keep * fs[i] + (even + odd)
                post[i + 1, k] = keep * fs[i + 1] + (even - odd)

    def turn(i, v):
        cy, cz = VEL[i][1], VEL[i][2]
        if cy:
            v = pltpu.roll(v, cy % 8, 0)
        if cz:
            v = pltpu.roll(v, cz % 256, 1)
        return v

    lane8 = iota((8, 128), 1)
    row8 = iota((8, 128), 0)

    def stream(step, target, wall_gain):
        for k in range(4):
            for c in range(3):
                gain[c, k] = wall_gain[c][k] * rho_ref[k] * (1.0 / 6.0)
        for x in range(4):
            zpack = jnp.zeros((8, 128), F32)
            for i in range(19):
                cx, cy, cz = VEL[i]
                k = (x - cx) % 4
                v = post[i, k]
                if i:
                    push = along(VEL[i], [gain[c, k] for c in range(3)])
                    v = v + (2.0 * push if i < 7 else push)
                v = turn(i, v)
                if k != x - cx:
                    side = 0 if cx > 0 else 1
                    xs[step, side, X_POPS[side].index(i)] = v
                    if cy:
                        r = 0 if cy > 0 else 7
                        ds[step, DIAGONAL.index(i)] = v[r : r + 1, :]
                else:
                    target[i, x] = v
                if cy:
                    side = 0 if cy > 0 else 1
                    r = 0 if cy > 0 else 7
                    ys[step, side, Y_POPS[side].index(i), x : x + 1, :] = v[r : r + 1, :]
                if cz:
                    col = v[:, 0:1] if cz > 0 else v[:, 255:256]
                    zpack = jnp.where(lane8 == Z_POPS.index(i), col, zpack)
            zs[step, x] = zpack
            zys[step, 0, x : x + 1, :] = zpack[0:1, :]
            zys[step, 1, x : x + 1, :] = zpack[7:8, :]
        xp, xm = lax.rem(f + 1, FX), lax.rem(f + FX - 1, FX)
        yp, ym = lax.rem(y + 1, FY), lax.rem(y + FY - 1, FY)
        zo = 1 - z
        jobs = [
            (xs.at[step, 0], xr.at[step, 0], (xp, y, z)),
            (xs.at[step, 1], xr.at[step, 1], (xm, y, z)),
            (ys.at[step, 0], yr.at[step, 0], (f, yp, z)),
            (ys.at[step, 1], yr.at[step, 1], (f, ym, z)),
            (zs.at[step], zr.at[step], (f, y, zo)),
            (ds.at[step, 0], dr.at[step, 0], (xp, yp, z)),
            (ds.at[step, 1], dr.at[step, 1], (xm, ym, z)),
            (ds.at[step, 2], dr.at[step, 2], (xp, ym, z)),
            (ds.at[step, 3], dr.at[step, 3], (xm, yp, z)),
            (zs.at[step, 0], zxr.at[step, 0], (xp, y, zo)),
            (zs.at[step, 3], zxr.at[step, 1], (xm, y, zo)),
            (zys.at[step, 0], zyr.at[step, 0], (f, yp, zo)),
            (zys.at[step, 1], zyr.at[step, 1], (f, ym, zo)),
        ]
        for n, (src, dst, device) in enumerate(jobs):
            send(src, dst, s_halo.at[step, n], r_halo.at[step, n], device)
        for n, (src, dst, device) in enumerate(jobs):
            wait(dst, r_halo.at[step, n])
        for side in range(2):
            for n, i in enumerate(X_POPS[side]):
                target[i, 0 if side == 0 else 3] = xr[step, side, n]
        for side in range(2):
            r = 0 if side == 0 else 7
            for n, i in enumerate(Y_POPS[side]):
                cx = VEL[i][0]
                for x in range(4):
                    if 0 <= x - cx <= 3:
                        target[i, x, r : r + 1, :] = yr[step, side, n, x : x + 1, :]
        for n, i in enumerate(DIAGONAL):
            cx, cy, _ = VEL[i]
            r = 0 if cy > 0 else 7
            target[i, 0 if cx > 0 else 3, r : r + 1, :] = dr[step, n]
        z11, z12, z13, z14, z15, z16, z17, z18 = [Z_POPS.index(i) for i in range(11, 19)]
        for x in range(4):
            zin = zr[step, x]
            if x == 0:
                zin = jnp.where((lane8 == z11) | (lane8 == z13), zxr[step, 0], zin)
            if x == 3:
                zin = jnp.where((lane8 == z12) | (lane8 == z14), zxr[step, 1], zin)
            low = (row8 == 0) & ((lane8 == z15) | (lane8 == z17))
            high = (row8 == 7) & ((lane8 == z16) | (lane8 == z18))
            zin = jnp.where(low, zyr[step, 0, x : x + 1, :], zin)
            zin = jnp.where(high, zyr[step, 1, x : x + 1, :], zin)
            for n, i in enumerate(Z_POPS):
                col = zin[:, n : n + 1]
                if VEL[i][2] > 0:
                    target[i, x, :, 0:128] = jnp.where(lane8 == 0, col, target[i, x, :, 0:128])
                else:
                    target[i, x, :, 128:256] = jnp.where(
                        lane8 == 127, col, target[i, x, :, 128:256]
                    )
        return jobs

    collide(pop)

    wait(sup_recv.at[pl.ds(0, OWN - 1)], r_sup)

    def supports(b, _):
        for r in range(4):
            n = sup_recv[b, r : r + 1, :].astype(I32)
            w = sup_recv[b, r + 4 : r + 5, :]
            sup_lo[b, :, r * 128 : r * 128 + 128] = jnp.where(
                iota((256, 128), 0) == lax.rem(n, 256), 1.0, 0.0
            ).astype(BF16)
            sup_hi[b, :, r * 128 : r * 128 + 128] = jnp.where(
                iota((16, 128), 0) == n // 256, w, 0.0
            )
        return 0

    lax.fori_loop(0, OWN, supports, 0)
    for c in range(3):
        for h in range(16):
            load_ref[c * 16 + h : c * 16 + h + 1, :] = vel[c : c + 1, h * 256 : h * 256 + 256]
    table = split2(load_ref[...])

    def answer(b, _):
        out = dot_nn(table, sup_lo[b])
        out = out[0:48] + out[48:96]
        hot = sup_hi[b]
        rows = []
        for c in range(3):
            m = out[c * 16 : c * 16 + 16] * hot
            m = m[:, 0:128] + m[:, 128:256] + m[:, 256:384] + m[:, 384:512]
            rows.append(jnp.sum(m, axis=0, keepdims=True))
        rows.append(jnp.zeros((1, 128), F32))
        for c in range(4):
            wall_send[b, c : c + 1, :] = rows[c]
        return 0

    lax.fori_loop(0, OWN, answer, 0)
    wall_recv[own] = wall_send[own]
    to_owners(lambda o: wall_send.at[o], wall_recv.at[own], s_wall, r_wall)

    def elements(values):
        both = split2(values)

        def gather(j, _):
            out = dot_nn(both, el_lo[j])
            out = out[0:80] + out[80:160]
            hot = el_hi[j]
            for c in range(3):
                pick[pl.ds(c * 8 + j, 1), :] = jnp.sum(
                    out[c * 24 : c * 24 + 24] * hot, axis=0, keepdims=True
                )
            return 0

        lax.fori_loop(0, 8, gather, 0)
        picked = pick[...]
        spread[...] = exact_dot(gram, picked) * modulus[...]
        ela[...] = jnp.zeros((160, 256), F32)

        def scatter(j, _):
            hot = el_hi[j]
            parts = [hot * spread[pl.ds(c * 8 + j, 1), :] for c in range(3)]
            parts.append(jnp.zeros((8, 512), F32))
            ela[...] += dot_nt(split2(jnp.concatenate(parts, axis=0)), el_lo[j])
            return 0

        lax.fori_loop(0, 8, scatter, 0)
        return ela[0:80] + ela[80:160], picked

    wait(edge_recv, r_edge)
    vec_r[...] = jnp.zeros((80, 256), F32)
    has_before = (own > 0).astype(F32)
    has_after = (own < OWN - 1).astype(F32)
    for c in range(3):
        for h in range(16):
            row = disp[c : c + 1, h * 256 : h * 256 + 256]
            vec_r[c * 24 + h : c * 24 + h + 1, :] = row
            vec_x[c * 16 + h : c * 16 + h + 1, :] = row
        vec_r[c * 24 + 16 : c * 24 + 17, :] = edge_recv[c : c + 1, :] * has_before
    vec_w[...] = elements(vec_r[...])[0]
    massc[:, 0:128] = mass[pl.ds(2 * f, 1), :]
    massc[:, 128:256] = mass[pl.ds(2 * f + 1, 1), :]

    wait(wall_recv.at[pl.ds(0, OWN - 1)], r_wall)
    wall = [None] * 4
    for g in range(4):
        total = jnp.zeros((4, 128), F32)
        for q in range(4):
            total = jnp.where(group == q, group_sum(wall_recv[g * 4 + q]), total)
        wall[g] = total * live_ref[g : g + 1, :]
    for g in range(4):
        hot = cell_hi[:, g * 128 : g * 128 + 128]
        parts = [hot * wall[g][c : c + 1, :] for c in range(3)]
        wallp[:, g * 128 : g * 128 + 128] = split2(jnp.concatenate(parts, axis=0))
    summed = dot_nt(wallp[...], cell_lo[...])
    summed = summed[0:96] + summed[96:192]
    wall_gain = [
        [summed[c * 32 + k * 8 : c * 32 + k * 8 + 8, :] for k in range(4)] for c in range(3)
    ]

    jobs0 = stream(0, field, wall_gain)
    collide(field)
    jobs1 = stream(1, out_pop, wall_gain)

    rows = [[], [], [], []]
    for k in range(4):
        rho, mom = moments([out_pop[i, k] for i in range(19)])
        for q, part in enumerate([rho] + mom):
            rows[q].append(part)
    values = jnp.concatenate([r for q in range(4) for r in rows[q]], axis=0)
    at_slots = dot_nn(split2(values), cell_lo[...])
    at_slots = at_slots[0:128] + at_slots[128:256]
    hot = cell_hi[...]
    slot = [
        jnp.sum(at_slots[q * 32 : q * 32 + 32] * hot, axis=0, keepdims=True) for q in range(4)
    ]
    row4 = iota((4, 128), 0)
    for g in range(4):
        at = slice(g * 128, g * 128 + 128)
        mom = jnp.zeros((4, 128), F32)
        for c in range(3):
            mom = jnp.where(row4 == c, slot[c + 1][:, at], mom)
        force = (mom - slot[0][:, at] * wall[g]) * live_ref[g : g + 1, :]
        for q in range(4):
            frc_send[g * 4 + q] = group_sum(jnp.where(group == q, force, 0.0))
    frc_recv[own] = frc_send[own]
    to_owners(lambda o: frc_send.at[o], frc_recv.at[own], s_frc, r_frc)
    wait(frc_recv.at[pl.ds(0, OWN - 1)], r_frc)

    load_ref[...] = jnp.zeros((48, 256), F32)

    def collect(b, _):
        force = frc_recv[b]
        parts = []
        for c in range(3):
            line = force[c : c + 1, :]
            line = jnp.concatenate([line] * 4, axis=1)
            parts.append(sup_hi[b] * line)
        got = dot_nt(split2(jnp.concatenate(parts, axis=0)), sup_lo[b])
        load_ref[...] += got[0:48] + got[48:96]
        return 0

    lax.fori_loop(0, OWN, collect, 0)

    row4w = iota((4, 256), 0)

    def exchange(app, sums, with_mass):
        for c in range(3):
            for h in range(17):
                rs_send[app, h, c : c + 1, :] = sums[c * 24 + h : c * 24 + h + 1, :]
        for h in range(17):
            rs_send[app, h, 3:4, :] = jnp.zeros((1, 256), F32)
        rs_recv[app, f] = rs_send[app, f]

        def go(d, _):
            j = lax.rem(f + d, FX)
            send(rs_send.at[app, j], rs_recv.at[app, f], s_rs.at[app], r_rs.at[app], (j, y, z))
            return 0

        lax.fori_loop(1, FX, go, 0)
        send(
            rs_send.at[app, 16], gh_recv.at[app, f], s_gh.at[app], r_gh.at[app],
            at_owner(before, FX - 1),
        )
        if with_mass is not None:
            to_owners(lambda o: sc_send.at[app], sc_recv.at[app, own], s_sc.at[app], r_sc.at[app])
        wait(rs_recv.at[app, pl.ds(0, FX - 1)], r_rs.at[app])
        total = rs_recv[app, 0]
        for n in range(1, FX):
            total = total + rs_recv[app, n]
        ag_send[app] = total

        @pl.when(f == FX - 1)
        def _():
            wait(gh_recv.at[app], r_gh.at[app])
            extra = gh_recv[app, 0]
            for n in range(1, FX):
                extra = extra + gh_recv[app, n]
            ag_send[app] = ag_send[app] + extra * has_after

        if with_mass is not None:
            wait(sc_recv.at[app, pl.ds(0, OWN - 1)], r_sc.at[app])
            part = sc_recv[app, 0]
            for n in range(1, OWN):
                part = part + sc_recv[app, n]
            mine = ag_send[app] + with_mass
            ag_send[app] = jnp.where(row4w == 3, jnp.concatenate([part, part], axis=1), mine)
        ag_recv[app, f] = ag_send[app]

        def spread_out(d, _):
            j = lax.rem(f + d, FX)
            send(ag_send.at[app], ag_recv.at[app, f], s_ag.at[app], r_ag.at[app], (j, y, z))
            return 0

        lax.fori_loop(1, FX, spread_out, 0)

        @pl.when(f == FX - 1)
        def _():
            def onward(j, _):
                send(
                    ag_send.at[app], ag_recv.at[app, 16], s_ag2.at[app], r_ag.at[app],
                    at_owner(after, j),
                )
                return 0

            lax.fori_loop(0, FX, onward, 0)

        wait(ag_recv.at[app, pl.ds(0, FX)], r_ag.at[app])

    def gathered(app, target):
        for c in range(3):
            for h in range(16):
                target[c * 24 + h : c * 24 + h + 1, :] = ag_recv[app, h, c : c + 1, :]
            target[c * 24 + 16 : c * 24 + 17, :] = ag_recv[app, 16, c : c + 1, :] * has_before

    kdisp = vec_w[...]
    pad8 = jnp.zeros((8, 256), F32)
    loads = []
    for c in range(3):
        loads += [FORCE_SCALE * load_ref[c * 16 : c * 16 + 16, :], pad8]
    loads.append(pad8)
    exchange(0, jnp.concatenate(loads, axis=0) - kdisp, None)
    gathered(0, vec_r)
    vec_p[...] = jnp.zeros((80, 256), F32)
    vec_s[...] = jnp.zeros((80, 256), F32)
    vec_w[...] = jnp.zeros((80, 256), F32)

    def iteration(app, carry):
        alpha, gamma = carry
        sums, picked = elements(vec_r[...])
        for c in range(3):
            rc[c : c + 1, :] = vec_r[pl.ds(c * 24 + f, 1), :]
        rc[3:4, :] = jnp.zeros((1, 256), F32)
        chunk = rc[...]
        weighted = massc[...] * chunk
        mine = jnp.sum(chunk * chunk, keepdims=True)
        energy = jnp.sum(picked * spread[...], keepdims=True) + jnp.sum(
            weighted * chunk, keepdims=True
        )
        scalars = jnp.where(lane == 0, mine, jnp.where(lane == 1, energy, 0.0))
        sc_send[app] = scalars
        sc_recv[app, own] = scalars
        exchange(app, sums, weighted)
        gathered(app, vec_w)
        both = ag_recv[app, 0]
        for n in range(1, FX):
            both = both + ag_recv[app, n]
        new = both[3:4, 0:1]
        delta = both[3:4, 1:2]
        beta = jnp.where(app == 1, 0.0, new / gamma)
        alpha = new / (delta - beta * new / alpha)
        p = vec_r[...] + beta * vec_p[...]
        s = vec_w[...] + beta * vec_s[...]
        vec_p[...] = p
        vec_s[...] = s
        vec_r[...] = vec_r[...] - alpha * s
        for c in range(3):
            vec_x[c * 16 : c * 16 + 16, :] += alpha * p[c * 24 : c * 24 + 16, :]
        return alpha, new

    one = jnp.ones((1, 1), F32)
    lax.fori_loop(1, APPS, iteration, (one, one))

    for c in range(3):
        for h in range(16):
            at = slice(h * 256, h * 256 + 256)
            out_sol[c : c + 1, at] = vec_x[c * 16 + h : c * 16 + h + 1, :]
            out_res[c : c + 1, at] = vec_r[c * 24 + h : c * 24 + h + 1, :]

    wait(sup_recv.at[pl.ds(0, OWN - 1)], s_sup)
    wait(edge_send, s_edge)
    wait(wall_recv.at[pl.ds(0, OWN - 1)], s_wall)
    wait(frc_recv.at[pl.ds(0, OWN - 1)], s_frc)
    for step, jobs in enumerate((jobs0, jobs1)):
        for n, (src, dst, device) in enumerate(jobs):
            wait(src, s_halo.at[step, n])
    for app in range(APPS):
        wait(rs_recv.at[app, pl.ds(0, FX - 1)], s_rs.at[app])
        wait(rs_send.at[app, 16], s_gh.at[app])
        if app:
            wait(sc_recv.at[app, pl.ds(0, OWN - 1)], s_sc.at[app])
        wait(ag_recv.at[app, pl.ds(0, FX - 1)], s_ag.at[app])

        @pl.when(f == FX - 1)
        def _():
            wait(ag_recv.at[app, pl.ds(0, FX)], s_ag2.at[app])


SCRATCH = dict(
    sup_send=(16, 8, 128), sup_recv=(16, 8, 128),
    wall_send=(16, 4, 128), wall_recv=(16, 4, 128),
    frc_send=(16, 4, 128), frc_recv=(16, 4, 128),
    edge_send=(4, 256), edge_recv=(4, 256),
    xs=(2, 2, 5, 8, 256), xr=(2, 2, 5, 8, 256),
    ys=(2, 2, 5, 4, 256), yr=(2, 2, 5, 4, 256),
    ds=(2, 4, 1, 256), dr=(2, 4, 1, 256),
    zs=(2, 4, 8, 128), zr=(2, 4, 8, 128), zxr=(2, 2, 8, 128),
    zys=(2, 2, 4, 128), zyr=(2, 2, 4, 128),
    rs_send=(APPS, 17, 4, 256), rs_recv=(APPS, 16, 4, 256), gh_recv=(APPS, 16, 4, 256),
    sc_send=(APPS, 1, 128), sc_recv=(APPS, 16, 1, 128),
    ag_send=(APPS, 4, 256), ag_recv=(APPS, 17, 4, 256),
    post=(19, 4, 8, 256), field=(19, 4, 8, 256), rho_ref=(4, 8, 256), gain=(3, 4, 8, 256),
    cell_lo=((256, 512), BF16), cell_hi=(32, 512), live_ref=(8, 128), wallp=((192, 512), BF16),
    sup_lo=((16, 256, 512), BF16), sup_hi=(16, 16, 512), lhs=(8, 128),
    el_lo=((8, 256, 512), BF16), el_hi=(8, 24, 512),
    pick=(24, 512), spread=(24, 512), ela=(160, 256),
    vec_r=(80, 256), vec_p=(80, 256), vec_s=(80, 256), vec_w=(80, 256), vec_x=(48, 256),
    massc=(1, 256), rc=(4, 256), load_ref=(48, 256),
)


def scratch_shapes():
    shapes = []
    for shape in SCRATCH.values():
        kind = F32
        if isinstance(shape[0], tuple):
            shape, kind = shape
        shapes.append(pltpu.VMEM(shape, kind))
    dma = pltpu.SemaphoreType.DMA
    shapes += [dma] * 8 + [dma((2, 13))] * 2 + [dma((APPS,))] * 9
    return shapes


def body(
    populations, relaxation, struct_velocity, iface_count, iface_cell, rbf_node, rbf_weight,
    disp_prev, node_mass, connect, modulus, strain_basis,
):
    vmem = pl.BlockSpec(memory_space=pltpu.VMEM)
    return pl.pallas_call(
        kernel,
        out_shape=(
            jax.ShapeDtypeStruct(populations.shape, F32),
            jax.ShapeDtypeStruct(disp_prev.shape, F32),
            jax.ShapeDtypeStruct(disp_prev.shape, F32),
        ),
        in_specs=[vmem] * 12,
        out_specs=(vmem, vmem, vmem),
        scratch_shapes=scratch_shapes(),
        compiler_params=pltpu.CompilerParams(
            has_side_effects=True, vmem_limit_bytes=48 * 1024 * 1024
        ),
        name="window",
    )(
        populations,
        relaxation,
        struct_velocity,
        iface_count.reshape(1, 16),
        iface_cell.reshape(16, 32),
        rbf_node.reshape(16, 16, 32),
        rbf_weight.reshape(16, 16, 32),
        disp_prev,
        node_mass.reshape(32, 128),
        connect.reshape(8, 512),
        modulus.reshape(1, 512),
        strain_basis,
    )


def solution(mesh):
    return jax.shard_map(
        body,
        mesh=mesh,
        in_specs=(
            P(None, "fx", "fy", "sz"),
            P("fx", "fy", "sz"),
            P(None, ("fy", "sz")),
            P("fx", "fy", "sz", None),
            P("fx", "fy", "sz", None, None),
            P("fx", "fy", "sz", None, None, None),
            P("fx", "fy", "sz", None, None, None),
            P(None, ("fy", "sz")),
            P(("fy", "sz")),
            P("fx", ("fy", "sz"), None, None),
            P("fx", ("fy", "sz"), None),
            P(),
        ),
        out_specs=(P(None, "fx", "fy", "sz"), P(None, ("fy", "sz")), P(None, ("fy", "sz"))),
        check_vma=False,
    )
```

```python
import jax
import jax.numpy as jnp
from jax import lax
from jax.experimental import pallas as pl
from jax.experimental.pallas import tpu as pltpu
from jax.sharding import PartitionSpec as P

F32 = jnp.float32
BF16 = jnp.bfloat16
I32 = jnp.int32
FX, FY, SZ = 16, 8, 2
OWN = 16
ITERS = 3
APPS = ITERS + 1
FORCE_SCALE = 20.0
VEL = [
    (0, 0, 0),
    (1, 0, 0),
    (-1, 0, 0),
    (0, 1, 0),
    (0, -1, 0),
    (0, 0, 1),
    (0, 0, -1),
    (1, 1, 0),
    (-1, -1, 0),
    (1, -1, 0),
    (-1, 1, 0),
    (1, 0, 1),
    (-1, 0, -1),
    (1, 0, -1),
    (-1, 0, 1),
    (0, 1, 1),
    (0, -1, -1),
    (0, 1, -1),
    (0, -1, 1),
]
X_POPS = [[i for i in range(19) if VEL[i][0] == s] for s in (1, -1)]
Y_POPS = [[i for i in range(19) if VEL[i][1] == s] for s in (1, -1)]
Z_POPS = [i for i in range(19) if VEL[i][2] != 0]
DIAGONAL = (7, 8, 9, 10)
MESH = pl.DeviceIdType.MESH
FAR_X = (8, 7, 9, 6, 10, 5, 11, 4, 12, 3, 13, 2, 14, 1, 15)
FAR_OWN = (
    (4, 1), (2, 1), (6, 1), (3, 1), (5, 1), (3, 0), (5, 0), (4, 0),
    (1, 1), (7, 1), (0, 1), (1, 0), (7, 0), (2, 0), (6, 0),
)
HIGH_RELAYS = (15, 7)
LOW_RELAYS = (14, 6)
INPUTS = 12


def split2(x):
    top = x.astype(BF16)
    rest = (x - top.astype(F32)).astype(BF16)
    return jnp.concatenate([top, rest], axis=0)


def dot_nt(a, b):
    return lax.dot_general(a, b, (((1,), (1,)), ((), ())), preferred_element_type=F32)


def dot_nn(a, b):
    return lax.dot_general(a, b, (((1,), (0,)), ((), ())), preferred_element_type=F32)


def exact_dot(a, b, dims=((1,), (0,))):
    return lax.dot_general(
        a, b, (dims, ((), ())), preferred_element_type=F32, precision=lax.Precision.HIGHEST
    )


def iota(shape, dim):
    return lax.broadcasted_iota(I32, shape, dim)


def group_sum(x):
    x = x + pltpu.roll(x, 64, x.ndim - 1)
    return x + pltpu.roll(x, 32, x.ndim - 1)


def send(src, dst, ssem, rsem, device):
    pltpu.make_async_remote_copy(
        src_ref=src,
        dst_ref=dst,
        send_sem=ssem,
        recv_sem=rsem,
        device_id=device,
        device_id_type=MESH,
    ).start()


def greet(f, y, z, own):
    sem = pltpu.get_barrier_semaphore()

    def tell(device):
        pl.semaphore_signal(sem, inc=1, device_id=device, device_id_type=MESH)

    for d in FAR_X:
        tell((lax.rem(f + d, FX), y, z))
    for dy, dz in FAR_OWN:
        tell((f, lax.rem(y + dy, FY), lax.rem(z + dz, SZ)))
    for dx in (1, FX - 1):
        tell((lax.rem(f + dx, FX), y, 1 - z))
        for dy in (1, FY - 1):
            tell((lax.rem(f + dx, FX), lax.rem(y + dy, FY), z))
    for relays, step in ((HIGH_RELAYS, 1), (LOW_RELAYS, OWN - 1)):
        there = lax.rem(own + step, OWN)

        for relay, first in zip(relays, (12, 4)):

            @pl.when(f == relay)
            def _():
                for n in range(8):
                    tell(((first + n) % FX, there // SZ, lax.rem(there, SZ)))

    pl.semaphore_wait(sem, 15 + 15 + 6 + 2)


def wait(ref, sem):
    pltpu.make_async_copy(ref, ref, sem).wait()


def kernel(
    pop_h, relax_h, vel_h, count_h, cell_h, node_h, weight_h, disp_h, mass_h, connect_h,
    modulus_h, basis_h,
    out_pop, out_sol, out_res,
    pop, relax, vel, count, cell, node, weight, disp, mass, connect, modulus, basis,
    sup_send, sup_recv, wall_send, wall_recv, frc_send, frc_recv, edge_send, edge_recv,
    xs, xr, ys, yr, ds, dr, zs, zr, zxr, zys, zyr,
    rs_send, rs_recv, rl_recv, sc_send, sc_recv, ag_send, ag_recv,
    post, field, rho_ref, gain, cell_lo, cell_hi, live_ref, wallp,
    sup_lo, sup_hi, el_lo, el_hi, pick, spread, vec_r, vec_p, vec_s, vec_w, vec_x,
    massx, rc, load_ref, s_in,
    s_sup, r_sup, s_wall, r_wall, s_frc, r_frc, s_edge, r_edge, s_halo, r_halo,
    s_rs, r_rs, s_rl, r_rl, s_sc, r_sc, s_ag, r_ag, s_ag2,
):
    f = lax.axis_index("fx")
    y = lax.axis_index("fy")
    z = lax.axis_index("sz")
    own = y * SZ + z

    def at_owner(o, fx=None):
        return (f if fx is None else fx, o // SZ, lax.rem(o, SZ))

    def to_owners(src_of, dst, ssem, rsem):
        for dy, dz in FAR_OWN:
            there = (f, lax.rem(y + dy, FY), lax.rem(z + dz, SZ))
            send(src_of(there[1] * SZ + there[2]), dst, ssem, rsem, there)

    inputs = [
        (node_h, node), (weight_h, weight), (disp_h, disp), (mass_h, mass), (connect_h, connect),
        (basis_h, basis), (cell_h, cell), (count_h, count), (pop_h, pop), (relax_h, relax),
        (vel_h, vel), (modulus_h, modulus),
    ]
    copies = [pltpu.make_async_copy(a, b, s_in.at[n]) for n, (a, b) in enumerate(inputs)]
    for copy in copies:
        copy.start()

    lane = iota((1, 128), 1)
    group = lane // 32
    expand = (iota((32, 128), 0) == lax.rem(iota((32, 128), 1), 32)).astype(F32)
    quarter = (lax.rem(iota((256, 128), 0), 16) // 4) == (iota((256, 128), 1) // 32)
    upper = iota((8, 128), 0) < 4
    copies[0].wait()
    copies[1].wait()
    spread_n = exact_dot(node[...].astype(F32).reshape(256, 32), expand)
    spread_w = exact_dot(weight[...].reshape(256, 32), expand)
    spread_n = jnp.where(quarter, spread_n, 0.0)
    spread_w = jnp.where(quarter, spread_w, 0.0)

    def packed(x, o):
        x = x[o * 16 : o * 16 + 8] + x[o * 16 + 8 : o * 16 + 16]
        return x + pltpu.roll(x, 4, 0)

    for o in range(OWN):
        sup_send[o] = jnp.where(upper, packed(spread_n, o), packed(spread_w, o))
    sup_recv[own] = sup_send[own]
    greet(f, y, z, own)
    to_owners(lambda o: sup_send.at[o], sup_recv.at[own], s_sup, r_sup)

    copies[2].wait()
    copies[3].wait()
    for c in range(3):
        edge_send[c : c + 1, :] = disp[c : c + 1, 3840:4096]
    massx[...] = jnp.zeros((24, 256), F32)
    for h in range(16):
        massx[h : h + 1, 0:128] = mass[2 * h : 2 * h + 1, :]
        massx[h : h + 1, 128:256] = mass[2 * h + 1 : 2 * h + 2, :]
    edge_send[3:4, :] = massx[15:16, :]
    after, before = lax.rem(own + 1, OWN), lax.rem(own + OWN - 1, OWN)
    send(edge_send, edge_recv, s_edge, r_edge, at_owner(after))

    copies[4].wait()
    copies[5].wait()
    for j in range(8):
        n = connect[j : j + 1, :]
        lo = lax.rem(n, 256)
        hi = jnp.where(n < 256, 16, n // 256 - 1)
        el_lo[j] = jnp.where(iota((256, 512), 0) == lo, 1.0, 0.0).astype(BF16)
        el_hi[j] = jnp.where(iota((24, 512), 0) == hi, 1.0, 0.0)
    base = basis[...]
    gram = exact_dot(base, base, ((0,), (0,)))

    copies[6].wait()
    copies[7].wait()
    cells = cell[...]
    cell_hi16 = exact_dot((cells // 256).astype(F32), expand)
    cell_lo16 = exact_dot(lax.rem(cells, 256).astype(F32), expand)
    diag = iota((16, 16), 0) == iota((16, 16), 1)
    counts = jnp.sum(jnp.where(diag, count[...].astype(F32), 0.0), axis=1, keepdims=True)
    live16 = (lax.rem(iota((16, 128), 1), 32).astype(F32) < counts).astype(F32)
    mine = lax.rem(iota((16, 128), 0), 4) == (iota((16, 128), 1) // 32)
    fold = ((iota((8, 16), 1) // 4) == iota((8, 16), 0)).astype(F32)

    def rows_of(x):
        return exact_dot(fold, jnp.where(mine, x, 0.0))

    hi_rows, lo_rows = rows_of(cell_hi16).astype(I32), rows_of(cell_lo16).astype(I32)
    live_ref[...] = rows_of(live16)
    for g in range(4):
        at = slice(g * 128, g * 128 + 128)
        cell_lo[:, at] = jnp.where(iota((256, 128), 0) == lo_rows[g : g + 1], 1.0, 0.0).astype(BF16)
        cell_hi[:, at] = jnp.where(iota((32, 128), 0) == hi_rows[g : g + 1], 1.0, 0.0)

    def moments(fs):
        rho = fs[0]
        for i in range(1, 19):
            rho = rho + fs[i]
        mom = []
        for a in range(3):
            total = None
            for i in range(1, 19, 2):
                s = VEL[i][a]
                if s:
                    pair = fs[i] - fs[i + 1] if s > 0 else fs[i + 1] - fs[i]
                    total = pair if total is None else total + pair
            mom.append(total)
        return rho, mom

    def along(c, v):
        total = None
        for a in range(3):
            if c[a] == 1:
                total = v[a] if total is None else total + v[a]
        for a in range(3):
            if c[a] == -1:
                total = -v[a] if total is None else total - v[a]
        return total

    def collide(source):
        for k in range(4):
            fs = [source[i, k] for i in range(19)]
            om = relax[k]
            rho, mom = moments(fs)
            inv = 1.0 / rho
            u = [m * inv for m in mom]
            sq = 1.5 * (u[0] * u[0] + u[1] * u[1] + u[2] * u[2])
            rho_ref[k] = rho
            keep = 1.0 - om
            scaled = om * rho
            post[0, k] = keep * fs[0] + (1.0 / 3.0) * scaled * (1.0 - sq)
            for i in range(1, 19, 2):
                t = (1.0 / 18.0) if i < 7 else (1.0 / 36.0)
                a = along(VEL[i], u)
                ts = t * scaled
                even = ts * (1.0 + 4.5 * a * a - sq)
                odd = ts * (3.0 * a)
                post[i, k] = keep * fs[i] + (even + odd)
                post[i + 1, k] = keep * fs[i + 1] + (even - odd)

    def turn(i, v):
        cy, cz = VEL[i][1], VEL[i][2]
        if cy:
            v = pltpu.roll(v, cy % 8, 0)
        if cz:
            v = pltpu.roll(v, cz % 256, 1)
        return v

    lane8 = iota((8, 128), 1)
    row8 = iota((8, 128), 0)

    def stream(step, target, wall_gain):
        for k in range(4):
            for c in range(3):
                gain[c, k] = wall_gain[c][k] * rho_ref[k] * (1.0 / 6.0)
        for x in range(4):
            zpack = jnp.zeros((8, 128), F32)
            for i in range(19):
                cx, cy, cz = VEL[i]
                k = (x - cx) % 4
                v = post[i, k]
                if i:
                    push = along(VEL[i], [gain[c, k] for c in range(3)])
                    v = v + (2.0 * push if i < 7 else push)
                v = turn(i, v)
                if k != x - cx:
                    side = 0 if cx > 0 else 1
                    xs[step, side, X_POPS[side].index(i)] = v
                    if cy:
                        r = 0 if cy > 0 else 7
                        ds[step, DIAGONAL.index(i)] = v[r : r + 1, :]
                else:
                    target[i, x] = v
                if cy:
                    side = 0 if cy > 0 else 1
                    r = 0 if cy > 0 else 7
                    ys[step, side, Y_POPS[side].index(i), x : x + 1, :] = v[r : r + 1, :]
                if cz:
                    col = v[:, 0:1] if cz > 0 else v[:, 255:256]
                    zpack = jnp.where(lane8 == Z_POPS.index(i), col, zpack)
            zs[step, x] = zpack
            zys[step, 0, x : x + 1, :] = zpack[0:1, :]
            zys[step, 1, x : x + 1, :] = zpack[7:8, :]
        xp, xm = lax.rem(f + 1, FX), lax.rem(f + FX - 1, FX)
        yp, ym = lax.rem(y + 1, FY), lax.rem(y + FY - 1, FY)
        zo = 1 - z
        jobs = [
            (ds.at[step, 0], dr.at[step, 0], (xp, yp, z)),
            (ds.at[step, 1], dr.at[step, 1], (xm, ym, z)),
            (ds.at[step, 2], dr.at[step, 2], (xp, ym, z)),
            (ds.at[step, 3], dr.at[step, 3], (xm, yp, z)),
            (zs.at[step, 0], zxr.at[step, 0], (xp, y, zo)),
            (zs.at[step, 3], zxr.at[step, 1], (xm, y, zo)),
            (zys.at[step, 0], zyr.at[step, 0], (f, yp, zo)),
            (zys.at[step, 1], zyr.at[step, 1], (f, ym, zo)),
            (zs.at[step], zr.at[step], (f, y, zo)),
            (ys.at[step, 0], yr.at[step, 0], (f, yp, z)),
            (ys.at[step, 1], yr.at[step, 1], (f, ym, z)),
            (xs.at[step, 0], xr.at[step, 0], (xp, y, z)),
            (xs.at[step, 1], xr.at[step, 1], (xm, y, z)),
        ]
        for n, (src, dst, device) in enumerate(jobs):
            send(src, dst, s_halo.at[step, n], r_halo.at[step, n], device)
        for n, (src, dst, device) in enumerate(jobs):
            wait(dst, r_halo.at[step, n])
        for side in range(2):
            for n, i in enumerate(X_POPS[side]):
                target[i, 0 if side == 0 else 3] = xr[step, side, n]
        for side in range(2):
            r = 0 if side == 0 else 7
            for n, i in enumerate(Y_POPS[side]):
                cx = VEL[i][0]
                for x in range(4):
                    if 0 <= x - cx <= 3:
                        target[i, x, r : r + 1, :] = yr[step, side, n, x : x + 1, :]
        for n, i in enumerate(DIAGONAL):
            cx, cy, _ = VEL[i]
            r = 0 if cy > 0 else 7
            target[i, 0 if cx > 0 else 3, r : r + 1, :] = dr[step, n]
        z11, z12, z13, z14, z15, z16, z17, z18 = [Z_POPS.index(i) for i in range(11, 19)]
        for x in range(4):
            zin = zr[step, x]
            if x == 0:
                zin = jnp.where((lane8 == z11) | (lane8 == z13), zxr[step, 0], zin)
            if x == 3:
                zin = jnp.where((lane8 == z12) | (lane8 == z14), zxr[step, 1], zin)
            low = (row8 == 0) & ((lane8 == z15) | (lane8 == z17))
            high = (row8 == 7) & ((lane8 == z16) | (lane8 == z18))
            zin = jnp.where(low, zyr[step, 0, x : x + 1, :], zin)
            zin = jnp.where(high, zyr[step, 1, x : x + 1, :], zin)
            for n, i in enumerate(Z_POPS):
                col = zin[:, n : n + 1]
                if VEL[i][2] > 0:
                    target[i, x, :, 0:128] = jnp.where(lane8 == 0, col, target[i, x, :, 0:128])
                else:
                    target[i, x, :, 128:256] = jnp.where(
                        lane8 == 127, col, target[i, x, :, 128:256]
                    )
        return jobs

    copies[8].wait()
    copies[9].wait()
    collide(pop)

    wait(sup_recv.at[pl.ds(0, OWN - 1)], r_sup)

    for b in range(OWN):
        for r in range(4):
            n = sup_recv[b, r : r + 1, :].astype(I32)
            w = sup_recv[b, r + 4 : r + 5, :]
            sup_lo[b, :, r * 128 : r * 128 + 128] = jnp.where(
                iota((256, 128), 0) == lax.rem(n, 256), 1.0, 0.0
            ).astype(BF16)
            sup_hi[b, :, r * 128 : r * 128 + 128] = jnp.where(
                iota((16, 128), 0) == n // 256, w, 0.0
            )
    copies[10].wait()
    copies[11].wait()
    for c in range(3):
        for h in range(16):
            load_ref[c * 16 + h : c * 16 + h + 1, :] = vel[c : c + 1, h * 256 : h * 256 + 256]
    table = split2(load_ref[...])

    for b in range(OWN):
        out = dot_nn(table, sup_lo[b])
        out = out[0:48] + out[48:96]
        hot = sup_hi[b]
        rows = []
        for c in range(3):
            m = out[c * 16 : c * 16 + 16] * hot
            m = m[:, 0:128] + m[:, 128:256] + m[:, 256:384] + m[:, 384:512]
            rows.append(jnp.sum(m, axis=0, keepdims=True))
        rows.append(jnp.zeros((1, 128), F32))
        for c in range(4):
            wall_send[b, c : c + 1, :] = rows[c]
    wall_recv[own] = wall_send[own]
    to_owners(lambda o: wall_send.at[o], wall_recv.at[own], s_wall, r_wall)

    def elements(values):
        both = split2(values)

        for j in range(8):
            out = dot_nn(both, el_lo[j])
            out = out[0:80] + out[80:160]
            hot = el_hi[j]
            for c in range(3):
                pick[c * 8 + j : c * 8 + j + 1, :] = jnp.sum(
                    out[c * 24 : c * 24 + 24] * hot, axis=0, keepdims=True
                )
        picked = pick[...]
        spread[...] = exact_dot(gram, picked) * modulus[...]
        total = None
        for j in range(8):
            hot = el_hi[j]
            parts = [hot * spread[c * 8 + j : c * 8 + j + 1, :] for c in range(3)]
            parts.append(jnp.zeros((8, 512), F32))
            part = dot_nt(split2(jnp.concatenate(parts, axis=0)), el_lo[j])
            total = part if total is None else total + part
        return total[0:80] + total[80:160], picked

    wait(edge_recv, r_edge)
    vec_r[...] = jnp.zeros((80, 256), F32)
    has_before = (own > 0).astype(F32)
    has_after = (own < OWN - 1).astype(F32)
    for c in range(3):
        for h in range(16):
            row = disp[c : c + 1, h * 256 : h * 256 + 256]
            vec_r[c * 24 + h : c * 24 + h + 1, :] = row
            vec_x[c * 16 + h : c * 16 + h + 1, :] = row
        vec_r[c * 24 + 16 : c * 24 + 17, :] = edge_recv[c : c + 1, :] * has_before
    vec_w[...] = elements(vec_r[...])[0]
    massx[16:17, :] = edge_recv[3:4, :]

    wait(wall_recv.at[pl.ds(0, OWN - 1)], r_wall)
    wall = [None] * 4
    for g in range(4):
        total = jnp.zeros((4, 128), F32)
        for q in range(4):
            total = jnp.where(group == q, group_sum(wall_recv[g * 4 + q]), total)
        wall[g] = total * live_ref[g : g + 1, :]
    for g in range(4):
        hot = cell_hi[:, g * 128 : g * 128 + 128]
        parts = [hot * wall[g][c : c + 1, :] for c in range(3)]
        wallp[:, g * 128 : g * 128 + 128] = split2(jnp.concatenate(parts, axis=0))
    summed = dot_nt(wallp[...], cell_lo[...])
    summed = summed[0:96] + summed[96:192]
    wall_gain = [
        [summed[c * 32 + k * 8 : c * 32 + k * 8 + 8, :] for k in range(4)] for c in range(3)
    ]

    jobs0 = stream(0, field, wall_gain)
    collide(field)
    jobs1 = stream(1, out_pop, wall_gain)

    rows = [[], [], [], []]
    for k in range(4):
        rho, mom = moments([out_pop[i, k] for i in range(19)])
        for q, part in enumerate([rho] + mom):
            rows[q].append(part)
    values = jnp.concatenate([r for q in range(4) for r in rows[q]], axis=0)
    at_slots = dot_nn(split2(values), cell_lo[...])
    at_slots = at_slots[0:128] + at_slots[128:256]
    hot = cell_hi[...]
    slot = [
        jnp.sum(at_slots[q * 32 : q * 32 + 32] * hot, axis=0, keepdims=True) for q in range(4)
    ]
    row4 = iota((4, 128), 0)
    for g in range(4):
        at = slice(g * 128, g * 128 + 128)
        mom = jnp.zeros((4, 128), F32)
        for c in range(3):
            mom = jnp.where(row4 == c, slot[c + 1][:, at], mom)
        force = (mom - slot[0][:, at] * wall[g]) * live_ref[g : g + 1, :]
        for q in range(4):
            frc_send[g * 4 + q] = group_sum(jnp.where(group == q, force, 0.0))
    frc_recv[own] = frc_send[own]
    to_owners(lambda o: frc_send.at[o], frc_recv.at[own], s_frc, r_frc)
    wait(frc_recv.at[pl.ds(0, OWN - 1)], r_frc)

    total = None
    for b in range(OWN):
        force = frc_recv[b]
        parts = []
        for c in range(3):
            line = force[c : c + 1, :]
            line = jnp.concatenate([line] * 4, axis=1)
            parts.append(sup_hi[b] * line)
        got = dot_nt(split2(jnp.concatenate(parts, axis=0)), sup_lo[b])
        total = got if total is None else total + got
    load_ref[...] = total[0:48] + total[48:96]

    row4w = iota((4, 256), 0)
    place = lax.rem(f + 4, FX)
    spot = lax.rem(place, 8)
    high = jnp.where(place < 8, HIGH_RELAYS[0], HIGH_RELAYS[1])
    low = high - 1
    is_high = (f == HIGH_RELAYS[0]) | (f == HIGH_RELAYS[1])
    is_low = (f == LOW_RELAYS[0]) | (f == LOW_RELAYS[1])
    is_double = (f == HIGH_RELAYS[1]) | is_low
    slot2 = jnp.where(f == HIGH_RELAYS[1], 16, jnp.where(f == LOW_RELAYS[0], 17, 18))
    keep_after = jnp.where(is_high, has_after, 1.0)

    def exchange(app, sums, scalars):
        for c in range(3):
            for h in range(17):
                rs_send[app, h, c : c + 1, :] = sums[c * 24 + h : c * 24 + h + 1, :]
        top, ghost = rs_send.at[app, 15], rs_send.at[app, 16]
        send(ghost, rl_recv.at[app, 8 + spot], s_rl.at[app], r_rl.at[app], at_owner(before, high))
        send(top, rl_recv.at[app, 8 + spot], s_rl.at[app], r_rl.at[app], at_owner(after, low))
        for d in FAR_X:
            j = lax.rem(f + d, FX)

            @pl.when(j < 15)
            def _():
                send(rs_send.at[app, j], rs_recv.at[app, f], s_rs.at[app], r_rs.at[app], (j, y, z))

        @pl.when(f != high)
        def _():
            send(top, rl_recv.at[app, spot], s_rl.at[app], r_rl.at[app], (high, y, z))

        @pl.when(f != low)
        def _():
            send(ghost, rl_recv.at[app, spot], s_rl.at[app], r_rl.at[app], (low, y, z))

        if scalars is not None:
            to_owners(lambda o: sc_send.at[app], sc_recv.at[app, own], s_sc.at[app], r_sc.at[app])
        rs_recv[app, f] = rs_send[app, f]

        @pl.when(f < 15)
        def _():
            wait(rs_recv.at[app, pl.ds(0, FX - 1)], r_rs.at[app])
            total = rs_recv[app, 0]
            for n in range(1, FX):
                total = total + rs_recv[app, n]
            ag_send[app, 0] = total

        @pl.when(is_high | is_low)
        def _():
            rl_recv[app, spot] = rs_send[app, jnp.where(is_high, 15, 16)]
            wait(rl_recv.at[app, pl.ds(0, 15)], r_rl.at[app])
            here, there = rl_recv[app, 0], rl_recv[app, 8]
            for n in range(1, 8):
                here = here + rl_recv[app, n]
                there = there + rl_recv[app, 8 + n]
            ag_send[app, 1] = here + keep_after * there

        @pl.when(is_double)
        def _():
            ag_recv[app, slot2] = ag_send[app, 1]
            for d in FAR_X:
                send(
                    ag_send.at[app, 1], ag_recv.at[app, slot2], s_ag2.at[app], r_ag.at[app],
                    (lax.rem(f + d, FX), y, z),
                )

        @pl.when(f == 15)
        def _():
            ag_send[app, 0] = ag_send[app, 1]

        if scalars is not None:
            wait(sc_recv.at[app, pl.ds(0, OWN - 1)], r_sc.at[app])
            part = sc_recv[app, 0]
            for n in range(1, OWN):
                part = part + sc_recv[app, n]
            ag_send[app, 0] = jnp.where(
                row4w == 3, jnp.concatenate([part, part], axis=1), ag_send[app, 0]
            )
        for d in FAR_X:
            send(
                ag_send.at[app, 0], ag_recv.at[app, f], s_ag.at[app], r_ag.at[app],
                (lax.rem(f + d, FX), y, z),
            )
        ag_recv[app, f] = ag_send[app, 0]

        @pl.when(is_double)
        def _():
            wait(ag_recv.at[app, pl.ds(0, 17)], r_ag.at[app])

        @pl.when(jnp.logical_not(is_double))
        def _():
            wait(ag_recv.at[app, pl.ds(0, 18)], r_ag.at[app])

    def gathered(app, target):
        for c in range(3):
            for h in range(15):
                target[c * 24 + h : c * 24 + h + 1, :] = ag_recv[app, h, c : c + 1, :]
            target[c * 24 + 15 : c * 24 + 16, :] = (
                ag_recv[app, 15, c : c + 1, :] + ag_recv[app, 16, c : c + 1, :]
            )
            target[c * 24 + 16 : c * 24 + 17, :] = has_before * (
                ag_recv[app, 17, c : c + 1, :] + ag_recv[app, 18, c : c + 1, :]
            )

    kdisp = vec_w[...]
    pad8 = jnp.zeros((8, 256), F32)
    loads = []
    for c in range(3):
        loads += [FORCE_SCALE * load_ref[c * 16 : c * 16 + 16, :], pad8]
    loads.append(pad8)
    exchange(0, jnp.concatenate(loads, axis=0) - kdisp, None)
    gathered(0, vec_r)
    vec_p[...] = jnp.zeros((80, 256), F32)
    vec_s[...] = jnp.zeros((80, 256), F32)
    vec_w[...] = jnp.zeros((80, 256), F32)

    def iteration(app, carry):
        alpha, gamma = carry
        sums, picked = elements(vec_r[...])
        for c in range(3):
            rc[c : c + 1, :] = vec_r[pl.ds(c * 24 + f, 1), :]
        rc[3:4, :] = jnp.zeros((1, 256), F32)
        chunk = rc[...]
        weighted = massx[pl.ds(f, 1), :] * chunk
        mine = jnp.sum(chunk * chunk, keepdims=True)
        energy = jnp.sum(picked * spread[...], keepdims=True) + jnp.sum(
            weighted * chunk, keepdims=True
        )
        scalars = jnp.where(lane == 0, mine, jnp.where(lane == 1, energy, 0.0))
        sc_send[app] = scalars
        sc_recv[app, own] = scalars
        exchange(app, sums, scalars)
        gathered(app, vec_w)
        both = ag_recv[app, 0]
        for n in range(1, FX):
            both = both + ag_recv[app, n]
        new = both[3:4, 0:1]
        delta = both[3:4, 1:2]
        beta = jnp.where(app == 1, 0.0, new / gamma)
        alpha = new / (delta - beta * new / alpha)
        weights = massx[...]
        weights = jnp.concatenate([weights] * 3 + [pad8], axis=0)
        p = vec_r[...] + beta * vec_p[...]
        s = vec_w[...] + weights * vec_r[...] + beta * vec_s[...]
        vec_p[...] = p
        vec_s[...] = s
        vec_r[...] = vec_r[...] - alpha * s
        for c in range(3):
            vec_x[c * 16 : c * 16 + 16, :] += alpha * p[c * 24 : c * 24 + 16, :]
        return alpha, new

    one = jnp.ones((1, 1), F32)
    lax.fori_loop(1, APPS, iteration, (one, one))

    for c in range(3):
        for h in range(16):
            at = slice(h * 256, h * 256 + 256)
            out_sol[c : c + 1, at] = vec_x[c * 16 + h : c * 16 + h + 1, :]
            out_res[c : c + 1, at] = vec_r[c * 24 + h : c * 24 + h + 1, :]

    wait(sup_recv.at[pl.ds(0, OWN - 1)], s_sup)
    wait(edge_send, s_edge)
    wait(wall_recv.at[pl.ds(0, OWN - 1)], s_wall)
    wait(frc_recv.at[pl.ds(0, OWN - 1)], s_frc)
    for step, jobs in enumerate((jobs0, jobs1)):
        for n, (src, dst, device) in enumerate(jobs):
            wait(src, s_halo.at[step, n])
    for app in range(APPS):
        wait(rs_recv.at[app, pl.ds(0, 14)], s_rs.at[app])
        wait(rs_recv.at[app, pl.ds(0, 3)], s_rl.at[app])
        if app:
            wait(sc_recv.at[app, pl.ds(0, OWN - 1)], s_sc.at[app])
        wait(ag_recv.at[app, pl.ds(0, FX - 1)], s_ag.at[app])

        @pl.when(f == 15)
        def _():
            wait(rs_recv.at[app, 0], s_rs.at[app])

        @pl.when(jnp.logical_not(is_high | is_low))
        def _():
            wait(rs_recv.at[app, 0], s_rl.at[app])

        @pl.when(is_double)
        def _():
            wait(ag_recv.at[app, pl.ds(0, FX - 1)], s_ag2.at[app])


SCRATCH = dict(
    pop=(19, 4, 8, 256), relax=(4, 8, 256), vel=(3, 4096), count=((1, 16), I32),
    cell=((16, 32), I32), node=((16, 16, 32), I32), weight=(16, 16, 32), disp=(3, 4096),
    mass=(32, 128), connect=((8, 512), I32), modulus=(1, 512), basis=(24, 24),
    sup_send=(16, 8, 128), sup_recv=(16, 8, 128),
    wall_send=(16, 4, 128), wall_recv=(16, 4, 128),
    frc_send=(16, 4, 128), frc_recv=(16, 4, 128),
    edge_send=(4, 256), edge_recv=(4, 256),
    xs=(2, 2, 5, 8, 256), xr=(2, 2, 5, 8, 256),
    ys=(2, 2, 5, 4, 256), yr=(2, 2, 5, 4, 256),
    ds=(2, 4, 1, 256), dr=(2, 4, 1, 256),
    zs=(2, 4, 8, 128), zr=(2, 4, 8, 128), zxr=(2, 2, 8, 128),
    zys=(2, 2, 4, 128), zyr=(2, 2, 4, 128),
    rs_send=(APPS, 17, 4, 256), rs_recv=(APPS, 16, 4, 256), rl_recv=(APPS, 16, 4, 256),
    sc_send=(APPS, 1, 128), sc_recv=(APPS, 16, 1, 128),
    ag_send=(APPS, 2, 4, 256), ag_recv=(APPS, 19, 4, 256),
    post=(19, 4, 8, 256), field=(19, 4, 8, 256), rho_ref=(4, 8, 256), gain=(3, 4, 8, 256),
    cell_lo=((256, 512), BF16), cell_hi=(32, 512), live_ref=(8, 128), wallp=((192, 512), BF16),
    sup_lo=((16, 256, 512), BF16), sup_hi=(16, 16, 512),
    el_lo=((8, 256, 512), BF16), el_hi=(8, 24, 512),
    pick=(24, 512), spread=(24, 512),
    vec_r=(80, 256), vec_p=(80, 256), vec_s=(80, 256), vec_w=(80, 256), vec_x=(48, 256),
    massx=(24, 256), rc=(4, 256), load_ref=(48, 256),
)


def scratch_shapes():
    shapes = []
    for shape in SCRATCH.values():
        kind = F32
        if isinstance(shape[0], tuple):
            shape, kind = shape
        shapes.append(pltpu.VMEM(shape, kind))
    dma = pltpu.SemaphoreType.DMA
    shapes += [dma((INPUTS,))] + [dma] * 8 + [dma((2, 13))] * 2 + [dma((APPS,))] * 9
    return shapes


def body(
    populations, relaxation, struct_velocity, iface_count, iface_cell, rbf_node, rbf_weight,
    disp_prev, node_mass, connect, modulus, strain_basis,
):
    vmem = pl.BlockSpec(memory_space=pltpu.VMEM)
    hbm = pl.BlockSpec(memory_space=pl.ANY)
    return pl.pallas_call(
        kernel,
        out_shape=(
            jax.ShapeDtypeStruct(populations.shape, F32),
            jax.ShapeDtypeStruct(disp_prev.shape, F32),
            jax.ShapeDtypeStruct(disp_prev.shape, F32),
        ),
        in_specs=[hbm] * INPUTS,
        out_specs=(vmem, vmem, vmem),
        scratch_shapes=scratch_shapes(),
        compiler_params=pltpu.CompilerParams(
            collective_id=0, has_side_effects=True, vmem_limit_bytes=48 * 1024 * 1024
        ),
        name="window",
    )(
        populations,
        relaxation,
        struct_velocity,
        iface_count.reshape(1, 16),
        iface_cell.reshape(16, 32),
        rbf_node.reshape(16, 16, 32),
        rbf_weight.reshape(16, 16, 32),
        disp_prev,
        node_mass.reshape(32, 128),
        connect.reshape(8, 512),
        modulus.reshape(1, 512),
        strain_basis,
    )


def solution(mesh):
    return jax.shard_map(
        body,
        mesh=mesh,
        in_specs=(
            P(None, "fx", "fy", "sz"),
            P("fx", "fy", "sz"),
            P(None, ("fy", "sz")),
            P("fx", "fy", "sz", None),
            P("fx", "fy", "sz", None, None),
            P("fx", "fy", "sz", None, None, None),
            P("fx", "fy", "sz", None, None, None),
            P(None, ("fy", "sz")),
            P(("fy", "sz")),
            P("fx", ("fy", "sz"), None, None),
            P("fx", ("fy", "sz"), None),
            P(),
        ),
        out_specs=(P(None, "fx", "fy", "sz"), P(None, ("fy", "sz")), P(None, ("fy", "sz"))),
        check_vma=False,
    )
```

```python
import jax
import jax.numpy as jnp
from jax import lax
from jax.experimental import pallas as pl
from jax.experimental.pallas import tpu as pltpu
from jax.sharding import PartitionSpec as P

F32 = jnp.float32
BF16 = jnp.bfloat16
I32 = jnp.int32
FX, FY, SZ = 16, 8, 2
OWN = 16
ITERS = 3
APPS = ITERS + 1
FORCE_SCALE = 20.0
VEL = [
    (0, 0, 0),
    (1, 0, 0),
    (-1, 0, 0),
    (0, 1, 0),
    (0, -1, 0),
    (0, 0, 1),
    (0, 0, -1),
    (1, 1, 0),
    (-1, -1, 0),
    (1, -1, 0),
    (-1, 1, 0),
    (1, 0, 1),
    (-1, 0, -1),
    (1, 0, -1),
    (-1, 0, 1),
    (0, 1, 1),
    (0, -1, -1),
    (0, 1, -1),
    (0, -1, 1),
]
X_POPS = [[i for i in range(19) if VEL[i][0] == s] for s in (1, -1)]
Y_POPS = [[i for i in range(19) if VEL[i][1] == s] for s in (1, -1)]
Z_POPS = [i for i in range(19) if VEL[i][2] != 0]
DIAGONAL = (7, 8, 9, 10)
MESH = pl.DeviceIdType.MESH
FAR_X = (8, 7, 9, 6, 10, 5, 11, 4, 12, 3, 13, 2, 14, 1, 15)
FAR_OWN = (
    (4, 1), (2, 1), (6, 1), (3, 1), (5, 1), (3, 0), (5, 0), (4, 0),
    (1, 1), (7, 1), (0, 1), (1, 0), (7, 0), (2, 0), (6, 0),
)
HIGH_RELAYS = (15, 7)
LOW_RELAYS = (14, 6)
INPUTS = 12


def split2(x):
    top = x.astype(BF16)
    rest = (x - top.astype(F32)).astype(BF16)
    return jnp.concatenate([top, rest], axis=0)


def dot_nt(a, b):
    return lax.dot_general(a, b, (((1,), (1,)), ((), ())), preferred_element_type=F32)


def dot_nn(a, b):
    return lax.dot_general(a, b, (((1,), (0,)), ((), ())), preferred_element_type=F32)


def exact_dot(a, b, dims=((1,), (0,))):
    return lax.dot_general(
        a, b, (dims, ((), ())), preferred_element_type=F32, precision=lax.Precision.HIGHEST
    )


def iota(shape, dim):
    return lax.broadcasted_iota(I32, shape, dim)


def group_sum(x):
    x = x + pltpu.roll(x, 64, x.ndim - 1)
    return x + pltpu.roll(x, 32, x.ndim - 1)


def send(src, dst, ssem, rsem, device):
    pltpu.make_async_remote_copy(
        src_ref=src,
        dst_ref=dst,
        send_sem=ssem,
        recv_sem=rsem,
        device_id=device,
        device_id_type=MESH,
    ).start()


def greet(f, y, z, own):
    sem = pltpu.get_barrier_semaphore()

    def tell(device):
        pl.semaphore_signal(sem, inc=1, device_id=device, device_id_type=MESH)

    for d in FAR_X:
        tell((lax.rem(f + d, FX), y, z))
    for dy, dz in FAR_OWN:
        tell((f, lax.rem(y + dy, FY), lax.rem(z + dz, SZ)))
    for dx in (1, FX - 1):
        tell((lax.rem(f + dx, FX), y, 1 - z))
        for dy in (1, FY - 1):
            tell((lax.rem(f + dx, FX), lax.rem(y + dy, FY), z))
    for relays, step in ((HIGH_RELAYS, 1), (LOW_RELAYS, OWN - 1)):
        there = lax.rem(own + step, OWN)

        for relay, first in zip(relays, (12, 4)):

            @pl.when(f == relay)
            def _():
                for n in range(8):
                    tell(((first + n) % FX, there // SZ, lax.rem(there, SZ)))

    pl.semaphore_wait(sem, 15 + 15 + 6 + 2)


def wait(ref, sem):
    pltpu.make_async_copy(ref, ref, sem).wait()


def kernel(
    pop_h, relax_h, vel_h, count_h, cell_h, node_h, weight_h, disp_h, mass_h, connect_h,
    modulus_h, basis_h,
    out_pop_h, out_sol, out_res,
    pop, relax, vel, count, cell, node, weight, disp, mass, connect, modulus, basis,
    sup_send, sup_recv, wall_send, wall_recv, frc_send, frc_recv, edge_send, edge_recv,
    xs, xr, ys, yr, ds, dr, zs, zr, zxr, zys, zyr,
    rs_send, rs_recv, rl_recv, sc_send, sc_recv, ag_send, ag_recv,
    post, field, rho_ref, gain, cell_lo, cell_hi, live_ref, wallp,
    sup_lo, sup_hi, el_lo, el_hi, pick, spread, vec_r, vec_p, vec_s, vec_w, vec_x,
    massx, rc, load_ref, out_pop, s_in, s_out,
    s_sup, r_sup, s_wall, r_wall, s_frc, r_frc, s_edge, r_edge, s_halo, r_halo,
    s_rs, r_rs, s_rl, r_rl, s_sc, r_sc, s_ag, r_ag, s_ag2,
):
    f = lax.axis_index("fx")
    y = lax.axis_index("fy")
    z = lax.axis_index("sz")
    own = y * SZ + z

    def at_owner(o, fx=None):
        return (f if fx is None else fx, o // SZ, lax.rem(o, SZ))

    def to_owners(src_of, dst, ssem, rsem):
        for dy, dz in FAR_OWN:
            there = (f, lax.rem(y + dy, FY), lax.rem(z + dz, SZ))
            send(src_of(there[1] * SZ + there[2]), dst, ssem, rsem, there)

    inputs = [
        (node_h, node), (weight_h, weight), (disp_h, disp), (mass_h, mass), (connect_h, connect),
        (basis_h, basis), (cell_h, cell), (count_h, count), (pop_h, pop), (relax_h, relax),
        (vel_h, vel), (modulus_h, modulus),
    ]
    copies = [pltpu.make_async_copy(a, b, s_in.at[n]) for n, (a, b) in enumerate(inputs)]
    for copy in copies:
        copy.start()

    lane = iota((1, 128), 1)
    group = lane // 32
    expand = (iota((32, 128), 0) == lax.rem(iota((32, 128), 1), 32)).astype(F32)
    quarter = (lax.rem(iota((256, 128), 0), 16) // 4) == (iota((256, 128), 1) // 32)
    upper = iota((8, 128), 0) < 4
    copies[0].wait()
    copies[1].wait()
    spread_n = exact_dot(node[...].astype(F32).reshape(256, 32), expand)
    spread_w = exact_dot(weight[...].reshape(256, 32), expand)
    spread_n = jnp.where(quarter, spread_n, 0.0)
    spread_w = jnp.where(quarter, spread_w, 0.0)

    def packed(x, o):
        x = x[o * 16 : o * 16 + 8] + x[o * 16 + 8 : o * 16 + 16]
        return x + pltpu.roll(x, 4, 0)

    for o in range(OWN):
        sup_send[o] = jnp.where(upper, packed(spread_n, o), packed(spread_w, o))
    sup_recv[own] = sup_send[own]
    greet(f, y, z, own)
    to_owners(lambda o: sup_send.at[o], sup_recv.at[own], s_sup, r_sup)

    copies[2].wait()
    copies[3].wait()
    for c in range(3):
        edge_send[c : c + 1, :] = disp[c : c + 1, 3840:4096]
    massx[...] = jnp.zeros((24, 256), F32)
    for h in range(16):
        massx[h : h + 1, 0:128] = mass[2 * h : 2 * h + 1, :]
        massx[h : h + 1, 128:256] = mass[2 * h + 1 : 2 * h + 2, :]
    edge_send[3:4, :] = massx[15:16, :]
    after, before = lax.rem(own + 1, OWN), lax.rem(own + OWN - 1, OWN)
    send(edge_send, edge_recv, s_edge, r_edge, at_owner(after))

    copies[4].wait()
    copies[5].wait()
    for j in range(8):
        n = connect[j : j + 1, :]
        lo = lax.rem(n, 256)
        hi = jnp.where(n < 256, 16, n // 256 - 1)
        el_lo[j] = jnp.where(iota((256, 512), 0) == lo, 1.0, 0.0).astype(BF16)
        el_hi[j] = jnp.where(iota((24, 512), 0) == hi, 1.0, 0.0)
    base = basis[...]
    gram = exact_dot(base, base, ((0,), (0,)))

    copies[6].wait()
    copies[7].wait()
    cells = cell[...]
    cell_hi16 = exact_dot((cells // 256).astype(F32), expand)
    cell_lo16 = exact_dot(lax.rem(cells, 256).astype(F32), expand)
    diag = iota((16, 16), 0) == iota((16, 16), 1)
    counts = jnp.sum(jnp.where(diag, count[...].astype(F32), 0.0), axis=1, keepdims=True)
    live16 = (lax.rem(iota((16, 128), 1), 32).astype(F32) < counts).astype(F32)
    mine = lax.rem(iota((16, 128), 0), 4) == (iota((16, 128), 1) // 32)
    fold = ((iota((8, 16), 1) // 4) == iota((8, 16), 0)).astype(F32)

    def rows_of(x):
        return exact_dot(fold, jnp.where(mine, x, 0.0))

    hi_rows, lo_rows = rows_of(cell_hi16).astype(I32), rows_of(cell_lo16).astype(I32)
    live_ref[...] = rows_of(live16)
    for g in range(4):
        at = slice(g * 128, g * 128 + 128)
        cell_lo[:, at] = jnp.where(iota((256, 128), 0) == lo_rows[g : g + 1], 1.0, 0.0).astype(BF16)
        cell_hi[:, at] = jnp.where(iota((32, 128), 0) == hi_rows[g : g + 1], 1.0, 0.0)

    def moments(fs):
        rho = fs[0]
        for i in range(1, 19):
            rho = rho + fs[i]
        mom = []
        for a in range(3):
            total = None
            for i in range(1, 19, 2):
                s = VEL[i][a]
                if s:
                    pair = fs[i] - fs[i + 1] if s > 0 else fs[i + 1] - fs[i]
                    total = pair if total is None else total + pair
            mom.append(total)
        return rho, mom

    def along(c, v):
        total = None
        for a in range(3):
            if c[a] == 1:
                total = v[a] if total is None else total + v[a]
        for a in range(3):
            if c[a] == -1:
                total = -v[a] if total is None else total - v[a]
        return total

    def collide(source):
        for k in range(4):
            fs = [source[i, k] for i in range(19)]
            om = relax[k]
            rho, mom = moments(fs)
            inv = 1.0 / rho
            u = [m * inv for m in mom]
            sq = 1.5 * (u[0] * u[0] + u[1] * u[1] + u[2] * u[2])
            rho_ref[k] = rho
            keep = 1.0 - om
            scaled = om * rho
            post[0, k] = keep * fs[0] + (1.0 / 3.0) * scaled * (1.0 - sq)
            for i in range(1, 19, 2):
                t = (1.0 / 18.0) if i < 7 else (1.0 / 36.0)
                a = along(VEL[i], u)
                ts = t * scaled
                even = ts * (1.0 + 4.5 * a * a - sq)
                odd = ts * (3.0 * a)
                post[i, k] = keep * fs[i] + (even + odd)
                post[i + 1, k] = keep * fs[i + 1] + (even - odd)

    def turn(i, v):
        cy, cz = VEL[i][1], VEL[i][2]
        if cy:
            v = pltpu.roll(v, cy % 8, 0)
        if cz:
            v = pltpu.roll(v, cz % 256, 1)
        return v

    lane8 = iota((8, 128), 1)
    row8 = iota((8, 128), 0)

    def stream(step, target, wall_gain):
        for k in range(4):
            for c in range(3):
                gain[c, k] = wall_gain[c][k] * rho_ref[k] * (1.0 / 6.0)
        for x in range(4):
            zpack = jnp.zeros((8, 128), F32)
            for i in range(19):
                cx, cy, cz = VEL[i]
                k = (x - cx) % 4
                v = post[i, k]
                if i:
                    push = along(VEL[i], [gain[c, k] for c in range(3)])
                    v = v + (2.0 * push if i < 7 else push)
                v = turn(i, v)
                if k != x - cx:
                    side = 0 if cx > 0 else 1
                    xs[step, side, X_POPS[side].index(i)] = v
                    if cy:
                        r = 0 if cy > 0 else 7
                        ds[step, DIAGONAL.index(i)] = v[r : r + 1, :]
                else:
                    target[i, x] = v
                if cy:
                    side = 0 if cy > 0 else 1
                    r = 0 if cy > 0 else 7
                    ys[step, side, Y_POPS[side].index(i), x : x + 1, :] = v[r : r + 1, :]
                if cz:
                    col = v[:, 0:1] if cz > 0 else v[:, 255:256]
                    zpack = jnp.where(lane8 == Z_POPS.index(i), col, zpack)
            zs[step, x] = zpack
            zys[step, 0, x : x + 1, :] = zpack[0:1, :]
            zys[step, 1, x : x + 1, :] = zpack[7:8, :]
        xp, xm = lax.rem(f + 1, FX), lax.rem(f + FX - 1, FX)
        yp, ym = lax.rem(y + 1, FY), lax.rem(y + FY - 1, FY)
        zo = 1 - z
        jobs = [
            (ds.at[step, 0], dr.at[step, 0], (xp, yp, z)),
            (ds.at[step, 1], dr.at[step, 1], (xm, ym, z)),
            (ds.at[step, 2], dr.at[step, 2], (xp, ym, z)),
            (ds.at[step, 3], dr.at[step, 3], (xm, yp, z)),
            (zs.at[step, 0], zxr.at[step, 0], (xp, y, zo)),
            (zs.at[step, 3], zxr.at[step, 1], (xm, y, zo)),
            (zys.at[step, 0], zyr.at[step, 0], (f, yp, zo)),
            (zys.at[step, 1], zyr.at[step, 1], (f, ym, zo)),
            (zs.at[step], zr.at[step], (f, y, zo)),
            (ys.at[step, 0], yr.at[step, 0], (f, yp, z)),
            (ys.at[step, 1], yr.at[step, 1], (f, ym, z)),
            (xs.at[step, 0], xr.at[step, 0], (xp, y, z)),
            (xs.at[step, 1], xr.at[step, 1], (xm, y, z)),
        ]
        for n, (src, dst, device) in enumerate(jobs):
            send(src, dst, s_halo.at[step, n], r_halo.at[step, n], device)
        for n, (src, dst, device) in enumerate(jobs):
            wait(dst, r_halo.at[step, n])
        for side in range(2):
            for n, i in enumerate(X_POPS[side]):
                target[i, 0 if side == 0 else 3] = xr[step, side, n]
        for side in range(2):
            r = 0 if side == 0 else 7
            for n, i in enumerate(Y_POPS[side]):
                cx = VEL[i][0]
                for x in range(4):
                    if 0 <= x - cx <= 3:
                        target[i, x, r : r + 1, :] = yr[step, side, n, x : x + 1, :]
        for n, i in enumerate(DIAGONAL):
            cx, cy, _ = VEL[i]
            r = 0 if cy > 0 else 7
            target[i, 0 if cx > 0 else 3, r : r + 1, :] = dr[step, n]
        z11, z12, z13, z14, z15, z16, z17, z18 = [Z_POPS.index(i) for i in range(11, 19)]
        for x in range(4):
            zin = zr[step, x]
            if x == 0:
                zin = jnp.where((lane8 == z11) | (lane8 == z13), zxr[step, 0], zin)
            if x == 3:
                zin = jnp.where((lane8 == z12) | (lane8 == z14), zxr[step, 1], zin)
            low = (row8 == 0) & ((lane8 == z15) | (lane8 == z17))
            high = (row8 == 7) & ((lane8 == z16) | (lane8 == z18))
            zin = jnp.where(low, zyr[step, 0, x : x + 1, :], zin)
            zin = jnp.where(high, zyr[step, 1, x : x + 1, :], zin)
            for n, i in enumerate(Z_POPS):
                col = zin[:, n : n + 1]
                if VEL[i][2] > 0:
                    target[i, x, :, 0:128] = jnp.where(lane8 == 0, col, target[i, x, :, 0:128])
                else:
                    target[i, x, :, 128:256] = jnp.where(
                        lane8 == 127, col, target[i, x, :, 128:256]
                    )
        return jobs

    copies[8].wait()
    copies[9].wait()
    collide(pop)

    wait(sup_recv.at[pl.ds(0, OWN - 1)], r_sup)

    for b in range(OWN):
        for r in range(4):
            n = sup_recv[b, r : r + 1, :].astype(I32)
            w = sup_recv[b, r + 4 : r + 5, :]
            sup_lo[b, :, r * 128 : r * 128 + 128] = jnp.where(
                iota((256, 128), 0) == lax.rem(n, 256), 1.0, 0.0
            ).astype(BF16)
            sup_hi[b, :, r * 128 : r * 128 + 128] = jnp.where(
                iota((16, 128), 0) == n // 256, w, 0.0
            )
    copies[10].wait()
    copies[11].wait()
    for c in range(3):
        for h in range(16):
            load_ref[c * 16 + h : c * 16 + h + 1, :] = vel[c : c + 1, h * 256 : h * 256 + 256]
    table = split2(load_ref[...])

    for b in range(OWN):
        out = dot_nn(table, sup_lo[b])
        out = out[0:48] + out[48:96]
        hot = sup_hi[b]
        rows = []
        for c in range(3):
            m = out[c * 16 : c * 16 + 16] * hot
            m = m[:, 0:128] + m[:, 128:256] + m[:, 256:384] + m[:, 384:512]
            rows.append(jnp.sum(m, axis=0, keepdims=True))
        rows.append(jnp.zeros((1, 128), F32))
        for c in range(4):
            wall_send[b, c : c + 1, :] = rows[c]
    wall_recv[own] = wall_send[own]
    to_owners(lambda o: wall_send.at[o], wall_recv.at[own], s_wall, r_wall)

    def elements(values):
        both = split2(values)

        for j in range(8):
            out = dot_nn(both, el_lo[j])
            out = out[0:80] + out[80:160]
            hot = el_hi[j]
            for c in range(3):
                pick[c * 8 + j : c * 8 + j + 1, :] = jnp.sum(
                    out[c * 24 : c * 24 + 24] * hot, axis=0, keepdims=True
                )
        picked = pick[...]
        spread[...] = exact_dot(gram, picked) * modulus[...]
        total = None
        for j in range(8):
            hot = el_hi[j]
            parts = [hot * spread[c * 8 + j : c * 8 + j + 1, :] for c in range(3)]
            parts.append(jnp.zeros((8, 512), F32))
            part = dot_nt(split2(jnp.concatenate(parts, axis=0)), el_lo[j])
            total = part if total is None else total + part
        return total[0:80] + total[80:160], picked

    wait(edge_recv, r_edge)
    vec_r[...] = jnp.zeros((80, 256), F32)
    has_before = (own > 0).astype(F32)
    has_after = (own < OWN - 1).astype(F32)
    for c in range(3):
        for h in range(16):
            row = disp[c : c + 1, h * 256 : h * 256 + 256]
            vec_r[c * 24 + h : c * 24 + h + 1, :] = row
            vec_x[c * 16 + h : c * 16 + h + 1, :] = row
        vec_r[c * 24 + 16 : c * 24 + 17, :] = edge_recv[c : c + 1, :] * has_before
    vec_w[...] = elements(vec_r[...])[0]
    massx[16:17, :] = edge_recv[3:4, :]

    wait(wall_recv.at[pl.ds(0, OWN - 1)], r_wall)
    wall = [None] * 4
    for g in range(4):
        total = jnp.zeros((4, 128), F32)
        for q in range(4):
            total = jnp.where(group == q, group_sum(wall_recv[g * 4 + q]), total)
        wall[g] = total * live_ref[g : g + 1, :]
    for g in range(4):
        hot = cell_hi[:, g * 128 : g * 128 + 128]
        parts = [hot * wall[g][c : c + 1, :] for c in range(3)]
        wallp[:, g * 128 : g * 128 + 128] = split2(jnp.concatenate(parts, axis=0))
    summed = dot_nt(wallp[...], cell_lo[...])
    summed = summed[0:96] + summed[96:192]
    wall_gain = [
        [summed[c * 32 + k * 8 : c * 32 + k * 8 + 8, :] for k in range(4)] for c in range(3)
    ]

    jobs0 = stream(0, field, wall_gain)
    collide(field)
    jobs1 = stream(1, out_pop, wall_gain)

    pop_copy = pltpu.make_async_copy(out_pop, out_pop_h, s_out)
    pop_copy.start()

    rows = [[], [], [], []]
    for k in range(4):
        rho, mom = moments([out_pop[i, k] for i in range(19)])
        for q, part in enumerate([rho] + mom):
            rows[q].append(part)
    values = jnp.concatenate([r for q in range(4) for r in rows[q]], axis=0)
    at_slots = dot_nn(split2(values), cell_lo[...])
    at_slots = at_slots[0:128] + at_slots[128:256]
    hot = cell_hi[...]
    slot = [
        jnp.sum(at_slots[q * 32 : q * 32 + 32] * hot, axis=0, keepdims=True) for q in range(4)
    ]
    row4 = iota((4, 128), 0)
    for g in range(4):
        at = slice(g * 128, g * 128 + 128)
        mom = jnp.zeros((4, 128), F32)
        for c in range(3):
            mom = jnp.where(row4 == c, slot[c + 1][:, at], mom)
        force = (mom - slot[0][:, at] * wall[g]) * live_ref[g : g + 1, :]
        for q in range(4):
            frc_send[g * 4 + q] = group_sum(jnp.where(group == q, force, 0.0))
    frc_recv[own] = frc_send[own]
    to_owners(lambda o: frc_send.at[o], frc_recv.at[own], s_frc, r_frc)
    wait(frc_recv.at[pl.ds(0, OWN - 1)], r_frc)

    total = None
    for b in range(OWN):
        force = frc_recv[b]
        parts = []
        for c in range(3):
            line = force[c : c + 1, :]
            line = jnp.concatenate([line] * 4, axis=1)
            parts.append(sup_hi[b] * line)
        got = dot_nt(split2(jnp.concatenate(parts, axis=0)), sup_lo[b])
        total = got if total is None else total + got
    load_ref[...] = total[0:48] + total[48:96]

    row4w = iota((4, 256), 0)
    place = lax.rem(f + 4, FX)
    spot = lax.rem(place, 8)
    high = jnp.where(place < 8, HIGH_RELAYS[0], HIGH_RELAYS[1])
    low = high - 1
    is_high = (f == HIGH_RELAYS[0]) | (f == HIGH_RELAYS[1])
    is_low = (f == LOW_RELAYS[0]) | (f == LOW_RELAYS[1])
    is_double = (f == HIGH_RELAYS[1]) | is_low
    slot2 = jnp.where(f == HIGH_RELAYS[1], 16, jnp.where(f == LOW_RELAYS[0], 17, 18))
    keep_after = jnp.where(is_high, has_after, 1.0)

    def exchange(app, sums, scalars):
        for c in range(3):
            for h in range(17):
                rs_send[app, h, c : c + 1, :] = sums[c * 24 + h : c * 24 + h + 1, :]
        top, ghost = rs_send.at[app, 15], rs_send.at[app, 16]
        send(ghost, rl_recv.at[app, 8 + spot], s_rl.at[app], r_rl.at[app], at_owner(before, high))
        send(top, rl_recv.at[app, 8 + spot], s_rl.at[app], r_rl.at[app], at_owner(after, low))
        for d in FAR_X:
            j = lax.rem(f + d, FX)

            @pl.when(j < 15)
            def _():
                send(rs_send.at[app, j], rs_recv.at[app, f], s_rs.at[app], r_rs.at[app], (j, y, z))

        @pl.when(f != high)
        def _():
            send(top, rl_recv.at[app, spot], s_rl.at[app], r_rl.at[app], (high, y, z))

        @pl.when(f != low)
        def _():
            send(ghost, rl_recv.at[app, spot], s_rl.at[app], r_rl.at[app], (low, y, z))

        if scalars is not None:
            to_owners(lambda o: sc_send.at[app], sc_recv.at[app, own], s_sc.at[app], r_sc.at[app])
        rs_recv[app, f] = rs_send[app, f]

        @pl.when(f < 15)
        def _():
            wait(rs_recv.at[app, pl.ds(0, FX - 1)], r_rs.at[app])
            total = rs_recv[app, 0]
            for n in range(1, FX):
                total = total + rs_recv[app, n]
            ag_send[app, 0] = total

        @pl.when(is_high | is_low)
        def _():
            rl_recv[app, spot] = rs_send[app, jnp.where(is_high, 15, 16)]
            wait(rl_recv.at[app, pl.ds(0, 15)], r_rl.at[app])
            here, there = rl_recv[app, 0], rl_recv[app, 8]
            for n in range(1, 8):
                here = here + rl_recv[app, n]
                there = there + rl_recv[app, 8 + n]
            ag_send[app, 1] = here + keep_after * there

        @pl.when(is_double)
        def _():
            ag_recv[app, slot2] = ag_send[app, 1]
            for d in FAR_X:
                send(
                    ag_send.at[app, 1], ag_recv.at[app, slot2], s_ag2.at[app], r_ag.at[app],
                    (lax.rem(f + d, FX), y, z),
                )

        @pl.when(f == 15)
        def _():
            ag_send[app, 0] = ag_send[app, 1]

        if scalars is not None:
            wait(sc_recv.at[app, pl.ds(0, OWN - 1)], r_sc.at[app])
            part = sc_recv[app, 0]
            for n in range(1, OWN):
                part = part + sc_recv[app, n]
            ag_send[app, 0] = jnp.where(
                row4w == 3, jnp.concatenate([part, part], axis=1), ag_send[app, 0]
            )
        for d in FAR_X:
            send(
                ag_send.at[app, 0], ag_recv.at[app, f], s_ag.at[app], r_ag.at[app],
                (lax.rem(f + d, FX), y, z),
            )
        ag_recv[app, f] = ag_send[app, 0]

        @pl.when(is_double)
        def _():
            wait(ag_recv.at[app, pl.ds(0, 17)], r_ag.at[app])

        @pl.when(jnp.logical_not(is_double))
        def _():
            wait(ag_recv.at[app, pl.ds(0, 18)], r_ag.at[app])

    def gathered(app, target):
        for c in range(3):
            for h in range(15):
                target[c * 24 + h : c * 24 + h + 1, :] = ag_recv[app, h, c : c + 1, :]
            target[c * 24 + 15 : c * 24 + 16, :] = (
                ag_recv[app, 15, c : c + 1, :] + ag_recv[app, 16, c : c + 1, :]
            )
            target[c * 24 + 16 : c * 24 + 17, :] = has_before * (
                ag_recv[app, 17, c : c + 1, :] + ag_recv[app, 18, c : c + 1, :]
            )

    kdisp = vec_w[...]
    pad8 = jnp.zeros((8, 256), F32)
    loads = []
    for c in range(3):
        loads += [FORCE_SCALE * load_ref[c * 16 : c * 16 + 16, :], pad8]
    loads.append(pad8)
    exchange(0, jnp.concatenate(loads, axis=0) - kdisp, None)
    gathered(0, vec_r)
    vec_p[...] = jnp.zeros((80, 256), F32)
    vec_s[...] = jnp.zeros((80, 256), F32)
    vec_w[...] = jnp.zeros((80, 256), F32)

    def iteration(app, carry):
        alpha, gamma = carry
        sums, picked = elements(vec_r[...])
        for c in range(3):
            rc[c : c + 1, :] = vec_r[pl.ds(c * 24 + f, 1), :]
        rc[3:4, :] = jnp.zeros((1, 256), F32)
        chunk = rc[...]
        weighted = massx[pl.ds(f, 1), :] * chunk
        mine = jnp.sum(chunk * chunk, keepdims=True)
        energy = jnp.sum(picked * spread[...], keepdims=True) + jnp.sum(
            weighted * chunk, keepdims=True
        )
        scalars = jnp.where(lane == 0, mine, jnp.where(lane == 1, energy, 0.0))
        sc_send[app] = scalars
        sc_recv[app, own] = scalars
        exchange(app, sums, scalars)
        gathered(app, vec_w)
        both = ag_recv[app, 0]
        for n in range(1, FX):
            both = both + ag_recv[app, n]
        new = both[3:4, 0:1]
        delta = both[3:4, 1:2]
        beta = jnp.where(app == 1, 0.0, new / gamma)
        alpha = new / (delta - beta * new / alpha)
        weights = massx[...]
        weights = jnp.concatenate([weights] * 3 + [pad8], axis=0)
        p = vec_r[...] + beta * vec_p[...]
        s = vec_w[...] + weights * vec_r[...] + beta * vec_s[...]
        vec_p[...] = p
        vec_s[...] = s
        vec_r[...] = vec_r[...] - alpha * s
        for c in range(3):
            vec_x[c * 16 : c * 16 + 16, :] += alpha * p[c * 24 : c * 24 + 16, :]
        return alpha, new

    one = jnp.ones((1, 1), F32)
    lax.fori_loop(1, APPS, iteration, (one, one))

    for c in range(3):
        for h in range(16):
            at = slice(h * 256, h * 256 + 256)
            out_sol[c : c + 1, at] = vec_x[c * 16 + h : c * 16 + h + 1, :]
            out_res[c : c + 1, at] = vec_r[c * 24 + h : c * 24 + h + 1, :]

    pop_copy.wait()
    wait(sup_recv.at[pl.ds(0, OWN - 1)], s_sup)
    wait(edge_send, s_edge)
    wait(wall_recv.at[pl.ds(0, OWN - 1)], s_wall)
    wait(frc_recv.at[pl.ds(0, OWN - 1)], s_frc)
    for step, jobs in enumerate((jobs0, jobs1)):
        for n, (src, dst, device) in enumerate(jobs):
            wait(src, s_halo.at[step, n])
    for app in range(APPS):
        wait(rs_recv.at[app, pl.ds(0, 14)], s_rs.at[app])
        wait(rs_recv.at[app, pl.ds(0, 3)], s_rl.at[app])
        if app:
            wait(sc_recv.at[app, pl.ds(0, OWN - 1)], s_sc.at[app])
        wait(ag_recv.at[app, pl.ds(0, FX - 1)], s_ag.at[app])

        @pl.when(f == 15)
        def _():
            wait(rs_recv.at[app, 0], s_rs.at[app])

        @pl.when(jnp.logical_not(is_high | is_low))
        def _():
            wait(rs_recv.at[app, 0], s_rl.at[app])

        @pl.when(is_double)
        def _():
            wait(ag_recv.at[app, pl.ds(0, FX - 1)], s_ag2.at[app])


SCRATCH = dict(
    pop=(19, 4, 8, 256), relax=(4, 8, 256), vel=(3, 4096), count=((1, 16), I32),
    cell=((16, 32), I32), node=((16, 16, 32), I32), weight=(16, 16, 32), disp=(3, 4096),
    mass=(32, 128), connect=((8, 512), I32), modulus=(1, 512), basis=(24, 24),
    sup_send=(16, 8, 128), sup_recv=(16, 8, 128),
    wall_send=(16, 4, 128), wall_recv=(16, 4, 128),
    frc_send=(16, 4, 128), frc_recv=(16, 4, 128),
    edge_send=(4, 256), edge_recv=(4, 256),
    xs=(2, 2, 5, 8, 256), xr=(2, 2, 5, 8, 256),
    ys=(2, 2, 5, 4, 256), yr=(2, 2, 5, 4, 256),
    ds=(2, 4, 1, 256), dr=(2, 4, 1, 256),
    zs=(2, 4, 8, 128), zr=(2, 4, 8, 128), zxr=(2, 2, 8, 128),
    zys=(2, 2, 4, 128), zyr=(2, 2, 4, 128),
    rs_send=(APPS, 17, 4, 256), rs_recv=(APPS, 16, 4, 256), rl_recv=(APPS, 16, 4, 256),
    sc_send=(APPS, 1, 128), sc_recv=(APPS, 16, 1, 128),
    ag_send=(APPS, 2, 4, 256), ag_recv=(APPS, 19, 4, 256),
    post=(19, 4, 8, 256), field=(19, 4, 8, 256), rho_ref=(4, 8, 256), gain=(3, 4, 8, 256),
    cell_lo=((256, 512), BF16), cell_hi=(32, 512), live_ref=(8, 128), wallp=((192, 512), BF16),
    sup_lo=((16, 256, 512), BF16), sup_hi=(16, 16, 512),
    el_lo=((8, 256, 512), BF16), el_hi=(8, 24, 512),
    pick=(24, 512), spread=(24, 512),
    vec_r=(80, 256), vec_p=(80, 256), vec_s=(80, 256), vec_w=(80, 256), vec_x=(48, 256),
    massx=(24, 256), rc=(4, 256), load_ref=(48, 256), out_pop=(19, 4, 8, 256),
)


def scratch_shapes():
    shapes = []
    for shape in SCRATCH.values():
        kind = F32
        if isinstance(shape[0], tuple):
            shape, kind = shape
        shapes.append(pltpu.VMEM(shape, kind))
    dma = pltpu.SemaphoreType.DMA
    shapes += [dma((INPUTS,)), dma] + [dma] * 8 + [dma((2, 13))] * 2 + [dma((APPS,))] * 9
    return shapes


def deliver(pop_h, sol_h, res_h, pop_out, sol_out, res_out, pop, sol, res, s_in, s_out):
    jobs = [(pop_h.at[pl.ds(n, 4)], pop.at[pl.ds(n, 4)], pop_out.at[pl.ds(n, 4)]) for n in (0, 4, 8, 12)]
    jobs.append((pop_h.at[pl.ds(16, 3)], pop.at[pl.ds(16, 3)], pop_out.at[pl.ds(16, 3)]))
    jobs += [(sol_h, sol, sol_out), (res_h, res, res_out)]
    copies = []
    for n, (a, b, c) in enumerate(jobs):
        copies.append(
            (pltpu.make_async_copy(a, b, s_in.at[n]), pltpu.make_async_copy(b, c, s_out.at[n]))
        )
        copies[n][0].start()
    for came, goes in copies:
        came.wait()
        goes.start()
    for came, goes in copies:
        goes.wait()


def body(
    populations, relaxation, struct_velocity, iface_count, iface_cell, rbf_node, rbf_weight,
    disp_prev, node_mass, connect, modulus, strain_basis,
):
    vmem = pl.BlockSpec(memory_space=pltpu.VMEM)
    hbm = pl.BlockSpec(memory_space=pl.ANY)
    shapes = (
        jax.ShapeDtypeStruct(populations.shape, F32),
        jax.ShapeDtypeStruct(disp_prev.shape, F32),
        jax.ShapeDtypeStruct(disp_prev.shape, F32),
    )
    results = pl.pallas_call(
        kernel,
        out_shape=shapes,
        in_specs=[hbm] * INPUTS,
        out_specs=(hbm, vmem, vmem),
        scratch_shapes=scratch_shapes(),
        compiler_params=pltpu.CompilerParams(
            collective_id=0, has_side_effects=True, vmem_limit_bytes=62 * 1024 * 1024
        ),
        name="window",
    )(
        populations,
        relaxation,
        struct_velocity,
        iface_count.reshape(1, 16),
        iface_cell.reshape(16, 32),
        rbf_node.reshape(16, 16, 32),
        rbf_weight.reshape(16, 16, 32),
        disp_prev,
        node_mass.reshape(32, 128),
        connect.reshape(8, 512),
        modulus.reshape(1, 512),
        strain_basis,
    )
    return pl.pallas_call(
        deliver,
        out_shape=shapes,
        in_specs=[hbm] * 3,
        out_specs=(hbm, hbm, hbm),
        scratch_shapes=[pltpu.VMEM(s.shape, F32) for s in shapes]
        + [pltpu.SemaphoreType.DMA((7,))] * 2,
        compiler_params=pltpu.CompilerParams(vmem_limit_bytes=62 * 1024 * 1024),
        name="deliver",
    )(*results)


def solution(mesh):
    return jax.shard_map(
        body,
        mesh=mesh,
        in_specs=(
            P(None, "fx", "fy", "sz"),
            P("fx", "fy", "sz"),
            P(None, ("fy", "sz")),
            P("fx", "fy", "sz", None),
            P("fx", "fy", "sz", None, None),
            P("fx", "fy", "sz", None, None, None),
            P("fx", "fy", "sz", None, None, None),
            P(None, ("fy", "sz")),
            P(("fy", "sz")),
            P("fx", ("fy", "sz"), None, None),
            P("fx", ("fy", "sz"), None),
            P(),
        ),
        out_specs=(P(None, "fx", "fy", "sz"), P(None, ("fy", "sz")), P(None, ("fy", "sz"))),
        check_vma=False,
    )
```

```python
import jax
import jax.numpy as jnp
from jax import lax
from jax.experimental import pallas as pl
from jax.experimental.pallas import tpu as pltpu
from jax.sharding import PartitionSpec as P

F32 = jnp.float32
BF16 = jnp.bfloat16
I32 = jnp.int32
FX, FY, SZ = 16, 8, 2
OWN = 16
ITERS = 3
APPS = ITERS + 1
FORCE_SCALE = 20.0
VEL = [
    (0, 0, 0),
    (1, 0, 0),
    (-1, 0, 0),
    (0, 1, 0),
    (0, -1, 0),
    (0, 0, 1),
    (0, 0, -1),
    (1, 1, 0),
    (-1, -1, 0),
    (1, -1, 0),
    (-1, 1, 0),
    (1, 0, 1),
    (-1, 0, -1),
    (1, 0, -1),
    (-1, 0, 1),
    (0, 1, 1),
    (0, -1, -1),
    (0, 1, -1),
    (0, -1, 1),
]
X_POPS = [[i for i in range(19) if VEL[i][0] == s] for s in (1, -1)]
Y_POPS = [[i for i in range(19) if VEL[i][1] == s] for s in (1, -1)]
Z_POPS = [i for i in range(19) if VEL[i][2] != 0]
DIAGONAL = (7, 8, 9, 10)
MESH = pl.DeviceIdType.MESH
FAR_X = (8, 7, 9, 6, 10, 5, 11, 4, 12, 3, 13, 2, 14, 1, 15)
FAR_OWN = (
    (4, 1), (2, 1), (6, 1), (3, 1), (5, 1), (3, 0), (5, 0), (4, 0),
    (1, 1), (7, 1), (0, 1), (1, 0), (7, 0), (2, 0), (6, 0),
)
HIGH_RELAYS = (15, 7)
LOW_RELAYS = (14, 6)
INPUTS = 12
NEAR = 10


def split2(x):
    top = x.astype(BF16)
    rest = (x - top.astype(F32)).astype(BF16)
    return jnp.concatenate([top, rest], axis=0)


def dot_nt(a, b):
    return lax.dot_general(a, b, (((1,), (1,)), ((), ())), preferred_element_type=F32)


def dot_nn(a, b):
    return lax.dot_general(a, b, (((1,), (0,)), ((), ())), preferred_element_type=F32)


def exact_dot(a, b, dims=((1,), (0,))):
    return lax.dot_general(
        a, b, (dims, ((), ())), preferred_element_type=F32, precision=lax.Precision.HIGHEST
    )


def iota(shape, dim):
    return lax.broadcasted_iota(I32, shape, dim)


def group_sum(x):
    x = x + pltpu.roll(x, 64, x.ndim - 1)
    return x + pltpu.roll(x, 32, x.ndim - 1)


def send(src, dst, ssem, rsem, device):
    pltpu.make_async_remote_copy(
        src_ref=src,
        dst_ref=dst,
        send_sem=ssem,
        recv_sem=rsem,
        device_id=device,
        device_id_type=MESH,
    ).start()


def greet(f, y, z, own):
    sem = pltpu.get_barrier_semaphore()

    def tell(device):
        pl.semaphore_signal(sem, inc=1, device_id=device, device_id_type=MESH)

    for d in FAR_X:
        tell((lax.rem(f + d, FX), y, z))
    for dy, dz in FAR_OWN:
        tell((f, lax.rem(y + dy, FY), lax.rem(z + dz, SZ)))
    for dx in (1, FX - 1):
        tell((lax.rem(f + dx, FX), y, 1 - z))
        for dy in (1, FY - 1):
            tell((lax.rem(f + dx, FX), lax.rem(y + dy, FY), z))
    for relays, step in ((HIGH_RELAYS, 1), (LOW_RELAYS, OWN - 1)):
        there = lax.rem(own + step, OWN)

        for relay, first in zip(relays, (12, 4)):

            @pl.when(f == relay)
            def _():
                for n in range(8):
                    tell(((first + n) % FX, there // SZ, lax.rem(there, SZ)))

    return sem


def wait(ref, sem):
    pltpu.make_async_copy(ref, ref, sem).wait()


def kernel(
    pop_h, relax_h, vel_h, count_h, cell_h, node_h, weight_h, disp_h, mass_h, connect_h,
    modulus_h, basis_h,
    out_pop_h, out_sol, out_res,
    pop, relax, vel, count, cell, node, weight, disp, mass, connect, modulus, basis,
    sup_send, sup_recv, wall_send, wall_recv, frc_send, frc_recv, edge_send, edge_recv,
    xs, xr, ys, yr, ds, dr, zs, zr, zxr, zys, zyr,
    rs_send, rs_recv, rl_recv, sc_send, sc_recv, ag_send, ag_recv,
    post, field, rho_ref, gain, cell_lo, cell_hi, live_ref, wallp,
    sup_lo, sup_hi, el_lo, el_hi, pick, spread, vec_r, vec_p, vec_s, vec_w, vec_x,
    massx, rc, load_ref, out_pop, s_in, s_out,
    s_sup, r_sup, s_wall, r_wall, s_frc, r_frc, s_edge, r_edge, s_halo, r_halo,
    s_rs, r_rs, s_rl, r_rl, s_sc, r_sc, s_ag, r_ag, s_ag2,
):
    f = lax.axis_index("fx")
    y = lax.axis_index("fy")
    z = lax.axis_index("sz")
    own = y * SZ + z

    def at_owner(o, fx=None):
        return (f if fx is None else fx, o // SZ, lax.rem(o, SZ))

    def to_owners(src_of, dst, ssem, rsem):
        for dy, dz in FAR_OWN:
            there = (f, lax.rem(y + dy, FY), lax.rem(z + dz, SZ))
            send(src_of(there[1] * SZ + there[2]), dst, ssem, rsem, there)

    inputs = [
        (node_h, node), (weight_h, weight), (disp_h, disp), (mass_h, mass), (connect_h, connect),
        (basis_h, basis), (cell_h, cell), (count_h, count), (pop_h, pop), (relax_h, relax),
        (vel_h, vel), (modulus_h, modulus),
    ]
    copies = [pltpu.make_async_copy(a, b, s_in.at[n]) for n, (a, b) in enumerate(inputs)]
    for copy in copies[:2]:
        copy.start()
    barrier = greet(f, y, z, own)
    for copy in copies[2:]:
        copy.start()

    lane = iota((1, 128), 1)
    group = lane // 32
    expand = (iota((32, 128), 0) == lax.rem(iota((32, 128), 1), 32)).astype(F32)
    quarter = (lax.rem(iota((256, 128), 0), 16) // 4) == (iota((256, 128), 1) // 32)
    upper = iota((8, 128), 0) < 4
    copies[0].wait()
    copies[1].wait()
    spread_n = exact_dot(node[...].astype(F32).reshape(256, 32), expand)
    spread_w = exact_dot(weight[...].reshape(256, 32), expand)
    spread_n = jnp.where(quarter, spread_n, 0.0)
    spread_w = jnp.where(quarter, spread_w, 0.0)

    def packed(x, o):
        x = x[o * 16 : o * 16 + 8] + x[o * 16 + 8 : o * 16 + 16]
        return x + pltpu.roll(x, 4, 0)

    for o in range(OWN):
        sup_send[o] = jnp.where(upper, packed(spread_n, o), packed(spread_w, o))
    sup_recv[own] = sup_send[own]
    pl.semaphore_wait(barrier, 15 + 15 + 6 + 2)
    to_owners(lambda o: sup_send.at[o], sup_recv.at[own], s_sup, r_sup.at[own])

    copies[2].wait()
    copies[3].wait()
    for c in range(3):
        edge_send[c : c + 1, :] = disp[c : c + 1, 3840:4096]
    massx[...] = jnp.zeros((24, 256), F32)
    for h in range(16):
        massx[h : h + 1, 0:128] = mass[2 * h : 2 * h + 1, :]
        massx[h : h + 1, 128:256] = mass[2 * h + 1 : 2 * h + 2, :]
    edge_send[3:4, :] = massx[15:16, :]
    after, before = lax.rem(own + 1, OWN), lax.rem(own + OWN - 1, OWN)
    send(edge_send, edge_recv, s_edge, r_edge, at_owner(after))

    copies[4].wait()
    copies[5].wait()
    for j in range(8):
        n = connect[j : j + 1, :]
        lo = lax.rem(n, 256)
        hi = jnp.where(n < 256, 16, n // 256 - 1)
        el_lo[j] = jnp.where(iota((256, 512), 0) == lo, 1.0, 0.0).astype(BF16)
        el_hi[j] = jnp.where(iota((24, 512), 0) == hi, 1.0, 0.0)
    base = basis[...]
    gram = exact_dot(base, base, ((0,), (0,)))
    thrice = lax.rem(iota((24, 96), 1), 32) == iota((24, 96), 0)
    gram = exact_dot(gram, thrice.astype(F32))
    gram_top = gram.astype(BF16).astype(F32)
    gram = jnp.where(iota((24, 96), 1) < 64, gram_top, gram - gram_top).astype(BF16)

    copies[6].wait()
    copies[7].wait()
    cells = cell[...]
    cell_hi16 = exact_dot((cells // 256).astype(F32), expand)
    cell_lo16 = exact_dot(lax.rem(cells, 256).astype(F32), expand)
    diag = iota((16, 16), 0) == iota((16, 16), 1)
    counts = jnp.sum(jnp.where(diag, count[...].astype(F32), 0.0), axis=1, keepdims=True)
    live16 = (lax.rem(iota((16, 128), 1), 32).astype(F32) < counts).astype(F32)
    mine = lax.rem(iota((16, 128), 0), 4) == (iota((16, 128), 1) // 32)
    fold = ((iota((8, 16), 1) // 4) == iota((8, 16), 0)).astype(F32)

    def rows_of(x):
        return exact_dot(fold, jnp.where(mine, x, 0.0))

    hi_rows, lo_rows = rows_of(cell_hi16).astype(I32), rows_of(cell_lo16).astype(I32)
    live_ref[...] = rows_of(live16)
    for g in range(4):
        at = slice(g * 128, g * 128 + 128)
        cell_lo[:, at] = jnp.where(iota((256, 128), 0) == lo_rows[g : g + 1], 1.0, 0.0).astype(BF16)
        cell_hi[:, at] = jnp.where(iota((32, 128), 0) == hi_rows[g : g + 1], 1.0, 0.0)

    def moments(fs):
        rho = fs[0]
        for i in range(1, 19):
            rho = rho + fs[i]
        mom = []
        for a in range(3):
            total = None
            for i in range(1, 19, 2):
                s = VEL[i][a]
                if s:
                    pair = fs[i] - fs[i + 1] if s > 0 else fs[i + 1] - fs[i]
                    total = pair if total is None else total + pair
            mom.append(total)
        return rho, mom

    def along(c, v):
        total = None
        for a in range(3):
            if c[a] == 1:
                total = v[a] if total is None else total + v[a]
        for a in range(3):
            if c[a] == -1:
                total = -v[a] if total is None else total - v[a]
        return total

    def collide(source):
        for k in range(4):
            fs = [source[i, k] for i in range(19)]
            om = relax[k]
            rho, mom = moments(fs)
            inv = 1.0 / rho
            u = [m * inv for m in mom]
            sq = 1.5 * (u[0] * u[0] + u[1] * u[1] + u[2] * u[2])
            rho_ref[k] = rho
            keep = 1.0 - om
            scaled = om * rho
            post[0, k] = keep * fs[0] + (1.0 / 3.0) * scaled * (1.0 - sq)
            for i in range(1, 19, 2):
                t = (1.0 / 18.0) if i < 7 else (1.0 / 36.0)
                a = along(VEL[i], u)
                ts = t * scaled
                even = ts * (1.0 + 4.5 * a * a - sq)
                odd = ts * (3.0 * a)
                post[i, k] = keep * fs[i] + (even + odd)
                post[i + 1, k] = keep * fs[i + 1] + (even - odd)

    def turn(i, v):
        cy, cz = VEL[i][1], VEL[i][2]
        if cy:
            v = pltpu.roll(v, cy % 8, 0)
        if cz:
            v = pltpu.roll(v, cz % 256, 1)
        return v

    lane8 = iota((8, 128), 1)
    row8 = iota((8, 128), 0)

    def stream(step, target, wall_gain):
        for k in range(4):
            for c in range(3):
                gain[c, k] = wall_gain[c][k] * rho_ref[k] * (1.0 / 6.0)
        xp, xm = lax.rem(f + 1, FX), lax.rem(f + FX - 1, FX)
        yp, ym = lax.rem(y + 1, FY), lax.rem(y + FY - 1, FY)
        zo = 1 - z
        jobs = {
            "x0": (xs.at[step, 0], xr.at[step, 0], (xp, y, z)),
            "x1": (xs.at[step, 1], xr.at[step, 1], (xm, y, z)),
            "y0": (ys.at[step, 0], yr.at[step, 0], (f, yp, z)),
            "y1": (ys.at[step, 1], yr.at[step, 1], (f, ym, z)),
            "d0": (ds.at[step, 0], dr.at[step, 0], (xp, yp, z)),
            "d1": (ds.at[step, 1], dr.at[step, 1], (xm, ym, z)),
            "d2": (ds.at[step, 2], dr.at[step, 2], (xp, ym, z)),
            "d3": (ds.at[step, 3], dr.at[step, 3], (xm, yp, z)),
            "zx0": (zs.at[step, 0], zxr.at[step, 0], (xp, y, zo)),
            "zx1": (zs.at[step, 3], zxr.at[step, 1], (xm, y, zo)),
            "zy0": (zys.at[step, 0], zyr.at[step, 0], (f, yp, zo)),
            "zy1": (zys.at[step, 1], zyr.at[step, 1], (f, ym, zo)),
            "z": (zs.at[step], zr.at[step], (f, y, zo)),
        }
        index = {name: n for n, name in enumerate(jobs)}

        def go(*names):
            for name in names:
                src, dst, device = jobs[name]
                n = index[name]
                send(src, dst, s_halo.at[step, n], r_halo.at[step, n], device)

        def came(*names):
            for name in names:
                wait(jobs[name][1], r_halo.at[step, index[name]])

        for x in (0, 3, 1, 2):
            zpack = jnp.zeros((8, 128), F32)
            for i in range(19):
                cx, cy, cz = VEL[i]
                k = (x - cx) % 4
                v = post[i, k]
                if i:
                    push = along(VEL[i], [gain[c, k] for c in range(3)])
                    v = v + (2.0 * push if i < 7 else push)
                v = turn(i, v)
                if k != x - cx:
                    side = 0 if cx > 0 else 1
                    xs[step, side, X_POPS[side].index(i)] = v
                    if cy:
                        r = 0 if cy > 0 else 7
                        ds[step, DIAGONAL.index(i)] = v[r : r + 1, :]
                else:
                    target[i, x] = v
                if cy:
                    side = 0 if cy > 0 else 1
                    r = 0 if cy > 0 else 7
                    ys[step, side, Y_POPS[side].index(i), x : x + 1, :] = v[r : r + 1, :]
                if cz:
                    col = v[:, 0:1] if cz > 0 else v[:, 255:256]
                    zpack = jnp.where(lane8 == Z_POPS.index(i), col, zpack)
            zs[step, x] = zpack
            zys[step, 0, x : x + 1, :] = zpack[0:1, :]
            zys[step, 1, x : x + 1, :] = zpack[7:8, :]
            if x == 0:
                go("zx0", "d0", "d2", "x0")
            if x == 3:
                go("zx1", "d1", "d3", "x1")
        go("zy0", "zy1", "z", "y0", "y1")
        came("x0", "x1")
        for side in range(2):
            for n, i in enumerate(X_POPS[side]):
                target[i, 0 if side == 0 else 3] = xr[step, side, n]
        came("y0", "y1")
        for side in range(2):
            r = 0 if side == 0 else 7
            for n, i in enumerate(Y_POPS[side]):
                cx = VEL[i][0]
                for x in range(4):
                    if 0 <= x - cx <= 3:
                        target[i, x, r : r + 1, :] = yr[step, side, n, x : x + 1, :]
        came("d0", "d1", "d2", "d3")
        for n, i in enumerate(DIAGONAL):
            cx, cy, _ = VEL[i]
            r = 0 if cy > 0 else 7
            target[i, 0 if cx > 0 else 3, r : r + 1, :] = dr[step, n]
        came("z", "zx0", "zx1", "zy0", "zy1")
        z11, z12, z13, z14, z15, z16, z17, z18 = [Z_POPS.index(i) for i in range(11, 19)]
        for x in range(4):
            zin = zr[step, x]
            if x == 0:
                zin = jnp.where((lane8 == z11) | (lane8 == z13), zxr[step, 0], zin)
            if x == 3:
                zin = jnp.where((lane8 == z12) | (lane8 == z14), zxr[step, 1], zin)
            low = (row8 == 0) & ((lane8 == z15) | (lane8 == z17))
            high = (row8 == 7) & ((lane8 == z16) | (lane8 == z18))
            zin = jnp.where(low, zyr[step, 0, x : x + 1, :], zin)
            zin = jnp.where(high, zyr[step, 1, x : x + 1, :], zin)
            for n, i in enumerate(Z_POPS):
                col = zin[:, n : n + 1]
                if VEL[i][2] > 0:
                    target[i, x, :, 0:128] = jnp.where(lane8 == 0, col, target[i, x, :, 0:128])
                else:
                    target[i, x, :, 128:256] = jnp.where(
                        lane8 == 127, col, target[i, x, :, 128:256]
                    )
        return list(jobs.values())

    copies[8].wait()
    copies[9].wait()
    collide(pop)

    copies[10].wait()
    copies[11].wait()
    for c in range(3):
        for h in range(16):
            load_ref[c * 16 + h : c * 16 + h + 1, :] = vel[c : c + 1, h * 256 : h * 256 + 256]
    table = split2(load_ref[...])
    steps = [(0, 0)] + list(reversed(FAR_OWN))
    batches = [list(enumerate(steps))[:NEAR], list(enumerate(steps))[NEAR:]]

    def partner(step):
        there = (f, lax.rem(y + step[0], FY), lax.rem(z + step[1], SZ))
        return there, there[1] * SZ + there[2]

    for batch in batches:
        for n, step in batch:
            if n:
                o = partner(step)[1]
                wait(sup_recv.at[o], r_sup.at[o])
        for n, step in batch:
            there, o = partner(step)
            tile = sup_recv[o]
            for r in range(4):
                node_row = tile[r : r + 1].astype(I32)
                sup_lo[n, :, r * 128 : r * 128 + 128] = jnp.where(
                    iota((256, 128), 0) == lax.rem(node_row, 256), 1.0, 0.0
                ).astype(BF16)
                sup_hi[n, :, r * 128 : r * 128 + 128] = jnp.where(
                    iota((16, 128), 0) == node_row // 256, tile[r + 4 : r + 5], 0.0
                )
        for n, step in batch:
            there, o = partner(step)
            out = dot_nn(table, sup_lo[n])
            out = out[0:48] + out[48:96]
            hot = sup_hi[n]
            for c in range(3):
                m = out[c * 16 : c * 16 + 16] * hot
                m = m[:, 0:128] + m[:, 128:256] + m[:, 256:384] + m[:, 384:512]
                wall_send[n, c : c + 1, :] = jnp.sum(m, axis=0, keepdims=True)
            wall_send[n, 3:4, :] = jnp.zeros((1, 128), F32)
        for n, step in reversed(batch):
            there, o = partner(step)
            if n:
                send(wall_send.at[n], wall_recv.at[own], s_wall, r_wall, there)
            else:
                wall_recv[own] = wall_send[0]

    def elements(values):
        both = split2(values)

        for j in range(8):
            out = dot_nn(both, el_lo[j])
            out = out[0:80] + out[80:160]
            hot = el_hi[j]
            for c in range(3):
                pick[c * 8 + j : c * 8 + j + 1, :] = jnp.sum(
                    out[c * 24 : c * 24 + 24] * hot, axis=0, keepdims=True
                )
        picked = pick[...]
        wide = jnp.concatenate([picked, jnp.zeros((8, 512), F32)], axis=0)
        top = wide.astype(BF16)
        rest = (wide - top.astype(F32)).astype(BF16)
        spread[...] = dot_nn(gram, jnp.concatenate([top, rest, top], axis=0)) * modulus[...]
        total = None
        for j in range(8):
            hot = el_hi[j]
            parts = [hot * spread[c * 8 + j : c * 8 + j + 1, :] for c in range(3)]
            parts.append(jnp.zeros((8, 512), F32))
            part = dot_nt(split2(jnp.concatenate(parts, axis=0)), el_lo[j])
            total = part if total is None else total + part
        return total[0:80] + total[80:160]

    wait(edge_recv, r_edge)
    vec_r[...] = jnp.zeros((80, 256), F32)
    has_before = (own > 0).astype(F32)
    has_after = (own < OWN - 1).astype(F32)
    for c in range(3):
        for h in range(16):
            row = disp[c : c + 1, h * 256 : h * 256 + 256]
            vec_r[c * 24 + h : c * 24 + h + 1, :] = row
            vec_x[c * 16 + h : c * 16 + h + 1, :] = row
        vec_r[c * 24 + 16 : c * 24 + 17, :] = edge_recv[c : c + 1, :] * has_before
    vec_w[...] = elements(vec_r[...])
    massx[16:17, :] = edge_recv[3:4, :]

    wait(wall_recv.at[pl.ds(0, OWN - 1)], r_wall)
    wall = [None] * 4
    for g in range(4):
        total = jnp.zeros((4, 128), F32)
        for q in range(4):
            total = jnp.where(group == q, group_sum(wall_recv[g * 4 + q]), total)
        wall[g] = total * live_ref[g : g + 1, :]
    for g in range(4):
        hot = cell_hi[:, g * 128 : g * 128 + 128]
        parts = [hot * wall[g][c : c + 1, :] for c in range(3)]
        wallp[:, g * 128 : g * 128 + 128] = split2(jnp.concatenate(parts, axis=0))
    summed = dot_nt(wallp[...], cell_lo[...])
    summed = summed[0:96] + summed[96:192]
    wall_gain = [
        [summed[c * 32 + k * 8 : c * 32 + k * 8 + 8, :] for k in range(4)] for c in range(3)
    ]

    jobs0 = stream(0, field, wall_gain)
    collide(field)
    jobs1 = stream(1, out_pop, wall_gain)

    pop_copy = pltpu.make_async_copy(out_pop, out_pop_h, s_out)
    pop_copy.start()

    rows = [[], [], [], []]
    for k in range(4):
        rho, mom = moments([out_pop[i, k] for i in range(19)])
        for q, part in enumerate([rho] + mom):
            rows[q].append(part)
    values = jnp.concatenate([r for q in range(4) for r in rows[q]], axis=0)
    at_slots = dot_nn(split2(values), cell_lo[...])
    at_slots = at_slots[0:128] + at_slots[128:256]
    hot = cell_hi[...]
    slot = [
        jnp.sum(at_slots[q * 32 : q * 32 + 32] * hot, axis=0, keepdims=True) for q in range(4)
    ]
    row4 = iota((4, 128), 0)
    for g in range(4):
        at = slice(g * 128, g * 128 + 128)
        mom = jnp.zeros((4, 128), F32)
        for c in range(3):
            mom = jnp.where(row4 == c, slot[c + 1][:, at], mom)
        force = (mom - slot[0][:, at] * wall[g]) * live_ref[g : g + 1, :]
        for q in range(4):
            frc_send[g * 4 + q] = group_sum(jnp.where(group == q, force, 0.0))
    frc_recv[own] = frc_send[own]
    to_owners(lambda o: frc_send.at[o], frc_recv.at[own], s_frc, r_frc.at[own])

    total = None
    for batch in batches:
        for n, step in batch:
            if n:
                o = partner(step)[1]
                wait(frc_recv.at[o], r_frc.at[o])
        for n, step in batch:
            force = frc_recv[partner(step)[1]]
            parts = []
            for c in range(3):
                line = force[c : c + 1, :]
                line = jnp.concatenate([line] * 4, axis=1)
                parts.append(sup_hi[n] * line)
            got = dot_nt(split2(jnp.concatenate(parts, axis=0)), sup_lo[n])
            total = got if total is None else total + got
    load_ref[...] = total[0:48] + total[48:96]

    row4w = iota((4, 256), 0)
    place = lax.rem(f + 4, FX)
    spot = lax.rem(place, 8)
    high = jnp.where(place < 8, HIGH_RELAYS[0], HIGH_RELAYS[1])
    low = high - 1
    is_high = (f == HIGH_RELAYS[0]) | (f == HIGH_RELAYS[1])
    is_low = (f == LOW_RELAYS[0]) | (f == LOW_RELAYS[1])
    is_double = (f == HIGH_RELAYS[1]) | is_low
    slot2 = jnp.where(f == HIGH_RELAYS[1], 16, jnp.where(f == LOW_RELAYS[0], 17, 18))
    keep_after = jnp.where(is_high, has_after, 1.0)

    def exchange(app, sums, scalars):
        for c in range(3):
            for h in range(17):
                rs_send[app, h, c : c + 1, :] = sums[c * 24 + h : c * 24 + h + 1, :]
        top, ghost = rs_send.at[app, 15], rs_send.at[app, 16]
        send(ghost, rl_recv.at[app, 8 + spot], s_rl.at[app], r_rl.at[app], at_owner(before, high))
        send(top, rl_recv.at[app, 8 + spot], s_rl.at[app], r_rl.at[app], at_owner(after, low))
        for d in FAR_X:
            j = lax.rem(f + d, FX)

            @pl.when(j < 15)
            def _():
                send(rs_send.at[app, j], rs_recv.at[app, f], s_rs.at[app], r_rs.at[app], (j, y, z))

        @pl.when(f != high)
        def _():
            send(top, rl_recv.at[app, spot], s_rl.at[app], r_rl.at[app], (high, y, z))

        @pl.when(f != low)
        def _():
            send(ghost, rl_recv.at[app, spot], s_rl.at[app], r_rl.at[app], (low, y, z))

        if scalars is not None:
            scalars()
            to_owners(lambda o: sc_send.at[app], sc_recv.at[app, own], s_sc.at[app], r_sc.at[app])
        rs_recv[app, f] = rs_send[app, f]

        @pl.when(f < 15)
        def _():
            wait(rs_recv.at[app, pl.ds(0, FX - 1)], r_rs.at[app])
            total = rs_recv[app, 0]
            for n in range(1, FX):
                total = total + rs_recv[app, n]
            ag_send[app, 0] = total

        @pl.when(is_high | is_low)
        def _():
            rl_recv[app, spot] = rs_send[app, jnp.where(is_high, 15, 16)]
            wait(rl_recv.at[app, pl.ds(0, 15)], r_rl.at[app])
            here, there = rl_recv[app, 0], rl_recv[app, 8]
            for n in range(1, 8):
                here = here + rl_recv[app, n]
                there = there + rl_recv[app, 8 + n]
            ag_send[app, 1] = here + keep_after * there

        @pl.when(is_double)
        def _():
            ag_recv[app, slot2] = ag_send[app, 1]
            for d in FAR_X:
                send(
                    ag_send.at[app, 1], ag_recv.at[app, slot2], s_ag2.at[app], r_ag.at[app],
                    (lax.rem(f + d, FX), y, z),
                )

        @pl.when(f == 15)
        def _():
            ag_send[app, 0] = ag_send[app, 1]

        if scalars is not None:
            wait(sc_recv.at[app, pl.ds(0, OWN - 1)], r_sc.at[app])
            part = sc_recv[app, 0]
            for n in range(1, OWN):
                part = part + sc_recv[app, n]
            ag_send[app, 0] = jnp.where(
                row4w == 3, part, ag_send[app, 0]
            )
        for d in FAR_X:
            send(
                ag_send.at[app, 0], ag_recv.at[app, f], s_ag.at[app], r_ag.at[app],
                (lax.rem(f + d, FX), y, z),
            )
        ag_recv[app, f] = ag_send[app, 0]

        @pl.when(is_double)
        def _():
            wait(ag_recv.at[app, pl.ds(0, 17)], r_ag.at[app])

        @pl.when(jnp.logical_not(is_double))
        def _():
            wait(ag_recv.at[app, pl.ds(0, 18)], r_ag.at[app])

    def gathered(app, target):
        for c in range(3):
            for h in range(15):
                target[c * 24 + h : c * 24 + h + 1, :] = ag_recv[app, h, c : c + 1, :]
            target[c * 24 + 15 : c * 24 + 16, :] = (
                ag_recv[app, 15, c : c + 1, :] + ag_recv[app, 16, c : c + 1, :]
            )
            target[c * 24 + 16 : c * 24 + 17, :] = has_before * (
                ag_recv[app, 17, c : c + 1, :] + ag_recv[app, 18, c : c + 1, :]
            )

    kdisp = vec_w[...]
    pad8 = jnp.zeros((8, 256), F32)
    loads = []
    for c in range(3):
        loads += [FORCE_SCALE * load_ref[c * 16 : c * 16 + 16, :], pad8]
    loads.append(pad8)
    exchange(0, jnp.concatenate(loads, axis=0) - kdisp, None)
    gathered(0, vec_r)
    vec_p[...] = jnp.zeros((80, 256), F32)
    vec_s[...] = jnp.zeros((80, 256), F32)
    vec_w[...] = jnp.zeros((80, 256), F32)

    def iteration(app, carry):
        alpha, gamma = carry
        for c in range(3):
            rc[c : c + 1, :] = vec_r[pl.ds(c * 24 + f, 1), :]
        rc[3:4, :] = jnp.zeros((1, 256), F32)
        chunk = rc[...]
        mine = jnp.sum(chunk * chunk, keepdims=True)
        held = jnp.sum(massx[pl.ds(f, 1), :] * chunk * chunk, keepdims=True)

        def tell():
            energy = held + jnp.sum(pick[...] * spread[...], keepdims=True)
            scalars = jnp.where(iota((1, 256), 1) < 128, mine, energy)
            sc_send[app] = scalars
            sc_recv[app, own] = scalars

        exchange(app, elements(vec_r[...]), tell)
        gathered(app, vec_w)
        both = ag_recv[app, 0]
        for n in range(1, FX):
            both = both + ag_recv[app, n]
        new = both[3:4, 0:128]
        delta = both[3:4, 128:256]
        beta = jnp.where(app == 1, 0.0, new / gamma)
        alpha = new / (delta - beta * new / alpha)
        weights = massx[...]
        weights = jnp.concatenate([weights] * 3 + [pad8], axis=0)
        beta2 = jnp.concatenate([beta, beta], axis=1)
        alpha2 = jnp.concatenate([alpha, alpha], axis=1)
        p = vec_r[...] + beta2 * vec_p[...]
        s = vec_w[...] + weights * vec_r[...] + beta2 * vec_s[...]
        vec_p[...] = p
        vec_s[...] = s
        vec_r[...] = vec_r[...] - alpha2 * s
        for c in range(3):
            vec_x[c * 16 : c * 16 + 16, :] += alpha2 * p[c * 24 : c * 24 + 16, :]
        return alpha, new

    one = jnp.ones((1, 128), F32)
    lax.fori_loop(1, APPS, iteration, (one, one))

    for c in range(3):
        for h in range(16):
            at = slice(h * 256, h * 256 + 256)
            out_sol[c : c + 1, at] = vec_x[c * 16 + h : c * 16 + h + 1, :]
            out_res[c : c + 1, at] = vec_r[c * 24 + h : c * 24 + h + 1, :]

    pop_copy.wait()
    wait(sup_recv.at[pl.ds(0, OWN - 1)], s_sup)
    wait(edge_send, s_edge)
    wait(wall_recv.at[pl.ds(0, OWN - 1)], s_wall)
    wait(frc_recv.at[pl.ds(0, OWN - 1)], s_frc)
    for step, jobs in enumerate((jobs0, jobs1)):
        for n, (src, dst, device) in enumerate(jobs):
            wait(src, s_halo.at[step, n])
    for app in range(APPS):
        wait(rs_recv.at[app, pl.ds(0, 14)], s_rs.at[app])
        wait(rs_recv.at[app, pl.ds(0, 3)], s_rl.at[app])
        if app:
            wait(sc_recv.at[app, pl.ds(0, OWN - 1)], s_sc.at[app])
        wait(ag_recv.at[app, pl.ds(0, FX - 1)], s_ag.at[app])

        @pl.when(f == 15)
        def _():
            wait(rs_recv.at[app, 0], s_rs.at[app])

        @pl.when(jnp.logical_not(is_high | is_low))
        def _():
            wait(rs_recv.at[app, 0], s_rl.at[app])

        @pl.when(is_double)
        def _():
            wait(ag_recv.at[app, pl.ds(0, FX - 1)], s_ag2.at[app])


SCRATCH = dict(
    pop=(19, 4, 8, 256), relax=(4, 8, 256), vel=(3, 4096), count=((1, 16), I32),
    cell=((16, 32), I32), node=((16, 16, 32), I32), weight=(16, 16, 32), disp=(3, 4096),
    mass=(32, 128), connect=((8, 512), I32), modulus=(1, 512), basis=(24, 24),
    sup_send=(16, 8, 128), sup_recv=(16, 8, 128),
    wall_send=(16, 4, 128), wall_recv=(16, 4, 128),
    frc_send=(16, 4, 128), frc_recv=(16, 4, 128),
    edge_send=(4, 256), edge_recv=(4, 256),
    xs=(2, 2, 5, 8, 256), xr=(2, 2, 5, 8, 256),
    ys=(2, 2, 5, 4, 256), yr=(2, 2, 5, 4, 256),
    ds=(2, 4, 1, 256), dr=(2, 4, 1, 256),
    zs=(2, 4, 8, 128), zr=(2, 4, 8, 128), zxr=(2, 2, 8, 128),
    zys=(2, 2, 4, 128), zyr=(2, 2, 4, 128),
    rs_send=(APPS, 17, 4, 256), rs_recv=(APPS, 16, 4, 256), rl_recv=(APPS, 16, 4, 256),
    sc_send=(APPS, 1, 256), sc_recv=(APPS, 16, 1, 256),
    ag_send=(APPS, 2, 4, 256), ag_recv=(APPS, 19, 4, 256),
    post=(19, 4, 8, 256), field=(19, 4, 8, 256), rho_ref=(4, 8, 256), gain=(3, 4, 8, 256),
    cell_lo=((256, 512), BF16), cell_hi=(32, 512), live_ref=(8, 128), wallp=((192, 512), BF16),
    sup_lo=((16, 256, 512), BF16), sup_hi=(16, 16, 512),
    el_lo=((8, 256, 512), BF16), el_hi=(8, 24, 512),
    pick=(24, 512), spread=(24, 512),
    vec_r=(80, 256), vec_p=(80, 256), vec_s=(80, 256), vec_w=(80, 256), vec_x=(48, 256),
    massx=(24, 256), rc=(4, 256), load_ref=(48, 256), out_pop=(19, 4, 8, 256),
)


def scratch_shapes():
    shapes = []
    for shape in SCRATCH.values():
        kind = F32
        if isinstance(shape[0], tuple):
            shape, kind = shape
        shapes.append(pltpu.VMEM(shape, kind))
    dma = pltpu.SemaphoreType.DMA
    shapes += [dma((INPUTS,)), dma]
    shapes += [dma, dma((OWN,)), dma, dma, dma, dma((OWN,)), dma, dma]
    shapes += [dma((2, 13))] * 2 + [dma((APPS,))] * 9
    return shapes


def deliver(pop_h, sol_h, res_h, pop_out, sol_out, res_out, pop, sol, res, s_in, s_out):
    jobs = [(pop_h.at[pl.ds(n, 4)], pop.at[pl.ds(n, 4)], pop_out.at[pl.ds(n, 4)]) for n in (0, 4, 8, 12)]
    jobs.append((pop_h.at[pl.ds(16, 3)], pop.at[pl.ds(16, 3)], pop_out.at[pl.ds(16, 3)]))
    jobs += [(sol_h, sol, sol_out), (res_h, res, res_out)]
    copies = []
    for n, (a, b, c) in enumerate(jobs):
        copies.append(
            (pltpu.make_async_copy(a, b, s_in.at[n]), pltpu.make_async_copy(b, c, s_out.at[n]))
        )
        copies[n][0].start()
    for came, goes in copies:
        came.wait()
        goes.start()
    for came, goes in copies:
        goes.wait()


def body(
    populations, relaxation, struct_velocity, iface_count, iface_cell, rbf_node, rbf_weight,
    disp_prev, node_mass, connect, modulus, strain_basis,
):
    vmem = pl.BlockSpec(memory_space=pltpu.VMEM)
    hbm = pl.BlockSpec(memory_space=pl.ANY)
    shapes = (
        jax.ShapeDtypeStruct(populations.shape, F32),
        jax.ShapeDtypeStruct(disp_prev.shape, F32),
        jax.ShapeDtypeStruct(disp_prev.shape, F32),
    )
    results = pl.pallas_call(
        kernel,
        out_shape=shapes,
        in_specs=[hbm] * INPUTS,
        out_specs=(hbm, vmem, vmem),
        scratch_shapes=scratch_shapes(),
        compiler_params=pltpu.CompilerParams(
            collective_id=0, has_side_effects=True, vmem_limit_bytes=62 * 1024 * 1024
        ),
        name="window",
    )(
        populations,
        relaxation,
        struct_velocity,
        iface_count.reshape(1, 16),
        iface_cell.reshape(16, 32),
        rbf_node.reshape(16, 16, 32),
        rbf_weight.reshape(16, 16, 32),
        disp_prev,
        node_mass.reshape(32, 128),
        connect.reshape(8, 512),
        modulus.reshape(1, 512),
        strain_basis,
    )
    return pl.pallas_call(
        deliver,
        out_shape=shapes,
        in_specs=[hbm] * 3,
        out_specs=(hbm, hbm, hbm),
        scratch_shapes=[pltpu.VMEM(s.shape, F32) for s in shapes]
        + [pltpu.SemaphoreType.DMA((7,))] * 2,
        compiler_params=pltpu.CompilerParams(vmem_limit_bytes=62 * 1024 * 1024),
        name="deliver",
    )(*results)


def solution(mesh):
    return jax.shard_map(
        body,
        mesh=mesh,
        in_specs=(
            P(None, "fx", "fy", "sz"),
            P("fx", "fy", "sz"),
            P(None, ("fy", "sz")),
            P("fx", "fy", "sz", None),
            P("fx", "fy", "sz", None, None),
            P("fx", "fy", "sz", None, None, None),
            P("fx", "fy", "sz", None, None, None),
            P(None, ("fy", "sz")),
            P(("fy", "sz")),
            P("fx", ("fy", "sz"), None, None),
            P("fx", ("fy", "sz"), None),
            P(),
        ),
        out_specs=(P(None, "fx", "fy", "sz"), P(None, ("fy", "sz")), P(None, ("fy", "sz"))),
        check_vma=False,
    )
```

```python
import jax
import jax.numpy as jnp
from jax import lax
from jax.experimental import pallas as pl
from jax.experimental.pallas import tpu as pltpu
from jax.sharding import PartitionSpec as P

F32 = jnp.float32
BF16 = jnp.bfloat16
I32 = jnp.int32
FX, FY, SZ = 16, 8, 2
OWN = 16
ITERS = 3
APPS = ITERS + 1
FORCE_SCALE = 20.0
VEL = [
    (0, 0, 0),
    (1, 0, 0),
    (-1, 0, 0),
    (0, 1, 0),
    (0, -1, 0),
    (0, 0, 1),
    (0, 0, -1),
    (1, 1, 0),
    (-1, -1, 0),
    (1, -1, 0),
    (-1, 1, 0),
    (1, 0, 1),
    (-1, 0, -1),
    (1, 0, -1),
    (-1, 0, 1),
    (0, 1, 1),
    (0, -1, -1),
    (0, 1, -1),
    (0, -1, 1),
]
X_POPS = [[i for i in range(19) if VEL[i][0] == s] for s in (1, -1)]
Y_POPS = [[i for i in range(19) if VEL[i][1] == s] for s in (1, -1)]
Z_POPS = [i for i in range(19) if VEL[i][2] != 0]
DIAGONAL = (7, 8, 9, 10)
MESH = pl.DeviceIdType.MESH
FAR_X = (8, 7, 9, 6, 10, 5, 11, 4, 12, 3, 13, 2, 14, 1, 15)
FAR_OWN = (
    (4, 1), (2, 1), (6, 1), (3, 1), (5, 1), (3, 0), (5, 0), (4, 0),
    (1, 1), (7, 1), (0, 1), (1, 0), (7, 0), (2, 0), (6, 0),
)
HIGH_RELAYS = (15, 7)
LOW_RELAYS = (14, 6)
INPUTS = 12
NEAR = 10


def split2(x):
    top = x.astype(BF16)
    rest = (x - top.astype(F32)).astype(BF16)
    return jnp.concatenate([top, rest], axis=0)


def dot_nt(a, b):
    return lax.dot_general(a, b, (((1,), (1,)), ((), ())), preferred_element_type=F32)


def dot_nn(a, b):
    return lax.dot_general(a, b, (((1,), (0,)), ((), ())), preferred_element_type=F32)


def exact_dot(a, b, dims=((1,), (0,))):
    return lax.dot_general(
        a, b, (dims, ((), ())), preferred_element_type=F32, precision=lax.Precision.HIGHEST
    )


def iota(shape, dim):
    return lax.broadcasted_iota(I32, shape, dim)


def group_sum(x):
    x = x + pltpu.roll(x, 64, x.ndim - 1)
    return x + pltpu.roll(x, 32, x.ndim - 1)


def send(src, dst, ssem, rsem, device):
    pltpu.make_async_remote_copy(
        src_ref=src,
        dst_ref=dst,
        send_sem=ssem,
        recv_sem=rsem,
        device_id=device,
        device_id_type=MESH,
    ).start()


def greet(f, y, z, own):
    sem = pltpu.get_barrier_semaphore()

    def tell(device):
        pl.semaphore_signal(sem, inc=1, device_id=device, device_id_type=MESH)

    for d in FAR_X:
        tell((lax.rem(f + d, FX), y, z))
    for dy, dz in FAR_OWN:
        tell((f, lax.rem(y + dy, FY), lax.rem(z + dz, SZ)))
    for dx in (1, FX - 1):
        tell((lax.rem(f + dx, FX), y, 1 - z))
        for dy in (1, FY - 1):
            tell((lax.rem(f + dx, FX), lax.rem(y + dy, FY), z))
    for relays, step in ((HIGH_RELAYS, 1), (LOW_RELAYS, OWN - 1)):
        there = lax.rem(own + step, OWN)

        for relay, first in zip(relays, (12, 4)):

            @pl.when(f == relay)
            def _():
                for n in range(8):
                    tell(((first + n) % FX, there // SZ, lax.rem(there, SZ)))

    return sem


def wait(ref, sem):
    pltpu.make_async_copy(ref, ref, sem).wait()


def kernel(
    pop_h, relax_h, vel_h, count_h, cell_h, node_h, weight_h, disp_h, mass_h, connect_h,
    modulus_h, basis_h,
    out_pop_h, out_sol, out_res,
    pop, relax, vel, count, cell, node, weight, disp, mass, connect, modulus, basis,
    sup_send, sup_recv, wall_send, wall_recv, frc_send, frc_recv, edge_send, edge_recv,
    xs, xr, ys, yr, ds, dr, zs, zr, zxr, zys, zyr,
    rs_send, rs_recv, rl_recv, sc_send, sc_recv, ag_send, ag_recv,
    post, field, rho_ref, gain, cell_lo, cell_hi, live_ref, wallp,
    sup_lo, sup_hi, el_lo, el_hi, pick, spread, vec_r, vec_p, vec_s, vec_w, vec_x,
    massx, rc, load_ref, out_pop, s_in, s_out,
    s_sup, r_sup, s_wall, r_wall, s_frc, r_frc, s_edge, r_edge, s_halo, r_halo,
    s_rs, r_rs, s_rl, r_rl, s_sc, r_sc, s_ag, r_ag,
):
    f = lax.axis_index("fx")
    y = lax.axis_index("fy")
    z = lax.axis_index("sz")
    own = y * SZ + z

    def at_owner(o, fx=None):
        return (f if fx is None else fx, o // SZ, lax.rem(o, SZ))

    def to_owners(src_of, dst, ssem, rsem):
        for dy, dz in FAR_OWN:
            there = (f, lax.rem(y + dy, FY), lax.rem(z + dz, SZ))
            send(src_of(there[1] * SZ + there[2]), dst, ssem, rsem, there)

    inputs = [
        (node_h, node), (weight_h, weight), (disp_h, disp), (mass_h, mass), (connect_h, connect),
        (basis_h, basis), (cell_h, cell), (count_h, count), (pop_h, pop), (relax_h, relax),
        (vel_h, vel), (modulus_h, modulus),
    ]
    copies = [pltpu.make_async_copy(a, b, s_in.at[n]) for n, (a, b) in enumerate(inputs)]
    for copy in copies[:2]:
        copy.start()
    barrier = greet(f, y, z, own)
    for copy in copies[2:]:
        copy.start()

    lane = iota((1, 128), 1)
    group = lane // 32
    expand = (iota((32, 128), 0) == lax.rem(iota((32, 128), 1), 32)).astype(F32)
    quarter = (lax.rem(iota((256, 128), 0), 16) // 4) == (iota((256, 128), 1) // 32)
    upper = iota((8, 128), 0) < 4
    copies[0].wait()
    copies[1].wait()
    spread_n = exact_dot(node[...].astype(F32).reshape(256, 32), expand)
    spread_w = exact_dot(weight[...].reshape(256, 32), expand)
    spread_n = jnp.where(quarter, spread_n, 0.0)
    spread_w = jnp.where(quarter, spread_w, 0.0)

    def packed(x, o):
        x = x[o * 16 : o * 16 + 8] + x[o * 16 + 8 : o * 16 + 16]
        return x + pltpu.roll(x, 4, 0)

    for o in range(OWN):
        sup_send[o] = jnp.where(upper, packed(spread_n, o), packed(spread_w, o))
    sup_recv[own] = sup_send[own]
    pl.semaphore_wait(barrier, 15 + 15 + 6 + 2)
    to_owners(lambda o: sup_send.at[o], sup_recv.at[own], s_sup, r_sup.at[own])

    copies[2].wait()
    copies[3].wait()
    for c in range(3):
        edge_send[c : c + 1, :] = disp[c : c + 1, 3840:4096]
    massx[...] = jnp.zeros((24, 256), F32)
    for h in range(16):
        massx[h : h + 1, 0:128] = mass[2 * h : 2 * h + 1, :]
        massx[h : h + 1, 128:256] = mass[2 * h + 1 : 2 * h + 2, :]
    edge_send[3:4, :] = massx[15:16, :]
    after, before = lax.rem(own + 1, OWN), lax.rem(own + OWN - 1, OWN)
    send(edge_send, edge_recv, s_edge, r_edge, at_owner(after))

    copies[4].wait()
    copies[5].wait()
    for j in range(8):
        n = connect[j : j + 1, :]
        lo = lax.rem(n, 256)
        hi = jnp.where(n < 256, 16, n // 256 - 1)
        el_lo[j] = jnp.where(iota((256, 512), 0) == lo, 1.0, 0.0).astype(BF16)
        el_hi[j] = jnp.where(iota((24, 512), 0) == hi, 1.0, 0.0)
    base = basis[...]
    gram = exact_dot(base, base, ((0,), (0,)))
    thrice = lax.rem(iota((24, 96), 1), 32) == iota((24, 96), 0)
    gram = exact_dot(gram, thrice.astype(F32))
    gram_top = gram.astype(BF16).astype(F32)
    gram = jnp.where(iota((24, 96), 1) < 64, gram_top, gram - gram_top).astype(BF16)

    copies[6].wait()
    copies[7].wait()
    cells = cell[...]
    cell_hi16 = exact_dot((cells // 256).astype(F32), expand)
    cell_lo16 = exact_dot(lax.rem(cells, 256).astype(F32), expand)
    diag = iota((16, 16), 0) == iota((16, 16), 1)
    counts = jnp.sum(jnp.where(diag, count[...].astype(F32), 0.0), axis=1, keepdims=True)
    live16 = (lax.rem(iota((16, 128), 1), 32).astype(F32) < counts).astype(F32)
    mine = lax.rem(iota((16, 128), 0), 4) == (iota((16, 128), 1) // 32)
    fold = ((iota((8, 16), 1) // 4) == iota((8, 16), 0)).astype(F32)

    def rows_of(x):
        return exact_dot(fold, jnp.where(mine, x, 0.0))

    hi_rows, lo_rows = rows_of(cell_hi16).astype(I32), rows_of(cell_lo16).astype(I32)
    live_ref[...] = rows_of(live16)
    for g in range(4):
        at = slice(g * 128, g * 128 + 128)
        cell_lo[:, at] = jnp.where(iota((256, 128), 0) == lo_rows[g : g + 1], 1.0, 0.0).astype(BF16)
        cell_hi[:, at] = jnp.where(iota((32, 128), 0) == hi_rows[g : g + 1], 1.0, 0.0)

    def moments(fs):
        rho = fs[0]
        for i in range(1, 19):
            rho = rho + fs[i]
        mom = []
        for a in range(3):
            total = None
            for i in range(1, 19, 2):
                s = VEL[i][a]
                if s:
                    pair = fs[i] - fs[i + 1] if s > 0 else fs[i + 1] - fs[i]
                    total = pair if total is None else total + pair
            mom.append(total)
        return rho, mom

    def along(c, v):
        total = None
        for a in range(3):
            if c[a] == 1:
                total = v[a] if total is None else total + v[a]
        for a in range(3):
            if c[a] == -1:
                total = -v[a] if total is None else total - v[a]
        return total

    def collide(source):
        for k in range(4):
            fs = [source[i, k] for i in range(19)]
            om = relax[k]
            rho, mom = moments(fs)
            inv = 1.0 / rho
            u = [m * inv for m in mom]
            sq = 1.5 * (u[0] * u[0] + u[1] * u[1] + u[2] * u[2])
            rho_ref[k] = rho
            keep = 1.0 - om
            scaled = om * rho
            post[0, k] = keep * fs[0] + (1.0 / 3.0) * scaled * (1.0 - sq)
            for i in range(1, 19, 2):
                t = (1.0 / 18.0) if i < 7 else (1.0 / 36.0)
                a = along(VEL[i], u)
                ts = t * scaled
                even = ts * (1.0 + 4.5 * a * a - sq)
                odd = ts * (3.0 * a)
                post[i, k] = keep * fs[i] + (even + odd)
                post[i + 1, k] = keep * fs[i + 1] + (even - odd)

    def turn(i, v):
        cy, cz = VEL[i][1], VEL[i][2]
        if cy:
            v = pltpu.roll(v, cy % 8, 0)
        if cz:
            v = pltpu.roll(v, cz % 256, 1)
        return v

    lane8 = iota((8, 128), 1)
    row8 = iota((8, 128), 0)

    def stream(step, target, wall_gain):
        for k in range(4):
            for c in range(3):
                gain[c, k] = wall_gain[c][k] * rho_ref[k] * (1.0 / 6.0)
        xp, xm = lax.rem(f + 1, FX), lax.rem(f + FX - 1, FX)
        yp, ym = lax.rem(y + 1, FY), lax.rem(y + FY - 1, FY)
        zo = 1 - z
        jobs = {
            "x0": (xs.at[step, 0], xr.at[step, 0], (xp, y, z)),
            "x1": (xs.at[step, 1], xr.at[step, 1], (xm, y, z)),
            "y0": (ys.at[step, 0], yr.at[step, 0], (f, yp, z)),
            "y1": (ys.at[step, 1], yr.at[step, 1], (f, ym, z)),
            "d0": (ds.at[step, 0], dr.at[step, 0], (xp, yp, z)),
            "d1": (ds.at[step, 1], dr.at[step, 1], (xm, ym, z)),
            "d2": (ds.at[step, 2], dr.at[step, 2], (xp, ym, z)),
            "d3": (ds.at[step, 3], dr.at[step, 3], (xm, yp, z)),
            "zx0": (zs.at[step, 0], zxr.at[step, 0], (xp, y, zo)),
            "zx1": (zs.at[step, 3], zxr.at[step, 1], (xm, y, zo)),
            "zy0": (zys.at[step, 0], zyr.at[step, 0], (f, yp, zo)),
            "zy1": (zys.at[step, 1], zyr.at[step, 1], (f, ym, zo)),
            "z": (zs.at[step], zr.at[step], (f, y, zo)),
        }
        index = {name: n for n, name in enumerate(jobs)}

        def go(*names):
            for name in names:
                src, dst, device = jobs[name]
                n = index[name]
                send(src, dst, s_halo.at[step, n], r_halo.at[step, n], device)

        def came(*names):
            for name in names:
                wait(jobs[name][1], r_halo.at[step, index[name]])

        for x in (0, 3, 1, 2):
            zpack = jnp.zeros((8, 128), F32)
            for i in range(19):
                cx, cy, cz = VEL[i]
                k = (x - cx) % 4
                v = post[i, k]
                if i:
                    push = along(VEL[i], [gain[c, k] for c in range(3)])
                    v = v + (2.0 * push if i < 7 else push)
                v = turn(i, v)
                if k != x - cx:
                    side = 0 if cx > 0 else 1
                    xs[step, side, X_POPS[side].index(i)] = v
                    if cy:
                        r = 0 if cy > 0 else 7
                        ds[step, DIAGONAL.index(i)] = v[r : r + 1, :]
                else:
                    target[i, x] = v
                if cy:
                    side = 0 if cy > 0 else 1
                    r = 0 if cy > 0 else 7
                    ys[step, side, Y_POPS[side].index(i), x : x + 1, :] = v[r : r + 1, :]
                if cz:
                    col = v[:, 0:1] if cz > 0 else v[:, 255:256]
                    zpack = jnp.where(lane8 == Z_POPS.index(i), col, zpack)
            zs[step, x] = zpack
            zys[step, 0, x : x + 1, :] = zpack[0:1, :]
            zys[step, 1, x : x + 1, :] = zpack[7:8, :]
            if x == 0:
                go("zx0", "d0", "d2", "x0")
            if x == 3:
                go("zx1", "d1", "d3", "x1")
        go("zy0", "zy1", "z", "y0", "y1")
        came("x0", "x1")
        for side in range(2):
            for n, i in enumerate(X_POPS[side]):
                target[i, 0 if side == 0 else 3] = xr[step, side, n]
        came("y0", "y1")
        for side in range(2):
            r = 0 if side == 0 else 7
            for n, i in enumerate(Y_POPS[side]):
                cx = VEL[i][0]
                for x in range(4):
                    if 0 <= x - cx <= 3:
                        target[i, x, r : r + 1, :] = yr[step, side, n, x : x + 1, :]
        came("d0", "d1", "d2", "d3")
        for n, i in enumerate(DIAGONAL):
            cx, cy, _ = VEL[i]
            r = 0 if cy > 0 else 7
            target[i, 0 if cx > 0 else 3, r : r + 1, :] = dr[step, n]
        came("z", "zx0", "zx1", "zy0", "zy1")
        z11, z12, z13, z14, z15, z16, z17, z18 = [Z_POPS.index(i) for i in range(11, 19)]
        for x in range(4):
            zin = zr[step, x]
            if x == 0:
                zin = jnp.where((lane8 == z11) | (lane8 == z13), zxr[step, 0], zin)
            if x == 3:
                zin = jnp.where((lane8 == z12) | (lane8 == z14), zxr[step, 1], zin)
            low = (row8 == 0) & ((lane8 == z15) | (lane8 == z17))
            high = (row8 == 7) & ((lane8 == z16) | (lane8 == z18))
            zin = jnp.where(low, zyr[step, 0, x : x + 1, :], zin)
            zin = jnp.where(high, zyr[step, 1, x : x + 1, :], zin)
            for n, i in enumerate(Z_POPS):
                col = zin[:, n : n + 1]
                if VEL[i][2] > 0:
                    target[i, x, :, 0:128] = jnp.where(lane8 == 0, col, target[i, x, :, 0:128])
                else:
                    target[i, x, :, 128:256] = jnp.where(
                        lane8 == 127, col, target[i, x, :, 128:256]
                    )
        return list(jobs.values())

    copies[8].wait()
    copies[9].wait()
    collide(pop)

    copies[10].wait()
    copies[11].wait()
    for c in range(3):
        for h in range(16):
            load_ref[c * 16 + h : c * 16 + h + 1, :] = vel[c : c + 1, h * 256 : h * 256 + 256]
    table = split2(load_ref[...])
    steps = [(0, 0)] + list(reversed(FAR_OWN))
    batches = [list(enumerate(steps))[:NEAR], list(enumerate(steps))[NEAR:]]

    def partner(step):
        there = (f, lax.rem(y + step[0], FY), lax.rem(z + step[1], SZ))
        return there, there[1] * SZ + there[2]

    for batch in batches:
        for n, step in batch:
            if n:
                o = partner(step)[1]
                wait(sup_recv.at[o], r_sup.at[o])
        for n, step in batch:
            there, o = partner(step)
            tile = sup_recv[o]
            for r in range(4):
                node_row = tile[r : r + 1].astype(I32)
                sup_lo[n, :, r * 128 : r * 128 + 128] = jnp.where(
                    iota((256, 128), 0) == lax.rem(node_row, 256), 1.0, 0.0
                ).astype(BF16)
                sup_hi[n, :, r * 128 : r * 128 + 128] = jnp.where(
                    iota((16, 128), 0) == node_row // 256, tile[r + 4 : r + 5], 0.0
                )
        for n, step in batch:
            there, o = partner(step)
            out = dot_nn(table, sup_lo[n])
            out = out[0:48] + out[48:96]
            hot = sup_hi[n]
            for c in range(3):
                m = out[c * 16 : c * 16 + 16] * hot
                m = m[:, 0:128] + m[:, 128:256] + m[:, 256:384] + m[:, 384:512]
                wall_send[n, c : c + 1, :] = jnp.sum(m, axis=0, keepdims=True)
            wall_send[n, 3:4, :] = jnp.zeros((1, 128), F32)
        for n, step in reversed(batch):
            there, o = partner(step)
            if n:
                send(wall_send.at[n], wall_recv.at[own], s_wall, r_wall, there)
            else:
                wall_recv[own] = wall_send[0]

    def elements(values):
        both = split2(values)

        for j in range(8):
            out = dot_nn(both, el_lo[j])
            out = out[0:80] + out[80:160]
            hot = el_hi[j]
            for c in range(3):
                pick[c * 8 + j : c * 8 + j + 1, :] = jnp.sum(
                    out[c * 24 : c * 24 + 24] * hot, axis=0, keepdims=True
                )
        picked = pick[...]
        wide = jnp.concatenate([picked, jnp.zeros((8, 512), F32)], axis=0)
        top = wide.astype(BF16)
        rest = (wide - top.astype(F32)).astype(BF16)
        spread[...] = dot_nn(gram, jnp.concatenate([top, rest, top], axis=0)) * modulus[...]
        total = None
        for j in range(8):
            hot = el_hi[j]
            parts = [hot * spread[c * 8 + j : c * 8 + j + 1, :] for c in range(3)]
            parts.append(jnp.zeros((8, 512), F32))
            part = dot_nt(split2(jnp.concatenate(parts, axis=0)), el_lo[j])
            total = part if total is None else total + part
        return total[0:80] + total[80:160]

    wait(edge_recv, r_edge)
    vec_r[...] = jnp.zeros((80, 256), F32)
    has_before = (own > 0).astype(F32)
    has_after = (own < OWN - 1).astype(F32)
    for c in range(3):
        for h in range(16):
            row = disp[c : c + 1, h * 256 : h * 256 + 256]
            vec_r[c * 24 + h : c * 24 + h + 1, :] = row
            vec_x[c * 16 + h : c * 16 + h + 1, :] = row
        vec_r[c * 24 + 16 : c * 24 + 17, :] = edge_recv[c : c + 1, :] * has_before
    vec_w[...] = elements(vec_r[...])
    massx[16:17, :] = edge_recv[3:4, :]

    wait(wall_recv.at[pl.ds(0, OWN - 1)], r_wall)
    wall = [None] * 4
    for g in range(4):
        total = jnp.zeros((4, 128), F32)
        for q in range(4):
            total = jnp.where(group == q, group_sum(wall_recv[g * 4 + q]), total)
        wall[g] = total * live_ref[g : g + 1, :]
    for g in range(4):
        hot = cell_hi[:, g * 128 : g * 128 + 128]
        parts = [hot * wall[g][c : c + 1, :] for c in range(3)]
        wallp[:, g * 128 : g * 128 + 128] = split2(jnp.concatenate(parts, axis=0))
    summed = dot_nt(wallp[...], cell_lo[...])
    summed = summed[0:96] + summed[96:192]
    wall_gain = [
        [summed[c * 32 + k * 8 : c * 32 + k * 8 + 8, :] for k in range(4)] for c in range(3)
    ]

    jobs0 = stream(0, field, wall_gain)
    collide(field)
    jobs1 = stream(1, out_pop, wall_gain)

    pop_copy = pltpu.make_async_copy(out_pop, out_pop_h, s_out)
    pop_copy.start()

    rows = [[], [], [], []]
    for k in range(4):
        rho, mom = moments([out_pop[i, k] for i in range(19)])
        for q, part in enumerate([rho] + mom):
            rows[q].append(part)
    values = jnp.concatenate([r for q in range(4) for r in rows[q]], axis=0)
    at_slots = dot_nn(split2(values), cell_lo[...])
    at_slots = at_slots[0:128] + at_slots[128:256]
    hot = cell_hi[...]
    slot = [
        jnp.sum(at_slots[q * 32 : q * 32 + 32] * hot, axis=0, keepdims=True) for q in range(4)
    ]
    row4 = iota((4, 128), 0)
    for g in range(4):
        at = slice(g * 128, g * 128 + 128)
        mom = jnp.zeros((4, 128), F32)
        for c in range(3):
            mom = jnp.where(row4 == c, slot[c + 1][:, at], mom)
        force = (mom - slot[0][:, at] * wall[g]) * live_ref[g : g + 1, :]
        for q in range(4):
            frc_send[g * 4 + q] = group_sum(jnp.where(group == q, force, 0.0))
    frc_recv[own] = frc_send[own]
    to_owners(lambda o: frc_send.at[o], frc_recv.at[own], s_frc, r_frc.at[own])
    wait(sup_recv.at[pl.ds(0, OWN - 1)], s_sup)
    wait(edge_send, s_edge)
    wait(wall_recv.at[pl.ds(0, OWN - 1)], s_wall)
    for step, jobs in enumerate((jobs0, jobs1)):
        for n, (src, dst, device) in enumerate(jobs):
            wait(src, s_halo.at[step, n])

    total = None
    for batch in batches:
        for n, step in batch:
            if n:
                o = partner(step)[1]
                wait(frc_recv.at[o], r_frc.at[o])
        for n, step in batch:
            force = frc_recv[partner(step)[1]]
            parts = []
            for c in range(3):
                line = force[c : c + 1, :]
                line = jnp.concatenate([line] * 4, axis=1)
                parts.append(sup_hi[n] * line)
            got = dot_nt(split2(jnp.concatenate(parts, axis=0)), sup_lo[n])
            total = got if total is None else total + got
    load_ref[...] = total[0:48] + total[48:96]

    row4w = iota((4, 256), 0)
    place = lax.rem(f + 4, FX)
    spot = lax.rem(place, 8)
    high = jnp.where(place < 8, HIGH_RELAYS[0], HIGH_RELAYS[1])
    low = high - 1
    is_high = (f == HIGH_RELAYS[0]) | (f == HIGH_RELAYS[1])
    is_low = (f == LOW_RELAYS[0]) | (f == LOW_RELAYS[1])
    is_double = (f == HIGH_RELAYS[1]) | is_low
    keep_after = jnp.where(is_high, has_after, 1.0)

    def exchange(app, sums, scalars):
        for c in range(3):
            for h in range(17):
                rs_send[app, h, c : c + 1, :] = sums[c * 24 + h : c * 24 + h + 1, :]
        top, ghost = rs_send.at[app, 15], rs_send.at[app, 16]
        send(ghost, rl_recv.at[app, 8 + spot], s_rl.at[app], r_rl.at[app], at_owner(before, high))
        send(top, rl_recv.at[app, 8 + spot], s_rl.at[app], r_rl.at[app], at_owner(after, low))
        for d in FAR_X:
            j = lax.rem(f + d, FX)

            @pl.when(j < 15)
            def _():
                send(rs_send.at[app, j], rs_recv.at[app, f], s_rs.at[app], r_rs.at[app], (j, y, z))

        @pl.when(f != high)
        def _():
            send(top, rl_recv.at[app, spot], s_rl.at[app], r_rl.at[app], (high, y, z))

        @pl.when(f != low)
        def _():
            send(ghost, rl_recv.at[app, spot], s_rl.at[app], r_rl.at[app], (low, y, z))

        if scalars is not None:
            scalars()
            to_owners(lambda o: sc_send.at[app], sc_recv.at[app, own], s_sc.at[app], r_sc.at[app])
        rs_recv[app, f] = rs_send[app, f]

        @pl.when(f < 15)
        def _():
            wait(rs_recv.at[app, pl.ds(0, FX - 1)], r_rs.at[app])
            total = rs_recv[app, 0]
            for n in range(1, FX):
                total = total + rs_recv[app, n]
            ag_send[app, 0] = total

        @pl.when(is_high | is_low)
        def _():
            rl_recv[app, spot] = rs_send[app, jnp.where(is_high, 15, 16)]
            wait(rl_recv.at[app, pl.ds(0, 15)], r_rl.at[app])
            here, there = rl_recv[app, 0], rl_recv[app, 8]
            for n in range(1, 8):
                here = here + rl_recv[app, n]
                there = there + rl_recv[app, 8 + n]
            ag_send[app, 1] = here + keep_after * there

        @pl.when(f == 15)
        def _():
            ag_send[app, 0] = ag_send[app, 1]

        if scalars is not None:
            wait(sc_recv.at[app, pl.ds(0, OWN - 1)], r_sc.at[app])
            part = sc_recv[app, 0]
            for n in range(1, OWN):
                part = part + sc_recv[app, n]
            ag_send[app, 0] = jnp.where(
                row4w == 3, part, ag_send[app, 0]
            )
        @pl.when(is_double)
        def _():
            for d in FAR_X:
                send(
                    ag_send.at[app], ag_recv.at[app, pl.ds(2 * f, 2)], s_ag.at[app], r_ag.at[app],
                    (lax.rem(f + d, FX), y, z),
                )
            ag_recv[app, 2 * f + 1] = ag_send[app, 1]

        @pl.when(jnp.logical_not(is_double))
        def _():
            for d in FAR_X:
                send(
                    ag_send.at[app, 0], ag_recv.at[app, 2 * f], s_ag.at[app], r_ag.at[app],
                    (lax.rem(f + d, FX), y, z),
                )

        ag_recv[app, 2 * f] = ag_send[app, 0]

        wait(rs_recv.at[app, pl.ds(0, 14)], s_rs.at[app])
        wait(rs_recv.at[app, pl.ds(0, 3)], s_rl.at[app])
        if scalars is not None:
            wait(sc_recv.at[app, pl.ds(0, OWN - 1)], s_sc.at[app])

        @pl.when(f == 15)
        def _():
            wait(rs_recv.at[app, 0], s_rs.at[app])

        @pl.when(jnp.logical_not(is_high | is_low))
        def _():
            wait(rs_recv.at[app, 0], s_rl.at[app])

        @pl.when(is_double)
        def _():
            wait(ag_recv.at[app, pl.ds(0, 17)], r_ag.at[app])

        @pl.when(jnp.logical_not(is_double))
        def _():
            wait(ag_recv.at[app, pl.ds(0, 18)], r_ag.at[app])

    def gathered(app, target):
        for c in range(3):
            for h in range(15):
                target[c * 24 + h : c * 24 + h + 1, :] = ag_recv[app, 2 * h, c : c + 1, :]
            target[c * 24 + 15 : c * 24 + 16, :] = (
                ag_recv[app, 2 * HIGH_RELAYS[0], c : c + 1, :]
                + ag_recv[app, 2 * HIGH_RELAYS[1] + 1, c : c + 1, :]
            )
            target[c * 24 + 16 : c * 24 + 17, :] = has_before * (
                ag_recv[app, 2 * LOW_RELAYS[0] + 1, c : c + 1, :]
                + ag_recv[app, 2 * LOW_RELAYS[1] + 1, c : c + 1, :]
            )

    kdisp = vec_w[...]
    pad8 = jnp.zeros((8, 256), F32)
    loads = []
    for c in range(3):
        loads += [FORCE_SCALE * load_ref[c * 16 : c * 16 + 16, :], pad8]
    loads.append(pad8)
    exchange(0, jnp.concatenate(loads, axis=0) - kdisp, None)
    gathered(0, vec_r)
    wait(frc_recv.at[pl.ds(0, OWN - 1)], s_frc)
    pop_copy.wait()
    vec_p[...] = jnp.zeros((80, 256), F32)
    vec_s[...] = jnp.zeros((80, 256), F32)
    vec_w[...] = jnp.zeros((80, 256), F32)

    def iteration(app, carry):
        alpha, gamma = carry
        for c in range(3):
            rc[c : c + 1, :] = vec_r[pl.ds(c * 24 + f, 1), :]
        rc[3:4, :] = jnp.zeros((1, 256), F32)
        chunk = rc[...]
        mine = jnp.sum(chunk * chunk, keepdims=True)
        held = jnp.sum(massx[pl.ds(f, 1), :] * chunk * chunk, keepdims=True)

        def tell():
            energy = held + jnp.sum(pick[...] * spread[...], keepdims=True)
            scalars = jnp.where(iota((1, 256), 1) < 128, mine, energy)
            sc_send[app] = scalars
            sc_recv[app, own] = scalars

        exchange(app, elements(vec_r[...]), tell)
        gathered(app, vec_w)
        both = ag_recv[app, 0]
        for n in range(1, FX):
            both = both + ag_recv[app, 2 * n]
        new = both[3:4, 0:128]
        delta = both[3:4, 128:256]
        beta = jnp.where(app == 1, 0.0, new / gamma)
        alpha = new / (delta - beta * new / alpha)
        weights = massx[...]
        weights = jnp.concatenate([weights] * 3 + [pad8], axis=0)
        beta2 = jnp.concatenate([beta, beta], axis=1)
        alpha2 = jnp.concatenate([alpha, alpha], axis=1)
        p = vec_r[...] + beta2 * vec_p[...]
        s = vec_w[...] + weights * vec_r[...] + beta2 * vec_s[...]
        vec_p[...] = p
        vec_s[...] = s
        vec_r[...] = vec_r[...] - alpha2 * s
        for c in range(3):
            vec_x[c * 16 : c * 16 + 16, :] += alpha2 * p[c * 24 : c * 24 + 16, :]
        return alpha, new

    one = jnp.ones((1, 128), F32)
    lax.fori_loop(1, APPS, iteration, (one, one))

    for c in range(3):
        for h in range(16):
            at = slice(h * 256, h * 256 + 256)
            out_sol[c : c + 1, at] = vec_x[c * 16 + h : c * 16 + h + 1, :]
            out_res[c : c + 1, at] = vec_r[c * 24 + h : c * 24 + h + 1, :]

    for app in range(APPS):
        wait(ag_recv.at[app, pl.ds(0, FX - 1)], s_ag.at[app])

        @pl.when(is_double)
        def _():
            wait(ag_recv.at[app, pl.ds(0, FX - 1)], s_ag.at[app])


SCRATCH = dict(
    pop=(19, 4, 8, 256), relax=(4, 8, 256), vel=(3, 4096), count=((1, 16), I32),
    cell=((16, 32), I32), node=((16, 16, 32), I32), weight=(16, 16, 32), disp=(3, 4096),
    mass=(32, 128), connect=((8, 512), I32), modulus=(1, 512), basis=(24, 24),
    sup_send=(16, 8, 128), sup_recv=(16, 8, 128),
    wall_send=(16, 4, 128), wall_recv=(16, 4, 128),
    frc_send=(16, 4, 128), frc_recv=(16, 4, 128),
    edge_send=(4, 256), edge_recv=(4, 256),
    xs=(2, 2, 5, 8, 256), xr=(2, 2, 5, 8, 256),
    ys=(2, 2, 5, 4, 256), yr=(2, 2, 5, 4, 256),
    ds=(2, 4, 1, 256), dr=(2, 4, 1, 256),
    zs=(2, 4, 8, 128), zr=(2, 4, 8, 128), zxr=(2, 2, 8, 128),
    zys=(2, 2, 4, 128), zyr=(2, 2, 4, 128),
    rs_send=(APPS, 17, 4, 256), rs_recv=(APPS, 16, 4, 256), rl_recv=(APPS, 16, 4, 256),
    sc_send=(APPS, 1, 256), sc_recv=(APPS, 16, 1, 256),
    ag_send=(APPS, 2, 4, 256), ag_recv=(APPS, 32, 4, 256),
    post=(19, 4, 8, 256), field=(19, 4, 8, 256), rho_ref=(4, 8, 256), gain=(3, 4, 8, 256),
    cell_lo=((256, 512), BF16), cell_hi=(32, 512), live_ref=(8, 128), wallp=((192, 512), BF16),
    sup_lo=((16, 256, 512), BF16), sup_hi=(16, 16, 512),
    el_lo=((8, 256, 512), BF16), el_hi=(8, 24, 512),
    pick=(24, 512), spread=(24, 512),
    vec_r=(80, 256), vec_p=(80, 256), vec_s=(80, 256), vec_w=(80, 256), vec_x=(48, 256),
    massx=(24, 256), rc=(4, 256), load_ref=(48, 256), out_pop=(19, 4, 8, 256),
)


def scratch_shapes():
    shapes = []
    for shape in SCRATCH.values():
        kind = F32
        if isinstance(shape[0], tuple):
            shape, kind = shape
        shapes.append(pltpu.VMEM(shape, kind))
    dma = pltpu.SemaphoreType.DMA
    shapes += [dma((INPUTS,)), dma]
    shapes += [dma, dma((OWN,)), dma, dma, dma, dma((OWN,)), dma, dma]
    shapes += [dma((2, 13))] * 2 + [dma((APPS,))] * 8
    return shapes


def deliver(pop_h, sol_h, res_h, pop_out, sol_out, res_out, pop, sol, res, s_in, s_out):
    jobs = [(pop_h.at[pl.ds(n, 4)], pop.at[pl.ds(n, 4)], pop_out.at[pl.ds(n, 4)]) for n in (0, 4, 8, 12)]
    jobs.append((pop_h.at[pl.ds(16, 3)], pop.at[pl.ds(16, 3)], pop_out.at[pl.ds(16, 3)]))
    jobs += [(sol_h, sol, sol_out), (res_h, res, res_out)]
    copies = []
    for n, (a, b, c) in enumerate(jobs):
        copies.append(
            (pltpu.make_async_copy(a, b, s_in.at[n]), pltpu.make_async_copy(b, c, s_out.at[n]))
        )
        copies[n][0].start()
    for came, goes in copies:
        came.wait()
        goes.start()
    for came, goes in copies:
        goes.wait()


def body(
    populations, relaxation, struct_velocity, iface_count, iface_cell, rbf_node, rbf_weight,
    disp_prev, node_mass, connect, modulus, strain_basis,
):
    vmem = pl.BlockSpec(memory_space=pltpu.VMEM)
    hbm = pl.BlockSpec(memory_space=pl.ANY)
    shapes = (
        jax.ShapeDtypeStruct(populations.shape, F32),
        jax.ShapeDtypeStruct(disp_prev.shape, F32),
        jax.ShapeDtypeStruct(disp_prev.shape, F32),
    )
    results = pl.pallas_call(
        kernel,
        out_shape=shapes,
        in_specs=[hbm] * INPUTS,
        out_specs=(hbm, vmem, vmem),
        scratch_shapes=scratch_shapes(),
        compiler_params=pltpu.CompilerParams(
            collective_id=0, has_side_effects=True, vmem_limit_bytes=62 * 1024 * 1024
        ),
        name="window",
    )(
        populations,
        relaxation,
        struct_velocity,
        iface_count.reshape(1, 16),
        iface_cell.reshape(16, 32),
        rbf_node.reshape(16, 16, 32),
        rbf_weight.reshape(16, 16, 32),
        disp_prev,
        node_mass.reshape(32, 128),
        connect.reshape(8, 512),
        modulus.reshape(1, 512),
        strain_basis,
    )
    return pl.pallas_call(
        deliver,
        out_shape=shapes,
        in_specs=[hbm] * 3,
        out_specs=(hbm, hbm, hbm),
        scratch_shapes=[pltpu.VMEM(s.shape, F32) for s in shapes]
        + [pltpu.SemaphoreType.DMA((7,))] * 2,
        compiler_params=pltpu.CompilerParams(vmem_limit_bytes=62 * 1024 * 1024),
        name="deliver",
    )(*results)


def solution(mesh):
    return jax.shard_map(
        body,
        mesh=mesh,
        in_specs=(
            P(None, "fx", "fy", "sz"),
            P("fx", "fy", "sz"),
            P(None, ("fy", "sz")),
            P("fx", "fy", "sz", None),
            P("fx", "fy", "sz", None, None),
            P("fx", "fy", "sz", None, None, None),
            P("fx", "fy", "sz", None, None, None),
            P(None, ("fy", "sz")),
            P(("fy", "sz")),
            P("fx", ("fy", "sz"), None, None),
            P("fx", ("fy", "sz"), None),
            P(),
        ),
        out_specs=(P(None, "fx", "fy", "sz"), P(None, ("fy", "sz")), P(None, ("fy", "sz"))),
        check_vma=False,
    )
```

```python
import jax
import jax.numpy as jnp
from jax import lax
from jax.experimental import pallas as pl
from jax.experimental.pallas import tpu as pltpu
from jax.sharding import PartitionSpec as P

F32 = jnp.float32
BF16 = jnp.bfloat16
I32 = jnp.int32
FX, FY, SZ = 16, 8, 2
OWN = 16
ITERS = 3
APPS = ITERS + 1
FORCE_SCALE = 20.0
VEL = [
    (0, 0, 0),
    (1, 0, 0),
    (-1, 0, 0),
    (0, 1, 0),
    (0, -1, 0),
    (0, 0, 1),
    (0, 0, -1),
    (1, 1, 0),
    (-1, -1, 0),
    (1, -1, 0),
    (-1, 1, 0),
    (1, 0, 1),
    (-1, 0, -1),
    (1, 0, -1),
    (-1, 0, 1),
    (0, 1, 1),
    (0, -1, -1),
    (0, 1, -1),
    (0, -1, 1),
]
X_POPS = [[i for i in range(19) if VEL[i][0] == s] for s in (1, -1)]
Y_POPS = [[i for i in range(19) if VEL[i][1] == s] for s in (1, -1)]
Z_POPS = [i for i in range(19) if VEL[i][2] != 0]
DIAGONAL = (7, 8, 9, 10)
MESH = pl.DeviceIdType.MESH
FAR_X = (8, 7, 9, 6, 10, 5, 11, 4, 12, 3, 13, 2, 14, 1, 15)
FAR_OWN = (
    (4, 1), (2, 1), (6, 1), (3, 1), (5, 1), (3, 0), (5, 0), (4, 0),
    (1, 1), (7, 1), (0, 1), (1, 0), (7, 0), (2, 0), (6, 0),
)
HIGH_RELAYS = (15, 7)
LOW_RELAYS = (14, 6)
INPUTS = 12
NEAR = 10


def split2(x):
    top = x.astype(BF16)
    rest = (x - top.astype(F32)).astype(BF16)
    return jnp.concatenate([top, rest], axis=0)


def dot_nt(a, b):
    return lax.dot_general(a, b, (((1,), (1,)), ((), ())), preferred_element_type=F32)


def dot_nn(a, b):
    return lax.dot_general(a, b, (((1,), (0,)), ((), ())), preferred_element_type=F32)


def exact_dot(a, b, dims=((1,), (0,))):
    return lax.dot_general(
        a, b, (dims, ((), ())), preferred_element_type=F32, precision=lax.Precision.HIGHEST
    )


def iota(shape, dim):
    return lax.broadcasted_iota(I32, shape, dim)


def group_sum(x):
    x = x + pltpu.roll(x, 64, x.ndim - 1)
    return x + pltpu.roll(x, 32, x.ndim - 1)


def send(src, dst, ssem, rsem, device):
    pltpu.make_async_remote_copy(
        src_ref=src,
        dst_ref=dst,
        send_sem=ssem,
        recv_sem=rsem,
        device_id=device,
        device_id_type=MESH,
    ).start()


def greet(f, y, z, own):
    sem = pltpu.get_barrier_semaphore()

    def tell(device):
        pl.semaphore_signal(sem, inc=1, device_id=device, device_id_type=MESH)

    for d in FAR_X:
        tell((lax.rem(f + d, FX), y, z))
    for dy, dz in FAR_OWN:
        tell((f, lax.rem(y + dy, FY), lax.rem(z + dz, SZ)))
    return sem


def wait(ref, sem):
    pltpu.make_async_copy(ref, ref, sem).wait()


def kernel(
    pop_h, relax_h, vel_h, count_h, cell_h, node_h, weight_h, disp_h, mass_h, connect_h,
    modulus_h, basis_h,
    out_pop_h, out_sol, out_res,
    pop, relax, vel, count, cell, node, weight, disp, mass, connect, modulus, basis,
    sup_send, sup_recv, wall_send, wall_recv, frc_send, frc_recv, edge_send, edge_recv,
    xs, xr, ys, yr, ds, dr, zs, zr, zxr, zys, zyr,
    rs_send, rs_recv, rl_recv, sc_send, sc_recv, ag_send, ag_recv,
    post, field, rho_ref, gain, cell_lo, cell_hi, live_ref, wallp,
    sup_lo, sup_hi, el_lo, el_hi, el_gh, pick, spread, vec_r, vec_p, vec_s, vec_w, vec_x,
    massx, rc, load_ref, out_pop, s_in, s_out,
    s_sup, r_sup, s_wall, r_wall, s_frc, r_frc, s_edge, r_edge, s_halo, r_halo,
    s_rs, r_rs, s_rl, r_rl, s_sc, r_sc, s_ag, r_ag,
):
    f = lax.axis_index("fx")
    y = lax.axis_index("fy")
    z = lax.axis_index("sz")
    own = y * SZ + z

    def at_owner(o, fx=None):
        return (f if fx is None else fx, o // SZ, lax.rem(o, SZ))

    def to_owners(src_of, dst, ssem, rsem):
        for dy, dz in FAR_OWN:
            there = (f, lax.rem(y + dy, FY), lax.rem(z + dz, SZ))
            send(src_of(there[1] * SZ + there[2]), dst, ssem, rsem, there)

    inputs = [
        (node_h, node), (weight_h, weight), (disp_h, disp), (mass_h, mass), (connect_h, connect),
        (basis_h, basis), (cell_h, cell), (count_h, count), (pop_h, pop), (relax_h, relax),
        (vel_h, vel), (modulus_h, modulus),
    ]
    copies = [pltpu.make_async_copy(a, b, s_in.at[n]) for n, (a, b) in enumerate(inputs)]
    for copy in copies[:2]:
        copy.start()
    barrier = greet(f, y, z, own)
    for copy in copies[2:]:
        copy.start()

    lane = iota((1, 128), 1)
    group = lane // 32
    expand = (iota((32, 128), 0) == lax.rem(iota((32, 128), 1), 32)).astype(F32)
    quarter = (lax.rem(iota((256, 128), 0), 16) // 4) == (iota((256, 128), 1) // 32)
    upper = iota((8, 128), 0) < 4
    copies[0].wait()
    copies[1].wait()
    spread_n = exact_dot(node[...].astype(F32).reshape(256, 32), expand)
    spread_w = exact_dot(weight[...].reshape(256, 32), expand)
    spread_n = jnp.where(quarter, spread_n, 0.0)
    spread_w = jnp.where(quarter, spread_w, 0.0)

    def packed(x, o):
        x = x[o * 16 : o * 16 + 8] + x[o * 16 + 8 : o * 16 + 16]
        return x + pltpu.roll(x, 4, 0)

    for o in range(OWN):
        sup_send[o] = jnp.where(upper, packed(spread_n, o), packed(spread_w, o))
    sup_recv[own] = sup_send[own]
    pl.semaphore_wait(barrier, 15 + 15)
    to_owners(lambda o: sup_send.at[o], sup_recv.at[own], s_sup, r_sup.at[own])

    copies[2].wait()
    copies[3].wait()
    for c in range(3):
        edge_send[c : c + 1, :] = disp[c : c + 1, 3840:4096]
    massx[...] = jnp.zeros((64, 256), F32)
    for h in range(16):
        massx[h : h + 1, 0:128] = mass[2 * h : 2 * h + 1, :]
        massx[h : h + 1, 128:256] = mass[2 * h + 1 : 2 * h + 2, :]
    massx[16:32, :] = massx[0:16, :]
    massx[32:48, :] = massx[0:16, :]
    edge_send[3:4, :] = massx[15:16, :]
    after, before = lax.rem(own + 1, OWN), lax.rem(own + OWN - 1, OWN)
    send(edge_send, edge_recv, s_edge, r_edge, at_owner(after))

    copies[4].wait()
    copies[5].wait()
    for j in range(8):
        n = connect[j : j + 1, :]
        lo = lax.rem(n, 256)
        hi = n // 256 - 1
        el_lo[j] = jnp.where(iota((256, 512), 0) == lo, 1.0, 0.0).astype(BF16)
        el_hi[j] = jnp.where(iota((16, 512), 0) == hi, 1.0, 0.0)
        el_gh[j : j + 1, :] = jnp.where(n < 256, 1.0, 0.0)
    base = basis[...]
    gram = exact_dot(base, base, ((0,), (0,)))
    thrice = lax.rem(iota((24, 96), 1), 32) == iota((24, 96), 0)
    gram = exact_dot(gram, thrice.astype(F32))
    gram_top = gram.astype(BF16).astype(F32)
    gram = jnp.where(iota((24, 96), 1) < 64, gram_top, gram - gram_top).astype(BF16)

    copies[6].wait()
    copies[7].wait()
    cells = cell[...]
    cell_hi16 = exact_dot((cells // 256).astype(F32), expand)
    cell_lo16 = exact_dot(lax.rem(cells, 256).astype(F32), expand)
    diag = iota((16, 16), 0) == iota((16, 16), 1)
    counts = jnp.sum(jnp.where(diag, count[...].astype(F32), 0.0), axis=1, keepdims=True)
    live16 = (lax.rem(iota((16, 128), 1), 32).astype(F32) < counts).astype(F32)
    mine = lax.rem(iota((16, 128), 0), 4) == (iota((16, 128), 1) // 32)
    fold = ((iota((8, 16), 1) // 4) == iota((8, 16), 0)).astype(F32)

    def rows_of(x):
        return exact_dot(fold, jnp.where(mine, x, 0.0))

    hi_rows, lo_rows = rows_of(cell_hi16).astype(I32), rows_of(cell_lo16).astype(I32)
    live_ref[...] = rows_of(live16)
    for g in range(4):
        at = slice(g * 128, g * 128 + 128)
        cell_lo[:, at] = jnp.where(iota((256, 128), 0) == lo_rows[g : g + 1], 1.0, 0.0).astype(BF16)
        cell_hi[:, at] = jnp.where(iota((32, 128), 0) == hi_rows[g : g + 1], 1.0, 0.0)

    def moments(fs):
        rho = fs[0]
        for i in range(1, 19):
            rho = rho + fs[i]
        mom = []
        for a in range(3):
            total = None
            for i in range(1, 19, 2):
                s = VEL[i][a]
                if s:
                    pair = fs[i] - fs[i + 1] if s > 0 else fs[i + 1] - fs[i]
                    total = pair if total is None else total + pair
            mom.append(total)
        return rho, mom

    def along(c, v):
        total = None
        for a in range(3):
            if c[a] == 1:
                total = v[a] if total is None else total + v[a]
        for a in range(3):
            if c[a] == -1:
                total = -v[a] if total is None else total - v[a]
        return total

    def collide(source):
        for k in range(4):
            fs = [source[i, k] for i in range(19)]
            om = relax[k]
            rho, mom = moments(fs)
            inv = 1.0 / rho
            u = [m * inv for m in mom]
            sq = 1.5 * (u[0] * u[0] + u[1] * u[1] + u[2] * u[2])
            rho_ref[k] = rho
            keep = 1.0 - om
            scaled = om * rho
            post[0, k] = keep * fs[0] + (1.0 / 3.0) * scaled * (1.0 - sq)
            for i in range(1, 19, 2):
                t = (1.0 / 18.0) if i < 7 else (1.0 / 36.0)
                a = along(VEL[i], u)
                ts = t * scaled
                even = ts * (1.0 + 4.5 * a * a - sq)
                odd = ts * (3.0 * a)
                post[i, k] = keep * fs[i] + (even + odd)
                post[i + 1, k] = keep * fs[i + 1] + (even - odd)

    def turn(i, v):
        cy, cz = VEL[i][1], VEL[i][2]
        if cy:
            v = pltpu.roll(v, cy % 8, 0)
        if cz:
            v = pltpu.roll(v, cz % 256, 1)
        return v

    lane8 = iota((8, 128), 1)
    row8 = iota((8, 128), 0)

    def stream(step, target, wall_gain):
        for k in range(4):
            for c in range(3):
                gain[c, k] = wall_gain[c][k] * rho_ref[k] * (1.0 / 6.0)
        xp, xm = lax.rem(f + 1, FX), lax.rem(f + FX - 1, FX)
        yp, ym = lax.rem(y + 1, FY), lax.rem(y + FY - 1, FY)
        zo = 1 - z
        jobs = {
            "x0": (xs.at[step, 0], xr.at[step, 0], (xp, y, z)),
            "x1": (xs.at[step, 1], xr.at[step, 1], (xm, y, z)),
            "y0": (ys.at[step, 0], yr.at[step, 0], (f, yp, z)),
            "y1": (ys.at[step, 1], yr.at[step, 1], (f, ym, z)),
            "d0": (ds.at[step, 0], dr.at[step, 0], (xp, yp, z)),
            "d1": (ds.at[step, 1], dr.at[step, 1], (xm, ym, z)),
            "d2": (ds.at[step, 2], dr.at[step, 2], (xp, ym, z)),
            "d3": (ds.at[step, 3], dr.at[step, 3], (xm, yp, z)),
            "zx0": (zs.at[step, 0], zxr.at[step, 0], (xp, y, zo)),
            "zx1": (zs.at[step, 3], zxr.at[step, 1], (xm, y, zo)),
            "zy0": (zys.at[step, 0], zyr.at[step, 0], (f, yp, zo)),
            "zy1": (zys.at[step, 1], zyr.at[step, 1], (f, ym, zo)),
            "z": (zs.at[step], zr.at[step], (f, y, zo)),
        }
        index = {name: n for n, name in enumerate(jobs)}

        def go(*names):
            for name in names:
                src, dst, device = jobs[name]
                n = index[name]
                send(src, dst, s_halo.at[step, n], r_halo.at[step, n], device)

        def came(*names):
            for name in names:
                wait(jobs[name][1], r_halo.at[step, index[name]])

        for x in (0, 3, 1, 2):
            zpack = jnp.zeros((8, 128), F32)
            for i in range(19):
                cx, cy, cz = VEL[i]
                k = (x - cx) % 4
                v = post[i, k]
                if i:
                    push = along(VEL[i], [gain[c, k] for c in range(3)])
                    v = v + (2.0 * push if i < 7 else push)
                v = turn(i, v)
                if k != x - cx:
                    side = 0 if cx > 0 else 1
                    xs[step, side, X_POPS[side].index(i)] = v
                    if cy:
                        r = 0 if cy > 0 else 7
                        ds[step, DIAGONAL.index(i)] = v[r : r + 1, :]
                else:
                    target[i, x] = v
                if cy:
                    side = 0 if cy > 0 else 1
                    r = 0 if cy > 0 else 7
                    ys[step, side, Y_POPS[side].index(i), x : x + 1, :] = v[r : r + 1, :]
                if cz:
                    col = v[:, 0:1] if cz > 0 else v[:, 255:256]
                    zpack = jnp.where(lane8 == Z_POPS.index(i), col, zpack)
            zs[step, x] = zpack
            zys[step, 0, x : x + 1, :] = zpack[0:1, :]
            zys[step, 1, x : x + 1, :] = zpack[7:8, :]
            if x == 0:
                go("zx0", "d0", "d2", "x0")
            if x == 3:
                go("zx1", "d1", "d3", "x1")
        go("zy0", "zy1", "z", "y0", "y1")
        came("x0", "x1")
        for side in range(2):
            for n, i in enumerate(X_POPS[side]):
                target[i, 0 if side == 0 else 3] = xr[step, side, n]
        came("y0", "y1")
        for side in range(2):
            r = 0 if side == 0 else 7
            for n, i in enumerate(Y_POPS[side]):
                cx = VEL[i][0]
                for x in range(4):
                    if 0 <= x - cx <= 3:
                        target[i, x, r : r + 1, :] = yr[step, side, n, x : x + 1, :]
        came("d0", "d1", "d2", "d3")
        for n, i in enumerate(DIAGONAL):
            cx, cy, _ = VEL[i]
            r = 0 if cy > 0 else 7
            target[i, 0 if cx > 0 else 3, r : r + 1, :] = dr[step, n]
        came("z", "zx0", "zx1", "zy0", "zy1")
        z11, z12, z13, z14, z15, z16, z17, z18 = [Z_POPS.index(i) for i in range(11, 19)]
        for x in range(4):
            zin = zr[step, x]
            if x == 0:
                zin = jnp.where((lane8 == z11) | (lane8 == z13), zxr[step, 0], zin)
            if x == 3:
                zin = jnp.where((lane8 == z12) | (lane8 == z14), zxr[step, 1], zin)
            low = (row8 == 0) & ((lane8 == z15) | (lane8 == z17))
            high = (row8 == 7) & ((lane8 == z16) | (lane8 == z18))
            zin = jnp.where(low, zyr[step, 0, x : x + 1, :], zin)
            zin = jnp.where(high, zyr[step, 1, x : x + 1, :], zin)
            for n, i in enumerate(Z_POPS):
                col = zin[:, n : n + 1]
                if VEL[i][2] > 0:
                    target[i, x, :, 0:128] = jnp.where(lane8 == 0, col, target[i, x, :, 0:128])
                else:
                    target[i, x, :, 128:256] = jnp.where(
                        lane8 == 127, col, target[i, x, :, 128:256]
                    )
        return list(jobs.values())

    copies[8].wait()
    copies[9].wait()
    collide(pop)

    copies[10].wait()
    copies[11].wait()
    for c in range(3):
        for h in range(16):
            load_ref[c * 16 + h : c * 16 + h + 1, :] = vel[c : c + 1, h * 256 : h * 256 + 256]
    table = split2(load_ref[...])
    steps = [(0, 0)] + list(reversed(FAR_OWN))
    batches = [list(enumerate(steps))[:NEAR], list(enumerate(steps))[NEAR:]]

    def partner(step):
        there = (f, lax.rem(y + step[0], FY), lax.rem(z + step[1], SZ))
        return there, there[1] * SZ + there[2]

    for batch in batches:
        for n, step in batch:
            if n:
                o = partner(step)[1]
                wait(sup_recv.at[o], r_sup.at[o])
        for n, step in batch:
            there, o = partner(step)
            tile = sup_recv[o]
            for r in range(4):
                node_row = tile[r : r + 1].astype(I32)
                sup_lo[n, :, r * 128 : r * 128 + 128] = jnp.where(
                    iota((256, 128), 0) == lax.rem(node_row, 256), 1.0, 0.0
                ).astype(BF16)
                sup_hi[n, :, r * 128 : r * 128 + 128] = jnp.where(
                    iota((16, 128), 0) == node_row // 256, tile[r + 4 : r + 5], 0.0
                )
        for n, step in batch:
            there, o = partner(step)
            out = dot_nn(table, sup_lo[n])
            out = out[0:48] + out[48:96]
            hot = sup_hi[n]
            for c in range(3):
                m = out[c * 16 : c * 16 + 16] * hot
                m = m[:, 0:128] + m[:, 128:256] + m[:, 256:384] + m[:, 384:512]
                wall_send[n, c : c + 1, :] = jnp.sum(m, axis=0, keepdims=True)
            wall_send[n, 3:4, :] = jnp.zeros((1, 128), F32)
        for n, step in reversed(batch):
            there, o = partner(step)
            if n:
                send(wall_send.at[n], wall_recv.at[own], s_wall, r_wall, there)
            else:
                wall_recv[own] = wall_send[0]

    def elements(values):
        both = split2(values)

        for j in range(8):
            out = dot_nn(both, el_lo[j])
            out = out[0:64] + out[64:128]
            hot, ghost = el_hi[j], el_gh[j : j + 1, :]
            for c in range(3):
                found = jnp.sum(out[c * 16 : c * 16 + 16] * hot, axis=0, keepdims=True)
                pick[c * 8 + j : c * 8 + j + 1, :] = found + out[48 + c : 49 + c] * ghost
        picked = pick[...]
        wide = jnp.concatenate([picked, jnp.zeros((8, 512), F32)], axis=0)
        top = wide.astype(BF16)
        rest = (wide - top.astype(F32)).astype(BF16)
        spread[...] = dot_nn(gram, jnp.concatenate([top, rest, top], axis=0)) * modulus[...]
        total = None
        for j in range(8):
            hot, ghost = el_hi[j], el_gh[j : j + 1, :]
            rows = [spread[c * 8 + j : c * 8 + j + 1, :] for c in range(3)]
            last = jnp.zeros((8, 512), F32)
            for c in range(3):
                last = jnp.where(iota((8, 512), 0) == c, rows[c] * ghost, last)
            parts = [hot * row for row in rows] + [last, jnp.zeros((8, 512), F32)]
            part = dot_nt(split2(jnp.concatenate(parts, axis=0)), el_lo[j])
            total = part if total is None else total + part
        return total[0:64] + total[64:128]

    wait(edge_recv, r_edge)
    vec_r[...] = jnp.zeros((64, 256), F32)
    has_before = (own > 0).astype(F32)
    has_after = (own < OWN - 1).astype(F32)
    for c in range(3):
        for h in range(16):
            row = disp[c : c + 1, h * 256 : h * 256 + 256]
            vec_r[c * 16 + h : c * 16 + h + 1, :] = row
            vec_x[c * 16 + h : c * 16 + h + 1, :] = row
        vec_r[48 + c : 49 + c, :] = edge_recv[c : c + 1, :] * has_before
    vec_w[...] = elements(vec_r[...])
    massx[48:51, :] = jnp.broadcast_to(edge_recv[3:4, :], (3, 256))

    wait(wall_recv.at[pl.ds(0, OWN - 1)], r_wall)
    wall = [None] * 4
    for g in range(4):
        total = jnp.zeros((4, 128), F32)
        for q in range(4):
            total = jnp.where(group == q, group_sum(wall_recv[g * 4 + q]), total)
        wall[g] = total * live_ref[g : g + 1, :]
    for g in range(4):
        hot = cell_hi[:, g * 128 : g * 128 + 128]
        parts = [hot * wall[g][c : c + 1, :] for c in range(3)]
        wallp[:, g * 128 : g * 128 + 128] = split2(jnp.concatenate(parts, axis=0))
    summed = dot_nt(wallp[...], cell_lo[...])
    summed = summed[0:96] + summed[96:192]
    wall_gain = [
        [summed[c * 32 + k * 8 : c * 32 + k * 8 + 8, :] for k in range(4)] for c in range(3)
    ]

    jobs0 = stream(0, field, wall_gain)
    collide(field)
    jobs1 = stream(1, out_pop, wall_gain)

    pop_copy = pltpu.make_async_copy(out_pop, out_pop_h, s_out)
    pop_copy.start()

    rows = [[], [], [], []]
    for k in range(4):
        rho, mom = moments([out_pop[i, k] for i in range(19)])
        for q, part in enumerate([rho] + mom):
            rows[q].append(part)
    values = jnp.concatenate([r for q in range(4) for r in rows[q]], axis=0)
    at_slots = dot_nn(split2(values), cell_lo[...])
    at_slots = at_slots[0:128] + at_slots[128:256]
    hot = cell_hi[...]
    slot = [
        jnp.sum(at_slots[q * 32 : q * 32 + 32] * hot, axis=0, keepdims=True) for q in range(4)
    ]
    row4 = iota((4, 128), 0)
    for g in range(4):
        at = slice(g * 128, g * 128 + 128)
        mom = jnp.zeros((4, 128), F32)
        for c in range(3):
            mom = jnp.where(row4 == c, slot[c + 1][:, at], mom)
        force = (mom - slot[0][:, at] * wall[g]) * live_ref[g : g + 1, :]
        for q in range(4):
            frc_send[g * 4 + q] = group_sum(jnp.where(group == q, force, 0.0))
    frc_recv[own] = frc_send[own]
    to_owners(lambda o: frc_send.at[o], frc_recv.at[own], s_frc, r_frc.at[own])
    wait(sup_recv.at[pl.ds(0, OWN - 1)], s_sup)
    wait(edge_send, s_edge)
    wait(wall_recv.at[pl.ds(0, OWN - 1)], s_wall)
    for step, jobs in enumerate((jobs0, jobs1)):
        for n, (src, dst, device) in enumerate(jobs):
            wait(src, s_halo.at[step, n])

    total = None
    for batch in batches:
        for n, step in batch:
            if n:
                o = partner(step)[1]
                wait(frc_recv.at[o], r_frc.at[o])
        for n, step in batch:
            force = frc_recv[partner(step)[1]]
            parts = []
            for c in range(3):
                line = force[c : c + 1, :]
                line = jnp.concatenate([line] * 4, axis=1)
                parts.append(sup_hi[n] * line)
            got = dot_nt(split2(jnp.concatenate(parts, axis=0)), sup_lo[n])
            total = got if total is None else total + got
    load_ref[...] = total[0:48] + total[48:96]

    row4w = iota((4, 256), 0)
    place = lax.rem(f + 4, FX)
    spot = lax.rem(place, 8)
    high = jnp.where(place < 8, HIGH_RELAYS[0], HIGH_RELAYS[1])
    low = high - 1
    is_high = (f == HIGH_RELAYS[0]) | (f == HIGH_RELAYS[1])
    is_low = (f == LOW_RELAYS[0]) | (f == LOW_RELAYS[1])
    is_double = (f == HIGH_RELAYS[1]) | is_low
    keep_after = jnp.where(is_high, has_after, 1.0)

    def exchange(app, sums, scalars):
        for c in range(3):
            for h in range(16):
                rs_send[app, h, c : c + 1, :] = sums[c * 16 + h : c * 16 + h + 1, :]
            rs_send[app, 16, c : c + 1, :] = sums[48 + c : 49 + c, :]
        top, ghost = rs_send.at[app, 15], rs_send.at[app, 16]
        send(ghost, rl_recv.at[app, 8 + spot], s_rl.at[app], r_rl.at[app], at_owner(before, high))
        send(top, rl_recv.at[app, 8 + spot], s_rl.at[app], r_rl.at[app], at_owner(after, low))
        for d in FAR_X:
            j = lax.rem(f + d, FX)

            @pl.when(j < 15)
            def _():
                send(rs_send.at[app, j], rs_recv.at[app, f], s_rs.at[app], r_rs.at[app], (j, y, z))

        @pl.when(f != high)
        def _():
            send(top, rl_recv.at[app, spot], s_rl.at[app], r_rl.at[app], (high, y, z))

        @pl.when(f != low)
        def _():
            send(ghost, rl_recv.at[app, spot], s_rl.at[app], r_rl.at[app], (low, y, z))

        if scalars is not None:
            scalars()
            to_owners(lambda o: sc_send.at[app], sc_recv.at[app, own], s_sc.at[app], r_sc.at[app])
        rs_recv[app, f] = rs_send[app, f]

        @pl.when(f < 15)
        def _():
            wait(rs_recv.at[app, pl.ds(0, FX - 1)], r_rs.at[app])
            total = rs_recv[app, 0]
            for n in range(1, FX):
                total = total + rs_recv[app, n]
            ag_send[app, 0] = total

        @pl.when(is_high | is_low)
        def _():
            rl_recv[app, spot] = rs_send[app, jnp.where(is_high, 15, 16)]
            wait(rl_recv.at[app, pl.ds(0, 15)], r_rl.at[app])
            here, there = rl_recv[app, 0], rl_recv[app, 8]
            for n in range(1, 8):
                here = here + rl_recv[app, n]
                there = there + rl_recv[app, 8 + n]
            ag_send[app, 1] = here + keep_after * there

        @pl.when(f == 15)
        def _():
            ag_send[app, 0] = ag_send[app, 1]

        if scalars is not None:
            wait(sc_recv.at[app, pl.ds(0, OWN - 1)], r_sc.at[app])
            part = sc_recv[app, 0]
            for n in range(1, OWN):
                part = part + sc_recv[app, n]
            ag_send[app, 0] = jnp.where(
                row4w == 3, part, ag_send[app, 0]
            )
        @pl.when(is_double)
        def _():
            for d in FAR_X:
                send(
                    ag_send.at[app], ag_recv.at[app, pl.ds(2 * f, 2)], s_ag.at[app], r_ag.at[app],
                    (lax.rem(f + d, FX), y, z),
                )
            ag_recv[app, 2 * f + 1] = ag_send[app, 1]

        @pl.when(jnp.logical_not(is_double))
        def _():
            for d in FAR_X:
                send(
                    ag_send.at[app, 0], ag_recv.at[app, 2 * f], s_ag.at[app], r_ag.at[app],
                    (lax.rem(f + d, FX), y, z),
                )

        ag_recv[app, 2 * f] = ag_send[app, 0]

        wait(rs_recv.at[app, pl.ds(0, 14)], s_rs.at[app])
        wait(rs_recv.at[app, pl.ds(0, 3)], s_rl.at[app])
        if scalars is not None:
            wait(sc_recv.at[app, pl.ds(0, OWN - 1)], s_sc.at[app])

        @pl.when(f == 15)
        def _():
            wait(rs_recv.at[app, 0], s_rs.at[app])

        @pl.when(jnp.logical_not(is_high | is_low))
        def _():
            wait(rs_recv.at[app, 0], s_rl.at[app])

        @pl.when(is_double)
        def _():
            wait(ag_recv.at[app, pl.ds(0, 17)], r_ag.at[app])

        @pl.when(jnp.logical_not(is_double))
        def _():
            wait(ag_recv.at[app, pl.ds(0, 18)], r_ag.at[app])

    def gathered(app, target):
        for c in range(3):
            for h in range(15):
                target[c * 16 + h : c * 16 + h + 1, :] = ag_recv[app, 2 * h, c : c + 1, :]
            target[c * 16 + 15 : c * 16 + 16, :] = (
                ag_recv[app, 2 * HIGH_RELAYS[0], c : c + 1, :]
                + ag_recv[app, 2 * HIGH_RELAYS[1] + 1, c : c + 1, :]
            )
            target[48 + c : 49 + c, :] = has_before * (
                ag_recv[app, 2 * LOW_RELAYS[0] + 1, c : c + 1, :]
                + ag_recv[app, 2 * LOW_RELAYS[1] + 1, c : c + 1, :]
            )

    kdisp = vec_w[...]
    loads = jnp.concatenate([FORCE_SCALE * load_ref[...], jnp.zeros((16, 256), F32)], axis=0)
    exchange(0, loads - kdisp, None)
    gathered(0, vec_r)
    wait(frc_recv.at[pl.ds(0, OWN - 1)], s_frc)
    pop_copy.wait()
    vec_p[...] = jnp.zeros((64, 256), F32)
    vec_s[...] = jnp.zeros((64, 256), F32)
    vec_w[...] = jnp.zeros((64, 256), F32)

    def iteration(app, carry):
        alpha, gamma = carry
        for c in range(3):
            rc[c : c + 1, :] = vec_r[pl.ds(c * 16 + f, 1), :]
        rc[3:4, :] = jnp.zeros((1, 256), F32)
        chunk = rc[...]
        mine = jnp.sum(chunk * chunk, keepdims=True)
        held = jnp.sum(massx[pl.ds(f, 1), :] * chunk * chunk, keepdims=True)

        def tell():
            energy = held + jnp.sum(pick[...] * spread[...], keepdims=True)
            scalars = jnp.where(iota((1, 256), 1) < 128, mine, energy)
            sc_send[app] = scalars
            sc_recv[app, own] = scalars

        exchange(app, elements(vec_r[...]), tell)
        gathered(app, vec_w)
        both = ag_recv[app, 0]
        for n in range(1, FX):
            both = both + ag_recv[app, 2 * n]
        new = both[3:4, 0:128]
        delta = both[3:4, 128:256]
        beta = jnp.where(app == 1, 0.0, new / gamma)
        alpha = new / (delta - beta * new / alpha)
        beta2 = jnp.concatenate([beta, beta], axis=1)
        alpha2 = jnp.concatenate([alpha, alpha], axis=1)
        p = vec_r[...] + beta2 * vec_p[...]
        s = vec_w[...] + massx[...] * vec_r[...] + beta2 * vec_s[...]
        vec_p[...] = p
        vec_s[...] = s
        vec_r[...] = vec_r[...] - alpha2 * s
        vec_x[...] += alpha2 * p[0:48]
        return alpha, new

    one = jnp.ones((1, 128), F32)
    lax.fori_loop(1, APPS, iteration, (one, one))

    for c in range(3):
        for h in range(16):
            at = slice(h * 256, h * 256 + 256)
            out_sol[c : c + 1, at] = vec_x[c * 16 + h : c * 16 + h + 1, :]
            out_res[c : c + 1, at] = vec_r[c * 16 + h : c * 16 + h + 1, :]

    for app in range(APPS):
        wait(ag_recv.at[app, pl.ds(0, FX - 1)], s_ag.at[app])

        @pl.when(is_double)
        def _():
            wait(ag_recv.at[app, pl.ds(0, FX - 1)], s_ag.at[app])


SCRATCH = dict(
    pop=(19, 4, 8, 256), relax=(4, 8, 256), vel=(3, 4096), count=((1, 16), I32),
    cell=((16, 32), I32), node=((16, 16, 32), I32), weight=(16, 16, 32), disp=(3, 4096),
    mass=(32, 128), connect=((8, 512), I32), modulus=(1, 512), basis=(24, 24),
    sup_send=(16, 8, 128), sup_recv=(16, 8, 128),
    wall_send=(16, 4, 128), wall_recv=(16, 4, 128),
    frc_send=(16, 4, 128), frc_recv=(16, 4, 128),
    edge_send=(4, 256), edge_recv=(4, 256),
    xs=(2, 2, 5, 8, 256), xr=(2, 2, 5, 8, 256),
    ys=(2, 2, 5, 4, 256), yr=(2, 2, 5, 4, 256),
    ds=(2, 4, 1, 256), dr=(2, 4, 1, 256),
    zs=(2, 4, 8, 128), zr=(2, 4, 8, 128), zxr=(2, 2, 8, 128),
    zys=(2, 2, 4, 128), zyr=(2, 2, 4, 128),
    rs_send=(APPS, 17, 4, 256), rs_recv=(APPS, 16, 4, 256), rl_recv=(APPS, 16, 4, 256),
    sc_send=(APPS, 1, 256), sc_recv=(APPS, 16, 1, 256),
    ag_send=(APPS, 2, 4, 256), ag_recv=(APPS, 32, 4, 256),
    post=(19, 4, 8, 256), field=(19, 4, 8, 256), rho_ref=(4, 8, 256), gain=(3, 4, 8, 256),
    cell_lo=((256, 512), BF16), cell_hi=(32, 512), live_ref=(8, 128), wallp=((192, 512), BF16),
    sup_lo=((16, 256, 512), BF16), sup_hi=(16, 16, 512),
    el_lo=((8, 256, 512), BF16), el_hi=(8, 16, 512), el_gh=(8, 512),
    pick=(24, 512), spread=(24, 512),
    vec_r=(64, 256), vec_p=(64, 256), vec_s=(64, 256), vec_w=(64, 256), vec_x=(48, 256),
    massx=(64, 256), rc=(4, 256), load_ref=(48, 256), out_pop=(19, 4, 8, 256),
)


def scratch_shapes():
    shapes = []
    for shape in SCRATCH.values():
        kind = F32
        if isinstance(shape[0], tuple):
            shape, kind = shape
        shapes.append(pltpu.VMEM(shape, kind))
    dma = pltpu.SemaphoreType.DMA
    shapes += [dma((INPUTS,)), dma]
    shapes += [dma, dma((OWN,)), dma, dma, dma, dma((OWN,)), dma, dma]
    shapes += [dma((2, 13))] * 2 + [dma((APPS,))] * 8
    return shapes


def deliver(pop_h, sol_h, res_h, pop_out, sol_out, res_out, pop, sol, res, s_in, s_out):
    jobs = [(pop_h.at[pl.ds(n, 4)], pop.at[pl.ds(n, 4)], pop_out.at[pl.ds(n, 4)]) for n in (0, 4, 8, 12)]
    jobs.append((pop_h.at[pl.ds(16, 3)], pop.at[pl.ds(16, 3)], pop_out.at[pl.ds(16, 3)]))
    jobs += [(sol_h, sol, sol_out), (res_h, res, res_out)]
    copies = []
    for n, (a, b, c) in enumerate(jobs):
        copies.append(
            (pltpu.make_async_copy(a, b, s_in.at[n]), pltpu.make_async_copy(b, c, s_out.at[n]))
        )
        copies[n][0].start()
    for came, goes in copies:
        came.wait()
        goes.start()
    for came, goes in copies:
        goes.wait()


def body(
    populations, relaxation, struct_velocity, iface_count, iface_cell, rbf_node, rbf_weight,
    disp_prev, node_mass, connect, modulus, strain_basis,
):
    vmem = pl.BlockSpec(memory_space=pltpu.VMEM)
    hbm = pl.BlockSpec(memory_space=pl.ANY)
    shapes = (
        jax.ShapeDtypeStruct(populations.shape, F32),
        jax.ShapeDtypeStruct(disp_prev.shape, F32),
        jax.ShapeDtypeStruct(disp_prev.shape, F32),
    )
    results = pl.pallas_call(
        kernel,
        out_shape=shapes,
        in_specs=[hbm] * INPUTS,
        out_specs=(hbm, vmem, vmem),
        scratch_shapes=scratch_shapes(),
        compiler_params=pltpu.CompilerParams(
            collective_id=0, has_side_effects=True, vmem_limit_bytes=62 * 1024 * 1024
        ),
        name="window",
    )(
        populations,
        relaxation,
        struct_velocity,
        iface_count.reshape(1, 16),
        iface_cell.reshape(16, 32),
        rbf_node.reshape(16, 16, 32),
        rbf_weight.reshape(16, 16, 32),
        disp_prev,
        node_mass.reshape(32, 128),
        connect.reshape(8, 512),
        modulus.reshape(1, 512),
        strain_basis,
    )
    return pl.pallas_call(
        deliver,
        out_shape=shapes,
        in_specs=[hbm] * 3,
        out_specs=(hbm, hbm, hbm),
        scratch_shapes=[pltpu.VMEM(s.shape, F32) for s in shapes]
        + [pltpu.SemaphoreType.DMA((7,))] * 2,
        compiler_params=pltpu.CompilerParams(vmem_limit_bytes=62 * 1024 * 1024),
        name="deliver",
    )(*results)


def solution(mesh):
    return jax.shard_map(
        body,
        mesh=mesh,
        in_specs=(
            P(None, "fx", "fy", "sz"),
            P("fx", "fy", "sz"),
            P(None, ("fy", "sz")),
            P("fx", "fy", "sz", None),
            P("fx", "fy", "sz", None, None),
            P("fx", "fy", "sz", None, None, None),
            P("fx", "fy", "sz", None, None, None),
            P(None, ("fy", "sz")),
            P(("fy", "sz")),
            P("fx", ("fy", "sz"), None, None),
            P("fx", ("fy", "sz"), None),
            P(),
        ),
        out_specs=(P(None, "fx", "fy", "sz"), P(None, ("fy", "sz")), P(None, ("fy", "sz"))),
        check_vma=False,
    )
```

```python
import jax
import jax.numpy as jnp
from jax import lax
from jax.experimental import pallas as pl
from jax.experimental.pallas import tpu as pltpu
from jax.sharding import PartitionSpec as P

F32 = jnp.float32
BF16 = jnp.bfloat16
I32 = jnp.int32
FX, FY, SZ = 16, 8, 2
OWN = 16
ITERS = 3
APPS = ITERS + 1
FORCE_SCALE = 20.0
VEL = [
    (0, 0, 0),
    (1, 0, 0),
    (-1, 0, 0),
    (0, 1, 0),
    (0, -1, 0),
    (0, 0, 1),
    (0, 0, -1),
    (1, 1, 0),
    (-1, -1, 0),
    (1, -1, 0),
    (-1, 1, 0),
    (1, 0, 1),
    (-1, 0, -1),
    (1, 0, -1),
    (-1, 0, 1),
    (0, 1, 1),
    (0, -1, -1),
    (0, 1, -1),
    (0, -1, 1),
]
X_POPS = [[i for i in range(19) if VEL[i][0] == s] for s in (1, -1)]
Y_POPS = [[i for i in range(19) if VEL[i][1] == s] for s in (1, -1)]
Z_POPS = [i for i in range(19) if VEL[i][2] != 0]
DIAGONAL = (7, 8, 9, 10)
MESH = pl.DeviceIdType.MESH
FAR_X = (8, 7, 9, 6, 10, 5, 11, 4, 12, 3, 13, 2, 14, 1, 15)
FAR_OWN = (
    (4, 1), (2, 1), (6, 1), (3, 1), (5, 1), (3, 0), (5, 0), (4, 0),
    (1, 1), (7, 1), (0, 1), (1, 0), (7, 0), (2, 0), (6, 0),
)
HIGH_RELAYS = (15, 7)
LOW_RELAYS = (14, 6)
INPUTS = 12
NEAR = 10


def split2(x):
    top = x.astype(BF16)
    rest = (x - top.astype(F32)).astype(BF16)
    return jnp.concatenate([top, rest], axis=0)


def dot_nt(a, b):
    return lax.dot_general(a, b, (((1,), (1,)), ((), ())), preferred_element_type=F32)


def dot_nn(a, b):
    return lax.dot_general(a, b, (((1,), (0,)), ((), ())), preferred_element_type=F32)


def exact_dot(a, b, dims=((1,), (0,))):
    return lax.dot_general(
        a, b, (dims, ((), ())), preferred_element_type=F32, precision=lax.Precision.HIGHEST
    )


def iota(shape, dim):
    return lax.broadcasted_iota(I32, shape, dim)


def group_sum(x):
    x = x + pltpu.roll(x, 64, x.ndim - 1)
    return x + pltpu.roll(x, 32, x.ndim - 1)


def send(src, dst, ssem, rsem, device):
    pltpu.make_async_remote_copy(
        src_ref=src,
        dst_ref=dst,
        send_sem=ssem,
        recv_sem=rsem,
        device_id=device,
        device_id_type=MESH,
    ).start()


def greet(f, y, z, own):
    sem = pltpu.get_barrier_semaphore()

    def tell(device):
        pl.semaphore_signal(sem, inc=1, device_id=device, device_id_type=MESH)

    for d in FAR_X:
        tell((lax.rem(f + d, FX), y, z))
    for dy, dz in FAR_OWN:
        tell((f, lax.rem(y + dy, FY), lax.rem(z + dz, SZ)))
    return sem


def wait(ref, sem):
    pltpu.make_async_copy(ref, ref, sem).wait()


def kernel(
    pop_h, relax_h, vel_h, count_h, cell_h, node_h, weight_h, disp_h, mass_h, connect_h,
    modulus_h, basis_h,
    out_pop_h, out_sol, out_res,
    pop, relax, vel, count, cell, node, weight, disp, mass, connect, modulus, basis,
    sup_send, sup_recv, wall_send, wall_recv, frc_send, frc_recv, edge_send, edge_recv,
    xs, xr, ys, yr, ds, dr, zs, zr, zxr, zys, zyr,
    rs_send, rs_recv, rl_recv, sc_send, sc_recv, ag_send, ag_recv,
    post, field, rho_ref, gain, cell_lo, cell_hi, live_ref, wallp,
    sup_lo, sup_hi, el_lo, el_hi, el_gh, pick, spread, vec_r, vec_p, vec_s, vec_w, vec_x,
    massx, rc, load_ref, out_pop, s_in, s_out,
    s_sup, r_sup, s_wall, r_wall, s_frc, r_frc, s_edge, r_edge, s_halo, r_halo,
    s_rs, r_rs, s_rl, r_rl, s_sc, r_sc, s_ag, r_ag,
):
    f = lax.axis_index("fx")
    y = lax.axis_index("fy")
    z = lax.axis_index("sz")
    own = y * SZ + z

    def at_owner(o, fx=None):
        return (f if fx is None else fx, o // SZ, lax.rem(o, SZ))

    def to_owners(src_of, dst, ssem, rsem):
        for dy, dz in FAR_OWN:
            there = (f, lax.rem(y + dy, FY), lax.rem(z + dz, SZ))
            send(src_of(there[1] * SZ + there[2]), dst, ssem, rsem, there)

    inputs = [
        (node_h, node), (weight_h, weight), (disp_h, disp), (mass_h, mass), (connect_h, connect),
        (basis_h, basis), (cell_h, cell), (count_h, count), (pop_h, pop), (relax_h, relax),
        (vel_h, vel), (modulus_h, modulus),
    ]
    copies = [pltpu.make_async_copy(a, b, s_in.at[n]) for n, (a, b) in enumerate(inputs)]
    for copy in copies[:2]:
        copy.start()
    barrier = greet(f, y, z, own)
    for copy in copies[2:]:
        copy.start()

    lane = iota((1, 128), 1)
    group = lane // 32
    expand = (iota((32, 128), 0) == lax.rem(iota((32, 128), 1), 32)).astype(F32)
    quarter = (lax.rem(iota((256, 128), 0), 16) // 4) == (iota((256, 128), 1) // 32)
    upper = iota((8, 128), 0) < 4
    copies[0].wait()
    copies[1].wait()
    spread_n = exact_dot(node[...].astype(F32).reshape(256, 32), expand)
    spread_w = exact_dot(weight[...].reshape(256, 32), expand)
    spread_n = jnp.where(quarter, spread_n, 0.0)
    spread_w = jnp.where(quarter, spread_w, 0.0)

    def packed(x, o):
        x = x[o * 16 : o * 16 + 8] + x[o * 16 + 8 : o * 16 + 16]
        return x + pltpu.roll(x, 4, 0)

    for o in range(OWN):
        sup_send[o] = jnp.where(upper, packed(spread_n, o), packed(spread_w, o))
    sup_recv[own] = sup_send[own]
    pl.semaphore_wait(barrier, 15 + 15)
    to_owners(lambda o: sup_send.at[o], sup_recv.at[own], s_sup, r_sup.at[own])

    copies[2].wait()
    copies[3].wait()
    for c in range(3):
        edge_send[c : c + 1, :] = disp[c : c + 1, 3840:4096]
    massx[...] = jnp.zeros((64, 256), F32)
    for h in range(16):
        massx[h : h + 1, 0:128] = mass[2 * h : 2 * h + 1, :]
        massx[h : h + 1, 128:256] = mass[2 * h + 1 : 2 * h + 2, :]
    massx[16:32, :] = massx[0:16, :]
    massx[32:48, :] = massx[0:16, :]
    edge_send[3:4, :] = massx[15:16, :]
    after, before = lax.rem(own + 1, OWN), lax.rem(own + OWN - 1, OWN)
    send(edge_send, edge_recv, s_edge, r_edge, at_owner(after))

    copies[4].wait()
    copies[5].wait()
    for j in range(8):
        n = connect[j : j + 1, :]
        lo = lax.rem(n, 256)
        hi = n // 256 - 1
        el_lo[j] = jnp.where(iota((256, 512), 0) == lo, 1.0, 0.0).astype(BF16)
        el_hi[j] = jnp.where(iota((16, 512), 0) == hi, 1.0, 0.0)
        el_gh[j : j + 1, :] = jnp.where(n < 256, 1.0, 0.0)
    base = basis[...]
    gram = exact_dot(base, base, ((0,), (0,)))
    thrice = lax.rem(iota((24, 96), 1), 32) == iota((24, 96), 0)
    gram = exact_dot(gram, thrice.astype(F32))
    gram_top = gram.astype(BF16).astype(F32)
    gram = jnp.where(iota((24, 96), 1) < 64, gram_top, gram - gram_top).astype(BF16)

    copies[6].wait()
    copies[7].wait()
    cells = cell[...]
    cell_hi16 = exact_dot((cells // 256).astype(F32), expand)
    cell_lo16 = exact_dot(lax.rem(cells, 256).astype(F32), expand)
    diag = iota((16, 16), 0) == iota((16, 16), 1)
    counts = jnp.sum(jnp.where(diag, count[...].astype(F32), 0.0), axis=1, keepdims=True)
    live16 = (lax.rem(iota((16, 128), 1), 32).astype(F32) < counts).astype(F32)
    mine = lax.rem(iota((16, 128), 0), 4) == (iota((16, 128), 1) // 32)
    fold = ((iota((8, 16), 1) // 4) == iota((8, 16), 0)).astype(F32)

    def rows_of(x):
        return exact_dot(fold, jnp.where(mine, x, 0.0))

    hi_rows, lo_rows = rows_of(cell_hi16).astype(I32), rows_of(cell_lo16).astype(I32)
    live_ref[...] = rows_of(live16)
    for g in range(4):
        at = slice(g * 128, g * 128 + 128)
        cell_lo[:, at] = jnp.where(iota((256, 128), 0) == lo_rows[g : g + 1], 1.0, 0.0).astype(BF16)
        cell_hi[:, at] = jnp.where(iota((32, 128), 0) == hi_rows[g : g + 1], 1.0, 0.0)

    def moments(fs):
        rho = fs[0]
        for i in range(1, 19):
            rho = rho + fs[i]
        mom = []
        for a in range(3):
            total = None
            for i in range(1, 19, 2):
                s = VEL[i][a]
                if s:
                    pair = fs[i] - fs[i + 1] if s > 0 else fs[i + 1] - fs[i]
                    total = pair if total is None else total + pair
            mom.append(total)
        return rho, mom

    def along(c, v):
        total = None
        for a in range(3):
            if c[a] == 1:
                total = v[a] if total is None else total + v[a]
        for a in range(3):
            if c[a] == -1:
                total = -v[a] if total is None else total - v[a]
        return total

    def collide(source):
        for k in range(4):
            fs = [source[i, k] for i in range(19)]
            om = relax[k]
            rho, mom = moments(fs)
            inv = 1.0 / rho
            u = [m * inv for m in mom]
            sq = 1.5 * (u[0] * u[0] + u[1] * u[1] + u[2] * u[2])
            rho_ref[k] = rho
            keep = 1.0 - om
            scaled = om * rho
            post[0, k] = keep * fs[0] + (1.0 / 3.0) * scaled * (1.0 - sq)
            for i in range(1, 19, 2):
                t = (1.0 / 18.0) if i < 7 else (1.0 / 36.0)
                a = along(VEL[i], u)
                ts = t * scaled
                even = ts * (1.0 + 4.5 * a * a - sq)
                odd = ts * (3.0 * a)
                post[i, k] = keep * fs[i] + (even + odd)
                post[i + 1, k] = keep * fs[i + 1] + (even - odd)

    def turn(i, v):
        cy, cz = VEL[i][1], VEL[i][2]
        if cy:
            v = pltpu.roll(v, cy % 8, 0)
        if cz:
            v = pltpu.roll(v, cz % 256, 1)
        return v

    lane8 = iota((8, 128), 1)
    row8 = iota((8, 128), 0)

    def stream(step, target, wall_gain):
        for k in range(4):
            for c in range(3):
                gain[c, k] = wall_gain[c][k] * rho_ref[k] * (1.0 / 6.0)
        xp, xm = lax.rem(f + 1, FX), lax.rem(f + FX - 1, FX)
        yp, ym = lax.rem(y + 1, FY), lax.rem(y + FY - 1, FY)
        zo = 1 - z
        jobs = {
            "x0": (xs.at[step, 0], xr.at[step, 0], (xp, y, z)),
            "x1": (xs.at[step, 1], xr.at[step, 1], (xm, y, z)),
            "y0": (ys.at[step, 0], yr.at[step, 0], (f, yp, z)),
            "y1": (ys.at[step, 1], yr.at[step, 1], (f, ym, z)),
            "d0": (ds.at[step, 0], dr.at[step, 0], (xp, yp, z)),
            "d1": (ds.at[step, 1], dr.at[step, 1], (xm, ym, z)),
            "d2": (ds.at[step, 2], dr.at[step, 2], (xp, ym, z)),
            "d3": (ds.at[step, 3], dr.at[step, 3], (xm, yp, z)),
            "zx0": (zs.at[step, 0], zxr.at[step, 0], (xp, y, zo)),
            "zx1": (zs.at[step, 3], zxr.at[step, 1], (xm, y, zo)),
            "zy0": (zys.at[step, 0], zyr.at[step, 0], (f, yp, zo)),
            "zy1": (zys.at[step, 1], zyr.at[step, 1], (f, ym, zo)),
            "z": (zs.at[step], zr.at[step], (f, y, zo)),
        }
        index = {name: n for n, name in enumerate(jobs)}

        def go(*names):
            for name in names:
                src, dst, device = jobs[name]
                n = index[name]
                send(src, dst, s_halo.at[step, n], r_halo.at[step, n], device)

        def came(*names):
            for name in names:
                wait(jobs[name][1], r_halo.at[step, index[name]])

        for x in (0, 3, 1, 2):
            zpack = jnp.zeros((8, 128), F32)
            for i in range(19):
                cx, cy, cz = VEL[i]
                k = (x - cx) % 4
                v = post[i, k]
                if i:
                    push = along(VEL[i], [gain[c, k] for c in range(3)])
                    v = v + (2.0 * push if i < 7 else push)
                v = turn(i, v)
                if k != x - cx:
                    side = 0 if cx > 0 else 1
                    xs[step, side, X_POPS[side].index(i)] = v
                    if cy:
                        r = 0 if cy > 0 else 7
                        ds[step, DIAGONAL.index(i)] = v[r : r + 1, :]
                else:
                    target[i, x] = v
                if cy:
                    side = 0 if cy > 0 else 1
                    r = 0 if cy > 0 else 7
                    ys[step, side, Y_POPS[side].index(i), x : x + 1, :] = v[r : r + 1, :]
                if cz:
                    col = v[:, 0:1] if cz > 0 else v[:, 255:256]
                    zpack = jnp.where(lane8 == Z_POPS.index(i), col, zpack)
            zs[step, x] = zpack
            zys[step, 0, x : x + 1, :] = zpack[0:1, :]
            zys[step, 1, x : x + 1, :] = zpack[7:8, :]
            if x == 0:
                go("zx0", "d0", "d2", "x0")
            if x == 3:
                go("zx1", "d1", "d3", "x1")
        go("zy0", "zy1", "z", "y0", "y1")
        came("x0", "x1")
        for side in range(2):
            for n, i in enumerate(X_POPS[side]):
                target[i, 0 if side == 0 else 3] = xr[step, side, n]
        came("y0", "y1")
        for side in range(2):
            r = 0 if side == 0 else 7
            for n, i in enumerate(Y_POPS[side]):
                cx = VEL[i][0]
                for x in range(4):
                    if 0 <= x - cx <= 3:
                        target[i, x, r : r + 1, :] = yr[step, side, n, x : x + 1, :]
        came("d0", "d1", "d2", "d3")
        for n, i in enumerate(DIAGONAL):
            cx, cy, _ = VEL[i]
            r = 0 if cy > 0 else 7
            target[i, 0 if cx > 0 else 3, r : r + 1, :] = dr[step, n]
        came("z", "zx0", "zx1", "zy0", "zy1")
        z11, z12, z13, z14, z15, z16, z17, z18 = [Z_POPS.index(i) for i in range(11, 19)]
        for x in range(4):
            zin = zr[step, x]
            if x == 0:
                zin = jnp.where((lane8 == z11) | (lane8 == z13), zxr[step, 0], zin)
            if x == 3:
                zin = jnp.where((lane8 == z12) | (lane8 == z14), zxr[step, 1], zin)
            low = (row8 == 0) & ((lane8 == z15) | (lane8 == z17))
            high = (row8 == 7) & ((lane8 == z16) | (lane8 == z18))
            zin = jnp.where(low, zyr[step, 0, x : x + 1, :], zin)
            zin = jnp.where(high, zyr[step, 1, x : x + 1, :], zin)
            for n, i in enumerate(Z_POPS):
                col = zin[:, n : n + 1]
                if VEL[i][2] > 0:
                    target[i, x, :, 0:128] = jnp.where(lane8 == 0, col, target[i, x, :, 0:128])
                else:
                    target[i, x, :, 128:256] = jnp.where(
                        lane8 == 127, col, target[i, x, :, 128:256]
                    )
        return list(jobs.values())

    copies[8].wait()
    copies[9].wait()
    collide(pop)

    copies[10].wait()
    copies[11].wait()
    for c in range(3):
        for h in range(16):
            load_ref[c * 16 + h : c * 16 + h + 1, :] = vel[c : c + 1, h * 256 : h * 256 + 256]
    table = split2(load_ref[...])
    steps = [(0, 0)] + list(reversed(FAR_OWN))
    batches = [list(enumerate(steps))[:NEAR], list(enumerate(steps))[NEAR:]]

    def partner(step):
        there = (f, lax.rem(y + step[0], FY), lax.rem(z + step[1], SZ))
        return there, there[1] * SZ + there[2]

    for batch in batches:
        for n, step in batch:
            if n:
                o = partner(step)[1]
                wait(sup_recv.at[o], r_sup.at[o])
        for n, step in batch:
            there, o = partner(step)
            tile = sup_recv[o]
            for r in range(4):
                node_row = tile[r : r + 1].astype(I32)
                sup_lo[n, :, r * 128 : r * 128 + 128] = jnp.where(
                    iota((256, 128), 0) == lax.rem(node_row, 256), 1.0, 0.0
                ).astype(BF16)
                sup_hi[n, :, r * 128 : r * 128 + 128] = jnp.where(
                    iota((16, 128), 0) == node_row // 256, tile[r + 4 : r + 5], 0.0
                )
        for n, step in batch:
            there, o = partner(step)
            out = dot_nn(table, sup_lo[n])
            out = out[0:48] + out[48:96]
            hot = sup_hi[n]
            for c in range(3):
                m = out[c * 16 : c * 16 + 16] * hot
                m = m[:, 0:128] + m[:, 128:256] + m[:, 256:384] + m[:, 384:512]
                wall_send[n, c : c + 1, :] = jnp.sum(m, axis=0, keepdims=True)
            wall_send[n, 3:4, :] = jnp.zeros((1, 128), F32)
        for n, step in reversed(batch):
            there, o = partner(step)
            if n:
                send(wall_send.at[n], wall_recv.at[own], s_wall, r_wall, there)
            else:
                wall_recv[own] = wall_send[0]

    def elements(values):
        both = split2(values)

        for j in range(8):
            out = dot_nn(both, el_lo[j])
            out = out[0:64] + out[64:128]
            hot, ghost = el_hi[j], el_gh[j : j + 1, :]
            for c in range(3):
                found = jnp.sum(out[c * 16 : c * 16 + 16] * hot, axis=0, keepdims=True)
                pick[c * 8 + j : c * 8 + j + 1, :] = found + out[48 + c : 49 + c] * ghost
        picked = pick[...]
        wide = jnp.concatenate([picked, jnp.zeros((8, 512), F32)], axis=0)
        top = wide.astype(BF16)
        rest = (wide - top.astype(F32)).astype(BF16)
        spread[...] = dot_nn(gram, jnp.concatenate([top, rest, top], axis=0)) * modulus[...]
        total = None
        for j in range(8):
            hot, ghost = el_hi[j], el_gh[j : j + 1, :]
            rows = [spread[c * 8 + j : c * 8 + j + 1, :] for c in range(3)]
            last = jnp.zeros((8, 512), F32)
            for c in range(3):
                last = jnp.where(iota((8, 512), 0) == c, rows[c] * ghost, last)
            parts = [hot * row for row in rows] + [last, jnp.zeros((8, 512), F32)]
            part = dot_nt(split2(jnp.concatenate(parts, axis=0)), el_lo[j])
            total = part if total is None else total + part
        return total[0:64] + total[64:128]

    wait(edge_recv, r_edge)
    vec_r[...] = jnp.zeros((64, 256), F32)
    has_before = (own > 0).astype(F32)
    has_after = (own < OWN - 1).astype(F32)
    for c in range(3):
        for h in range(16):
            row = disp[c : c + 1, h * 256 : h * 256 + 256]
            vec_r[c * 16 + h : c * 16 + h + 1, :] = row
            vec_x[c * 16 + h : c * 16 + h + 1, :] = row
        vec_r[48 + c : 49 + c, :] = edge_recv[c : c + 1, :] * has_before
    vec_w[...] = elements(vec_r[...])
    massx[48:51, :] = jnp.broadcast_to(edge_recv[3:4, :], (3, 256))

    wait(wall_recv.at[pl.ds(0, OWN - 1)], r_wall)
    wall = [None] * 4
    for g in range(4):
        total = jnp.zeros((4, 128), F32)
        for q in range(4):
            total = jnp.where(group == q, group_sum(wall_recv[g * 4 + q]), total)
        wall[g] = total * live_ref[g : g + 1, :]
    for g in range(4):
        hot = cell_hi[:, g * 128 : g * 128 + 128]
        parts = [hot * wall[g][c : c + 1, :] for c in range(3)]
        wallp[:, g * 128 : g * 128 + 128] = split2(jnp.concatenate(parts, axis=0))
    summed = dot_nt(wallp[...], cell_lo[...])
    summed = summed[0:96] + summed[96:192]
    wall_gain = [
        [summed[c * 32 + k * 8 : c * 32 + k * 8 + 8, :] for k in range(4)] for c in range(3)
    ]

    jobs0 = stream(0, field, wall_gain)
    collide(field)
    jobs1 = stream(1, out_pop, wall_gain)

    pop_copy = pltpu.make_async_copy(out_pop, out_pop_h, s_out)
    pop_copy.start()

    rows = [[], [], [], []]
    for k in range(4):
        rho, mom = moments([out_pop[i, k] for i in range(19)])
        for q, part in enumerate([rho] + mom):
            rows[q].append(part)
    values = jnp.concatenate([r for q in range(4) for r in rows[q]], axis=0)
    at_slots = dot_nn(split2(values), cell_lo[...])
    at_slots = at_slots[0:128] + at_slots[128:256]
    hot = cell_hi[...]
    slot = [
        jnp.sum(at_slots[q * 32 : q * 32 + 32] * hot, axis=0, keepdims=True) for q in range(4)
    ]
    row4 = iota((4, 128), 0)
    for g in range(4):
        at = slice(g * 128, g * 128 + 128)
        mom = jnp.zeros((4, 128), F32)
        for c in range(3):
            mom = jnp.where(row4 == c, slot[c + 1][:, at], mom)
        force = (mom - slot[0][:, at] * wall[g]) * live_ref[g : g + 1, :]
        for q in range(4):
            frc_send[g * 4 + q] = group_sum(jnp.where(group == q, force, 0.0))
    frc_recv[own] = frc_send[own]
    to_owners(lambda o: frc_send.at[o], frc_recv.at[own], s_frc, r_frc.at[own])
    wait(sup_recv.at[pl.ds(0, OWN - 1)], s_sup)
    wait(edge_send, s_edge)
    wait(wall_recv.at[pl.ds(0, OWN - 1)], s_wall)
    for step, jobs in enumerate((jobs0, jobs1)):
        for n, (src, dst, device) in enumerate(jobs):
            wait(src, s_halo.at[step, n])

    total = None
    for batch in batches:
        for n, step in batch:
            if n:
                o = partner(step)[1]
                wait(frc_recv.at[o], r_frc.at[o])
        for n, step in batch:
            force = frc_recv[partner(step)[1]]
            parts = []
            for c in range(3):
                line = force[c : c + 1, :]
                line = jnp.concatenate([line] * 4, axis=1)
                parts.append(sup_hi[n] * line)
            got = dot_nt(split2(jnp.concatenate(parts, axis=0)), sup_lo[n])
            total = got if total is None else total + got
    load_ref[...] = total[0:48] + total[48:96]

    row4w = iota((4, 256), 0)
    place = lax.rem(f + 4, FX)
    spot = lax.rem(place, 8)
    high = jnp.where(place < 8, HIGH_RELAYS[0], HIGH_RELAYS[1])
    low = high - 1
    is_high = (f == HIGH_RELAYS[0]) | (f == HIGH_RELAYS[1])
    is_low = (f == LOW_RELAYS[0]) | (f == LOW_RELAYS[1])
    is_double = (f == HIGH_RELAYS[1]) | is_low
    keep_after = jnp.where(is_high, has_after, 1.0)

    def exchange(app, sums, scalars):
        if scalars is not None:
            scalars()
        for c in range(3):
            for h in range(16):
                rs_send[app, h, c : c + 1, :] = sums[c * 16 + h : c * 16 + h + 1, :]
            rs_send[app, 16, c : c + 1, :] = sums[48 + c : 49 + c, :]
        top, ghost = rs_send.at[app, 15], rs_send.at[app, 16]
        send(ghost, rl_recv.at[app, 8 + spot], s_rl.at[app], r_rl.at[app], at_owner(before, high))
        send(top, rl_recv.at[app, 8 + spot], s_rl.at[app], r_rl.at[app], at_owner(after, low))
        for d in FAR_X:
            j = lax.rem(f + d, FX)

            @pl.when(j < 15)
            def _():
                send(rs_send.at[app, j], rs_recv.at[app, f], s_rs.at[app], r_rs.at[app], (j, y, z))

        @pl.when(f != high)
        def _():
            send(top, rl_recv.at[app, spot], s_rl.at[app], r_rl.at[app], (high, y, z))

        @pl.when(f != low)
        def _():
            send(ghost, rl_recv.at[app, spot], s_rl.at[app], r_rl.at[app], (low, y, z))

        if scalars is not None:
            to_owners(lambda o: sc_send.at[app], sc_recv.at[app, own], s_sc.at[app], r_sc.at[app])
        rs_recv[app, f] = rs_send[app, f]

        @pl.when(f < 15)
        def _():
            wait(rs_recv.at[app, pl.ds(0, FX - 1)], r_rs.at[app])
            total = rs_recv[app, 0]
            for n in range(1, FX):
                total = total + rs_recv[app, n]
            ag_send[app, 0] = total

        @pl.when(is_high | is_low)
        def _():
            rl_recv[app, spot] = rs_send[app, jnp.where(is_high, 15, 16)]
            wait(rl_recv.at[app, pl.ds(0, 15)], r_rl.at[app])
            here, there = rl_recv[app, 0], rl_recv[app, 8]
            for n in range(1, 8):
                here = here + rl_recv[app, n]
                there = there + rl_recv[app, 8 + n]
            ag_send[app, 1] = here + keep_after * there

        @pl.when(f == 15)
        def _():
            ag_send[app, 0] = ag_send[app, 1]

        if scalars is not None:
            wait(sc_recv.at[app, pl.ds(0, OWN - 1)], r_sc.at[app])
            part = sc_recv[app, 0]
            for n in range(1, OWN):
                part = part + sc_recv[app, n]
            ag_send[app, 0] = jnp.where(
                row4w == 3, part, ag_send[app, 0]
            )
        @pl.when(is_double)
        def _():
            for d in FAR_X:
                send(
                    ag_send.at[app], ag_recv.at[app, pl.ds(2 * f, 2)], s_ag.at[app], r_ag.at[app],
                    (lax.rem(f + d, FX), y, z),
                )
            ag_recv[app, 2 * f + 1] = ag_send[app, 1]

        @pl.when(jnp.logical_not(is_double))
        def _():
            for d in FAR_X:
                send(
                    ag_send.at[app, 0], ag_recv.at[app, 2 * f], s_ag.at[app], r_ag.at[app],
                    (lax.rem(f + d, FX), y, z),
                )

        ag_recv[app, 2 * f] = ag_send[app, 0]

        wait(rs_recv.at[app, pl.ds(0, 14)], s_rs.at[app])
        wait(rs_recv.at[app, pl.ds(0, 3)], s_rl.at[app])
        if scalars is not None:
            wait(sc_recv.at[app, pl.ds(0, OWN - 1)], s_sc.at[app])

        @pl.when(f == 15)
        def _():
            wait(rs_recv.at[app, 0], s_rs.at[app])

        @pl.when(jnp.logical_not(is_high | is_low))
        def _():
            wait(rs_recv.at[app, 0], s_rl.at[app])

        @pl.when(is_double)
        def _():
            wait(ag_recv.at[app, pl.ds(0, 17)], r_ag.at[app])

        @pl.when(jnp.logical_not(is_double))
        def _():
            wait(ag_recv.at[app, pl.ds(0, 18)], r_ag.at[app])

    def gathered(app, target):
        for c in range(3):
            for h in range(15):
                target[c * 16 + h : c * 16 + h + 1, :] = ag_recv[app, 2 * h, c : c + 1, :]
            target[c * 16 + 15 : c * 16 + 16, :] = (
                ag_recv[app, 2 * HIGH_RELAYS[0], c : c + 1, :]
                + ag_recv[app, 2 * HIGH_RELAYS[1] + 1, c : c + 1, :]
            )
            target[48 + c : 49 + c, :] = has_before * (
                ag_recv[app, 2 * LOW_RELAYS[0] + 1, c : c + 1, :]
                + ag_recv[app, 2 * LOW_RELAYS[1] + 1, c : c + 1, :]
            )

    kdisp = vec_w[...]
    loads = jnp.concatenate([FORCE_SCALE * load_ref[...], jnp.zeros((16, 256), F32)], axis=0)
    exchange(0, loads - kdisp, None)
    gathered(0, vec_r)
    wait(frc_recv.at[pl.ds(0, OWN - 1)], s_frc)
    pop_copy.wait()
    vec_p[...] = jnp.zeros((64, 256), F32)
    vec_s[...] = jnp.zeros((64, 256), F32)
    vec_w[...] = jnp.zeros((64, 256), F32)

    def iteration(app, carry):
        alpha, gamma = carry
        for c in range(3):
            rc[c : c + 1, :] = vec_r[pl.ds(c * 16 + f, 1), :]
        rc[3:4, :] = jnp.zeros((1, 256), F32)
        chunk = rc[...]
        mine = jnp.sum(chunk * chunk, keepdims=True)
        held = jnp.sum(massx[pl.ds(f, 1), :] * chunk * chunk, keepdims=True)

        def tell():
            energy = held + jnp.sum(pick[...] * spread[...], keepdims=True)
            scalars = jnp.where(iota((1, 256), 1) < 128, mine, energy)
            sc_send[app] = scalars
            sc_recv[app, own] = scalars

        exchange(app, elements(vec_r[...]), tell)
        gathered(app, vec_w)
        both = ag_recv[app, 0]
        for n in range(1, FX):
            both = both + ag_recv[app, 2 * n]
        new = both[3:4, 0:128]
        delta = both[3:4, 128:256]
        beta = jnp.where(app == 1, 0.0, new / gamma)
        alpha = new / (delta - beta * new / alpha)
        beta2 = jnp.concatenate([beta, beta], axis=1)
        alpha2 = jnp.concatenate([alpha, alpha], axis=1)
        p = vec_r[...] + beta2 * vec_p[...]
        s = vec_w[...] + massx[...] * vec_r[...] + beta2 * vec_s[...]
        vec_p[...] = p
        vec_s[...] = s
        vec_r[...] = vec_r[...] - alpha2 * s
        vec_x[...] += alpha2 * p[0:48]
        return alpha, new

    one = jnp.ones((1, 128), F32)
    lax.fori_loop(1, APPS, iteration, (one, one))

    for c in range(3):
        for h in range(16):
            at = slice(h * 256, h * 256 + 256)
            out_sol[c : c + 1, at] = vec_x[c * 16 + h : c * 16 + h + 1, :]
            out_res[c : c + 1, at] = vec_r[c * 16 + h : c * 16 + h + 1, :]

    for app in range(APPS):
        wait(ag_recv.at[app, pl.ds(0, FX - 1)], s_ag.at[app])

        @pl.when(is_double)
        def _():
            wait(ag_recv.at[app, pl.ds(0, FX - 1)], s_ag.at[app])


SCRATCH = dict(
    pop=(19, 4, 8, 256), relax=(4, 8, 256), vel=(3, 4096), count=((1, 16), I32),
    cell=((16, 32), I32), node=((16, 16, 32), I32), weight=(16, 16, 32), disp=(3, 4096),
    mass=(32, 128), connect=((8, 512), I32), modulus=(1, 512), basis=(24, 24),
    sup_send=(16, 8, 128), sup_recv=(16, 8, 128),
    wall_send=(16, 4, 128), wall_recv=(16, 4, 128),
    frc_send=(16, 4, 128), frc_recv=(16, 4, 128),
    edge_send=(4, 256), edge_recv=(4, 256),
    xs=(2, 2, 5, 8, 256), xr=(2, 2, 5, 8, 256),
    ys=(2, 2, 5, 4, 256), yr=(2, 2, 5, 4, 256),
    ds=(2, 4, 1, 256), dr=(2, 4, 1, 256),
    zs=(2, 4, 8, 128), zr=(2, 4, 8, 128), zxr=(2, 2, 8, 128),
    zys=(2, 2, 4, 128), zyr=(2, 2, 4, 128),
    rs_send=(APPS, 17, 4, 256), rs_recv=(APPS, 16, 4, 256), rl_recv=(APPS, 16, 4, 256),
    sc_send=(APPS, 1, 256), sc_recv=(APPS, 16, 1, 256),
    ag_send=(APPS, 2, 4, 256), ag_recv=(APPS, 32, 4, 256),
    post=(19, 4, 8, 256), field=(19, 4, 8, 256), rho_ref=(4, 8, 256), gain=(3, 4, 8, 256),
    cell_lo=((256, 512), BF16), cell_hi=(32, 512), live_ref=(8, 128), wallp=((192, 512), BF16),
    sup_lo=((16, 256, 512), BF16), sup_hi=(16, 16, 512),
    el_lo=((8, 256, 512), BF16), el_hi=(8, 16, 512), el_gh=(8, 512),
    pick=(24, 512), spread=(24, 512),
    vec_r=(64, 256), vec_p=(64, 256), vec_s=(64, 256), vec_w=(64, 256), vec_x=(48, 256),
    massx=(64, 256), rc=(4, 256), load_ref=(48, 256), out_pop=(19, 4, 8, 256),
)


def scratch_shapes():
    shapes = []
    for shape in SCRATCH.values():
        kind = F32
        if isinstance(shape[0], tuple):
            shape, kind = shape
        shapes.append(pltpu.VMEM(shape, kind))
    dma = pltpu.SemaphoreType.DMA
    shapes += [dma((INPUTS,)), dma]
    shapes += [dma, dma((OWN,)), dma, dma, dma, dma((OWN,)), dma, dma]
    shapes += [dma((2, 13))] * 2 + [dma((APPS,))] * 8
    return shapes


def deliver(pop_h, sol_h, res_h, pop_out, sol_out, res_out, pop, sol, res, s_in, s_out):
    jobs = [(pop_h.at[pl.ds(n, 4)], pop.at[pl.ds(n, 4)], pop_out.at[pl.ds(n, 4)]) for n in (0, 4, 8, 12)]
    jobs.append((pop_h.at[pl.ds(16, 3)], pop.at[pl.ds(16, 3)], pop_out.at[pl.ds(16, 3)]))
    jobs += [(sol_h, sol, sol_out), (res_h, res, res_out)]
    copies = []
    for n, (a, b, c) in enumerate(jobs):
        copies.append(
            (pltpu.make_async_copy(a, b, s_in.at[n]), pltpu.make_async_copy(b, c, s_out.at[n]))
        )
        copies[n][0].start()
    for came, goes in copies:
        came.wait()
        goes.start()
    for came, goes in copies:
        goes.wait()


def body(
    populations, relaxation, struct_velocity, iface_count, iface_cell, rbf_node, rbf_weight,
    disp_prev, node_mass, connect, modulus, strain_basis,
):
    vmem = pl.BlockSpec(memory_space=pltpu.VMEM)
    hbm = pl.BlockSpec(memory_space=pl.ANY)
    shapes = (
        jax.ShapeDtypeStruct(populations.shape, F32),
        jax.ShapeDtypeStruct(disp_prev.shape, F32),
        jax.ShapeDtypeStruct(disp_prev.shape, F32),
    )
    results = pl.pallas_call(
        kernel,
        out_shape=shapes,
        in_specs=[hbm] * INPUTS,
        out_specs=(hbm, vmem, vmem),
        scratch_shapes=scratch_shapes(),
        compiler_params=pltpu.CompilerParams(
            collective_id=0, has_side_effects=True, vmem_limit_bytes=62 * 1024 * 1024
        ),
        name="window",
    )(
        populations,
        relaxation,
        struct_velocity,
        iface_count.reshape(1, 16),
        iface_cell.reshape(16, 32),
        rbf_node.reshape(16, 16, 32),
        rbf_weight.reshape(16, 16, 32),
        disp_prev,
        node_mass.reshape(32, 128),
        connect.reshape(8, 512),
        modulus.reshape(1, 512),
        strain_basis,
    )
    return pl.pallas_call(
        deliver,
        out_shape=shapes,
        in_specs=[hbm] * 3,
        out_specs=(hbm, hbm, hbm),
        scratch_shapes=[pltpu.VMEM(s.shape, F32) for s in shapes]
        + [pltpu.SemaphoreType.DMA((7,))] * 2,
        compiler_params=pltpu.CompilerParams(vmem_limit_bytes=62 * 1024 * 1024),
        name="deliver",
    )(*results)


def solution(mesh):
    return jax.shard_map(
        body,
        mesh=mesh,
        in_specs=(
            P(None, "fx", "fy", "sz"),
            P("fx", "fy", "sz"),
            P(None, ("fy", "sz")),
            P("fx", "fy", "sz", None),
            P("fx", "fy", "sz", None, None),
            P("fx", "fy", "sz", None, None, None),
            P("fx", "fy", "sz", None, None, None),
            P(None, ("fy", "sz")),
            P(("fy", "sz")),
            P("fx", ("fy", "sz"), None, None),
            P("fx", ("fy", "sz"), None),
            P(),
        ),
        out_specs=(P(None, "fx", "fy", "sz"), P(None, ("fy", "sz")), P(None, ("fy", "sz"))),
        check_vma=False,
    )
```
